32 devices in a mesh: batch: 8 (over y, x, core), field: 4 (over z).
Axes of the slice: x: 2, y: 2, z: 4, core: 2. Of those that a mesh axis runs over, the one named last changes fastest.
Arguments:
- inputs: bfloat16 [65536, 512], P('batch', 'field'), may hold values from -6 to 6
- labels: int32 [65536, 2], P(('batch', 'field')), may hold values 0 or 1
- user_ids: int32 [65536], P(('batch', 'field')), may hold values from 0 to 16383
- first_weight: float32 [512, 2048], P('field'), may hold values from -0.25 to 0.25
- first_mean: float32 [512, 2048], P('field'), may hold values from -28 to 28
- first_square: float32 [512, 2048], P('field'), may hold values from 1.048576 to 17.03936
- gate_weight: float32 [512, 16], P('field'), may hold values from -0.125 to 0.125
- gate_mean: float32 [512, 16], P('field'), may hold values from -224 to 224
- gate_square: float32 [512, 16], P('field'), may hold values from 72.0896 to 1179.648
- second_weight: float32 [2048, 128], replicated, may hold values from -0.375 to 0.375
- second_mean: float32 [2048, 128], replicated, may hold values from -40 to 40
- second_square: float32 [2048, 128], replicated, may hold values from 1.96608 to 32.768
- tower_weight: float32 [128, 128], replicated, may hold values from -0.5 to 0.5
- tower_mean: float32 [128, 128], replicated, may hold values from -320 to 320
- tower_square: float32 [128, 128], replicated, may hold values from 131.072 to 2097.152
- head_weight: float32 [128], replicated, may hold values from -0.75 to 0.75
- head_mean: float32 [128], replicated, may hold values from -7168 to 7168
- head_square: float32 [128], replicated, may hold values from 65536 to 1048576
- biases: float32 [3202], replicated, may hold values from -0.625 to 0.625
- bias_mean: float32 [3202], replicated, may hold values from -768 to 768
- bias_square: float32 [3202], replicated, may hold values from 0.65536 to 1048576
- second_average: float32 [2048, 128], replicated, may hold values from -0.375 to 0.375
- tower_average: float32 [128, 128], replicated, may hold values from -0.5 to 0.5
- head_average: float32 [128], replicated, may hold values from -0.75 to 0.75
Outputs:
- predicted: float32 [65536, 2], P(('batch', 'field'))
- input_grad: float32 [65536, 512], P('batch', 'field')
- updated_first: float32 [512, 2048], P('field')
- moment_first: float32 [512, 2048], P('field')
- square_first: float32 [512, 2048], P('field')
- updated_gate: float32 [512, 16], P('field')
- moment_gate: float32 [512, 16], P('field')
- square_gate: float32 [512, 16], P('field')
- updated_second: float32 [2048, 128], replicated
- moment_second: float32 [2048, 128], replicated
- square_second: float32 [2048, 128], replicated
- updated_tower: float32 [128, 128], replicated
- moment_tower: float32 [128, 128], replicated
- square_tower: float32 [128, 128], replicated
- updated_head: float32 [128], replicated
- moment_head: float32 [128], replicated
- square_head: float32 [128], replicated
- updated_bias: float32 [3202], replicated
- moment_bias: float32 [3202], replicated
- square_bias: float32 [3202], replicated
- average_second: float32 [2048, 128], replicated
- average_tower: float32 [128, 128], replicated
- average_head: float32 [128], replicated
The draws below stay inside these ranges and needn't reach their ends.
Inputs may be any that keep to these rules, and one draw needn't show every extreme that they name: `user_ids`: each impression's user.
All inputs are finite; a program needn't handle non-finite values. No bound on the sum of `labels` on one device may be relied on, other than what follows from the above.
Results may differ from the reference program's by a relative error of at most 0.012.
The reference program's roundings to bfloat16 on the way count: a program that leaves them out, or rounds other values in their place, can miss the bound.
Values may be sent and summed in bfloat16 or wider, within the bound.
No kernel may reach another device: no remote copies, remote signals or barrier semaphores. Data moves between devices by JAX's collectives and lax.ppermute only.
A program may use at most 192 MiB of HBM per device.

```python
import math
import jax
import jax.numpy as jnp
from jax import lax

D_IN = 512
EXPERTS = 8
EXP_H1 = 256
EXP_H2 = 128
TASKS = 2
TOWER = 64
BLOCK_ROWS = 4096
STEP = 10
TOKENS = 65536
USERS = 16384
H1 = 2048
H2 = 1024
NBIAS = 3202


def plant(drawn, rng, smallest, top_value):
    index_at = [jax.random.randint(jax.random.fold_in(rng, axis), (), 0, length) for axis, length in enumerate(drawn.shape)]
    widest = drawn.shape.index(max(drawn.shape))
    next_to = index_at[:widest] + [(index_at[widest] + 1) % drawn.shape[widest]] + index_at[widest + 1:]
    return drawn.at[tuple(index_at)].set(smallest).at[tuple(next_to)].set(top_value)


def levels(own_key, shape, cuts, low, high):
    def one(dim, blocks):
        steps = jax.random.uniform(jax.random.fold_in(jax.random.fold_in(own_key, 6), dim), (blocks,), jnp.float32, low / len(cuts), high / len(cuts))
        return jnp.repeat(jnp.exp(steps), shape[dim] // blocks).reshape((-1,) + (1,) * (len(shape) - dim - 1))

    level = one(*cuts[0])
    for cut in cuts[1:]:
        level = level * one(*cut)
    return level


def noise(own_key, extent, spread, bound, pieces=(), kind=jnp.bfloat16):
    gain = levels(own_key, extent, pieces, -0.22, 0.18) if pieces else 1.0
    array = jax.random.normal(own_key, extent, jnp.float32) * spread * gain
    return jnp.minimum(jnp.maximum(array, -bound), bound).astype(kind)


def setup_inputs(seed: int = 0) -> dict:
    key_list = jax.random.split(jax.random.key(seed), 25)
    inputs = noise(key_list[0], (TOKENS, D_IN), 1.0, 6.0, ((0, 8), (1, 4)))
    labels = plant((jax.random.randint(key_list[1], (TOKENS, TASKS), 0, 2) < 1).astype(jnp.int32), jax.random.fold_in(key_list[1], 1), 0, 1)
    user_ids = plant(jax.random.randint(key_list[2], (TOKENS,), 0, USERS), jax.random.fold_in(key_list[2], 1), 0, USERS - 1).astype(jnp.int32)
    first_weight = noise(key_list[3], (D_IN, H1), D_IN ** -0.5, 0.25, ((0, 4),), jnp.float32)
    first_mean = noise(key_list[4], (D_IN, H1), (0.018 * TOKENS ** 0.5), 28.0, ((0, 4),), jnp.float32)
    first_square = jnp.clip(jnp.exp(math.log(17.03936) - 2.7880929 * jax.random.uniform(key_list[5], (D_IN, H1), jnp.float32) ** levels(key_list[5], (D_IN, H1), ((0, 4),), -0.2, 0.2)), 1.048576, 17.03936)
    gate_weight = noise(key_list[6], (D_IN, TASKS * EXPERTS), (0.5 * D_IN ** -0.5), 0.125, ((0, 4),), jnp.float32)
    gate_mean = noise(key_list[7], (D_IN, TASKS * EXPERTS), (0.15 * TOKENS ** 0.5), 224.0, ((0, 4),), jnp.float32)
    gate_square = jnp.clip(jnp.exp(math.log(1179.648) - 2.7950615 * jax.random.uniform(key_list[8], (D_IN, TASKS * EXPERTS), jnp.float32) ** levels(key_list[8], (D_IN, TASKS * EXPERTS), ((0, 4),), -0.2, 0.2)), 72.0896, 1179.648)
    second_weight = noise(key_list[9], (H1, EXP_H2), EXP_H1 ** -0.5, 0.375, (), jnp.float32)
    second_mean = noise(key_list[10], (H1, EXP_H2), (0.025 * TOKENS ** 0.5), 40.0, (), jnp.float32)
    second_square = jnp.clip(jnp.exp(jax.random.uniform(key_list[11], (H1, EXP_H2), jnp.float32, math.log(1.96608), math.log(32.768))), 1.96608, 32.768)
    tower_weight = noise(key_list[12], (EXP_H2, TASKS * TOWER), EXP_H2 ** -0.5, 0.5, (), jnp.float32)
    tower_mean = noise(key_list[13], (EXP_H2, TASKS * TOWER), (0.2 * TOKENS ** 0.5), 320.0, (), jnp.float32)
    tower_square = jnp.clip(jnp.exp(jax.random.uniform(key_list[14], (EXP_H2, TASKS * TOWER), jnp.float32, math.log(131.072), math.log(2097.152))), 131.072, 2097.152)
    head_weight = noise(key_list[15], (TASKS * TOWER,), TOWER ** -0.5, 0.75, (), jnp.float32)
    head_mean = noise(key_list[16], (TASKS * TOWER,), (4.5 * TOKENS ** 0.5), 7168.0, (), jnp.float32)
    head_square = jnp.clip(jnp.exp(jax.random.uniform(key_list[17], (TASKS * TOWER,), jnp.float32, math.log(65536.0), math.log(1048576))), 65536.0, 1048576)
    biases = noise(key_list[18], (NBIAS,), 0.1, 0.625, (), jnp.float32)
    bias_mean = noise(key_list[19], (NBIAS,), (0.5 * TOKENS ** 0.5), 768.0, (), jnp.float32)
    bias_square = jnp.clip(jnp.exp(jax.random.uniform(key_list[20], (NBIAS,), jnp.float32, math.log(0.65536), math.log(1048576))), 0.65536, 1048576)
    second_average = noise(key_list[21], (H1, EXP_H2), EXP_H1 ** -0.5, 0.375, (), jnp.float32)
    tower_average = noise(key_list[22], (EXP_H2, TASKS * TOWER), EXP_H2 ** -0.5, 0.5, (), jnp.float32)
    head_average = noise(key_list[23], (TASKS * TOWER,), TOWER ** -0.5, 0.75, (), jnp.float32)
    return dict(inputs=inputs, labels=labels, user_ids=user_ids, first_weight=first_weight, first_mean=first_mean, first_square=first_square, gate_weight=gate_weight, gate_mean=gate_mean, gate_square=gate_square, second_weight=second_weight, second_mean=second_mean, second_square=second_square, tower_weight=tower_weight, tower_mean=tower_mean, tower_square=tower_square, head_weight=head_weight, head_mean=head_mean, head_square=head_square, biases=biases, bias_mean=bias_mean, bias_square=bias_square, second_average=second_average, tower_average=tower_average, head_average=head_average)


beta_one = 0.9
beta_two = 0.999
learn_rate = 0.1
decay_rate = 0.01
adam_eps = 1e-08
average_rate = 0.8
loss_scale = 512.0

@jax.custom_vjp
def low(v):
    return lax.optimization_barrier(v.astype(jnp.bfloat16)).astype(jnp.float32)

@jax.custom_vjp
def low_back(v):
    return v

def low_keep(v):
    return (low(v), None)

def low_pass(kept, grad):
    return (grad,)

def back_keep(v):
    return (v, None)

def back_low(kept, grad):
    return (low(grad),)
low.defvjp(low_keep, low_pass)
low_back.defvjp(back_keep, back_low)

def dot_high(left, right):
    return jnp.dot(left, right, precision=lax.Precision.HIGHEST, preferred_element_type=jnp.float32)

def forward(params, block_inputs, targets, row_weight):
    first_weight, gate_weight, second_weight, tower_weight, head_weight, biases = params
    first_low = low(first_weight)
    gate_low = low(gate_weight)
    second_low = low(second_weight).reshape(EXPERTS, EXP_H1, EXP_H2)
    tower_low = low(tower_weight).reshape(EXP_H2, TASKS, TOWER)
    bias_first = biases[:H1]
    bias_second = biases[H1:H1 + H2].reshape(EXPERTS, EXP_H2)
    bias_tower = biases[H1 + H2:H1 + H2 + TASKS * TOWER].reshape(TASKS, TOWER)
    bias_head = biases[H1 + H2 + TASKS * TOWER:]
    pre_one = low_back(dot_high(block_inputs, first_low) + bias_first)
    hidden_one = low(jax.nn.silu(pre_one)).reshape(-1, EXPERTS, EXP_H1)
    logits = low_back(dot_high(block_inputs, gate_low)).reshape(-1, TASKS, EXPERTS)
    gate_values = jax.nn.softmax(logits, axis=-1)
    pre_two = low_back(jnp.einsum('rei,eio->reo', hidden_one, second_low, precision=lax.Precision.HIGHEST, preferred_element_type=jnp.float32) + bias_second)
    hidden_two = jax.nn.silu(pre_two)
    mixed_rows = low(lax.optimization_barrier(jnp.sum(gate_values[:, :, :, None] * hidden_two[:, None], axis=2)))
    pre_tower = low_back(jnp.einsum('rko,okj->rkj', mixed_rows, tower_low, precision=lax.Precision.HIGHEST, preferred_element_type=jnp.float32) + bias_tower)
    upper_act = jax.nn.silu(pre_tower)
    logit_rows = lax.optimization_barrier(jnp.sum(upper_act * head_weight.reshape(TASKS, TOWER), axis=-1)) + bias_head
    prob_rows = jax.nn.sigmoid(logit_rows)
    loss_value = jnp.sum(row_weight[:, None] * (jax.nn.softplus(logit_rows) - targets * logit_rows))
    return (loss_value, prob_rows)

def adamw(weight, moment, square, gradient):
    new_moment = beta_one * moment + (1.0 - beta_one) * gradient
    new_square = beta_two * square + (1.0 - beta_two) * gradient * gradient
    moment_hat = new_moment / (1.0 - beta_one ** STEP)
    square_hat = new_square / (1.0 - beta_two ** STEP)
    new_weight = weight - learn_rate * (moment_hat / (jnp.sqrt(square_hat) + adam_eps) + decay_rate * weight)
    return (new_weight, new_moment, new_square)

def reference(inputs, labels, user_ids, first_weight, first_mean, first_square, gate_weight, gate_mean, gate_square, second_weight, second_mean, second_square, tower_weight, tower_mean, tower_square, head_weight, head_mean, head_square, biases, bias_mean, bias_square, second_average, tower_average, head_average):
    counts = jax.ops.segment_sum(jnp.ones((TOKENS,), jnp.float32), user_ids, num_segments=USERS)
    present = jnp.sum(jnp.where(counts > 0.0, 1.0, 0.0).astype(jnp.float32))
    row_weight = loss_scale * USERS / (present * counts[user_ids])
    params = (first_weight, gate_weight, second_weight, tower_weight, head_weight, biases)
    all_inputs = inputs.astype(jnp.float32)
    targets = labels.astype(jnp.float32)
    nblocks = TOKENS // BLOCK_ROWS

    def block_step(totals, block_index):
        start = (block_index * BLOCK_ROWS).astype(jnp.int32)
        block_inputs = lax.dynamic_slice_in_dim(all_inputs, start, BLOCK_ROWS, 0)
        block_targets = lax.dynamic_slice_in_dim(targets, start, BLOCK_ROWS, 0)
        block_weight = lax.dynamic_slice_in_dim(row_weight, start, BLOCK_ROWS, 0)

        def local_loss(weights_now, rows_now):
            return forward(weights_now, rows_now, block_targets, block_weight)
        loss_value, pullback, prob_rows = jax.vjp(local_loss, params, block_inputs, has_aux=True)
        grads, row_grads = pullback(jnp.ones_like(loss_value))
        totals = jax.tree.map(jnp.add, totals, grads)
        return (totals, (prob_rows, row_grads))
    zeros = jax.tree.map(jnp.zeros_like, params)
    grads, (probs, row_grads) = lax.scan(block_step, zeros, jnp.arange(nblocks, dtype=jnp.int32))
    predicted = probs.reshape(TOKENS, TASKS)
    input_grad = row_grads.reshape(TOKENS, D_IN)
    g_first, g_gate, g_second, g_tower, g_head, g_bias = grads
    new_first = adamw(first_weight, first_mean, first_square, g_first)
    new_gate = adamw(gate_weight, gate_mean, gate_square, g_gate)
    new_second = adamw(second_weight, second_mean, second_square, g_second)
    new_tower = adamw(tower_weight, tower_mean, tower_square, g_tower)
    new_head = adamw(head_weight, head_mean, head_square, g_head)
    new_bias = adamw(biases, bias_mean, bias_square, g_bias)
    avg_second = average_rate * second_average + (1.0 - average_rate) * new_second[0]
    avg_tower = average_rate * tower_average + (1.0 - average_rate) * new_tower[0]
    avg_head = average_rate * head_average + (1.0 - average_rate) * new_head[0]
    return (predicted, input_grad, new_first[0], new_first[1], new_first[2], new_gate[0], new_gate[1], new_gate[2], new_second[0], new_second[1], new_second[2], new_tower[0], new_tower[1], new_tower[2], new_head[0], new_head[1], new_head[2], new_bias[0], new_bias[1], new_bias[2], avg_second, avg_tower, avg_head)
```

```python
import functools

import jax
import jax.numpy as jnp
from jax import lax
from jax.experimental import pallas as pl
from jax.experimental.pallas import tpu as pltpu
from jax.sharding import PartitionSpec as P

EXPERTS = 8
EXP_H1 = 256
EXP_H2 = 128
TASKS = 2
TOWER = 64
USER_ROWS = 4
STEP = 10
H1 = 2048
H2 = 1024
GATES = TASKS * EXPERTS
LANES = 128
GROUP = 8
CHUNKS = 2
SUB_ROWS = 256
VMEM_BYTES = 56 * 1024 * 1024

beta_one = 0.9
beta_two = 0.999
learn_rate = 0.1
decay_rate = 0.01
adam_eps = 1e-08
average_rate = 0.8
loss_scale = 512.0

f32 = jnp.float32
bf16 = jnp.bfloat16


def sigmoid(values):
    return 0.5 * jnp.tanh(0.5 * values) + 0.5


def dot(left, right):
    return jnp.dot(left, right, preferred_element_type=f32)


def dot_nt(left, right, precision=None):
    return lax.dot_general(
        left, right, (((1,), (1,)), ((), ())), precision=precision, preferred_element_type=f32
    )


def adamw(weight, moment, square, gradient):
    new_moment = beta_one * moment + (1.0 - beta_one) * gradient
    new_square = beta_two * square + (1.0 - beta_two) * gradient * gradient
    moment_hat = new_moment / (1.0 - beta_one**STEP)
    square_hat = new_square / (1.0 - beta_two**STEP)
    new_weight = weight - learn_rate * (
        moment_hat / (jnp.sqrt(square_hat) + adam_eps) + decay_rate * weight
    )
    return (new_weight, new_moment, new_square)


def blend(average, weight):
    return average_rate * average + (1.0 - average_rate) * weight


def params(**kwargs):
    return pltpu.CompilerParams(vmem_limit_bytes=VMEM_BYTES, **kwargs)


def cost(flops, nbytes):
    return pl.CostEstimate(flops=int(flops), bytes_accessed=int(nbytes), transcendentals=0)


def count_kernel(ids_ref, out_ref):
    ids = ids_ref[...]
    width = ids.shape[1]
    high = lax.broadcasted_iota(jnp.int32, (out_ref.shape[0], width), 0)
    low = lax.broadcasted_iota(jnp.int32, (LANES, width), 0)
    one_high = jnp.where(high == ids // LANES, 1.0, 0.0).astype(bf16)
    one_low = jnp.where(low == ids % LANES, 1.0, 0.0).astype(bf16)
    out_ref[...] = dot_nt(one_high, one_low)


def weight_kernel(scale, ids_ref, counts_ref, out_ref):
    ids = ids_ref[...]
    counts = counts_ref[...]
    width = ids.shape[1]
    present = jnp.sum(jnp.where(counts > 0.0, 1.0, 0.0), keepdims=True)
    high = lax.broadcasted_iota(jnp.int32, (counts.shape[0], width), 0)
    low = lax.broadcasted_iota(jnp.int32, (LANES, width), 0)
    one_high = jnp.where(high == ids // LANES, 1.0, 0.0)
    columns = lax.dot_general(
        counts,
        one_high,
        (((0,), (0,)), ((), ())),
        precision=lax.Precision.HIGHEST,
        preferred_element_type=f32,
    )
    mine = jnp.sum(jnp.where(low == ids % LANES, columns, 0.0), axis=0, keepdims=True)
    out_ref[...] = scale / (present * mine)


def prepare_kernel(place_ref, *refs):
    pieces, (first_ref, turned_ref) = refs[:GROUP], refs[GROUP:]
    for slot, piece_ref in enumerate(pieces):
        expert = place_ref[0] ^ slot
        start = pl.multiple_of(expert * EXP_H1, EXP_H1)
        piece = piece_ref[...]
        first_ref[:, pl.ds(start, EXP_H1)] = piece
        turned_ref[pl.ds(start, EXP_H1), :] = piece.T


def layers_kernel(
    last,
    with_sums,
    place_ref,
    x0,
    x1,
    x2,
    x3,
    labels_ref,
    weights_ref,
    turned_ref,
    gate_ref,
    second_ref,
    second_t_ref,
    tower_fwd_ref,
    tower_bwd_ref,
    bias_one_ref,
    bias_two_ref,
    bias_top_ref,
    *rest,
):
    nsum = 5
    sums_in, rest = (rest[:nsum], rest[nsum:]) if with_sums else (None, rest)
    d_ref, prob_ref, rest = rest[0], rest[1], rest[2:]
    if last:
        packed_ref, gate_out_ref, small_ref = rest[:3]
        rest = rest[3:]
        sums, rest = rest[:nsum], rest[nsum:]
    else:
        sums, rest = rest[:nsum], rest[nsum:]
    sum_first, sum_second, sum_tower, sum_bias, sum_top = sums
    hidden_ref, slope_ref, two_ref, slope_two_ref = rest
    rows = SUB_ROWS
    step = pl.program_id(0)

    @pl.when(step == 0)
    def _():
        if with_sums:
            for total, given in zip(sums, sums_in):
                total[...] = given[...]
        else:
            for total in sums:
                total[...] = jnp.zeros_like(total)

    def fold(values):
        out = values[:, :LANES]
        for at in range(LANES, values.shape[1], LANES):
            out = out + values[:, at : at + LANES]
        return out

    def wide(values):
        return jnp.concatenate([values] * (rows // LANES), axis=1)

    inputs = jnp.concatenate([x0[...], x1[...], x2[...], x3[...]], axis=1)
    turned_in = inputs.T
    logits = dot(gate_ref[...], turned_in).reshape(TASKS, EXPERTS, rows)
    shifted = jnp.exp(logits - jnp.max(logits, axis=1, keepdims=True))
    gates = shifted / jnp.sum(shifted, axis=1, keepdims=True)
    mixed = [jnp.zeros((EXP_H2, rows), f32) for _ in range(TASKS)]
    for e in range(EXPERTS):
        one, two = pl.ds(e * EXP_H1, EXP_H1), pl.ds(e * EXP_H2, EXP_H2)
        pre_one = dot(turned_ref[one, :], turned_in) + wide(bias_one_ref[one, :])
        logistic = sigmoid(pre_one)
        hidden = pre_one * logistic
        slope_ref[one, :] = logistic + hidden * (1.0 - logistic)
        hidden_low = hidden.astype(bf16)
        hidden_ref[one, :] = hidden_low
        pre_two = dot(second_t_ref[two, :], hidden_low) + wide(bias_two_ref[two, :])
        logistic = sigmoid(pre_two)
        hidden = pre_two * logistic
        slope_two_ref[two, :] = logistic + hidden * (1.0 - logistic)
        two_ref[two, :] = hidden
        for k in range(TASKS):
            mixed[k] = mixed[k] + gates[k, e : e + 1, :] * hidden
    mixed_low = jnp.concatenate(mixed, axis=0).astype(bf16)
    pre_tower = dot(tower_fwd_ref[...], mixed_low) + wide(bias_top_ref[0])
    logistic = sigmoid(pre_tower)
    upper = pre_tower * logistic
    slope_tower = logistic + upper * (1.0 - logistic)
    head = wide(bias_top_ref[1])
    logit = jnp.sum((upper * head).reshape(TASKS, TOWER, rows), axis=1)
    logit = logit + wide(bias_top_ref[2])[:TASKS, :]
    prob = 1.0 / (1.0 + jnp.exp(-logit))
    prob_ref[...] = prob
    d_logit = weights_ref[...] * (prob - labels_ref[...].astype(f32))
    d_wide = jnp.broadcast_to(d_logit[:, None, :], (TASKS, TOWER, rows)).reshape(LANES, rows)
    d_tower = (d_wide * head * slope_tower).astype(bf16)
    sum_top[0] += fold(d_tower.astype(f32))
    sum_top[1] += fold(d_wide * upper)
    sum_top[2, :TASKS, :] += fold(d_logit)
    sum_tower[...] += dot_nt(mixed_low, d_tower)
    d_mixed = dot(tower_bwd_ref[...], d_tower)
    parts = [d_mixed[k * EXP_H2 : (k + 1) * EXP_H2, :] for k in range(TASKS)]
    d_gates = [[], []]
    for e in range(EXPERTS):
        one, two = pl.ds(e * EXP_H1, EXP_H1), pl.ds(e * EXP_H2, EXP_H2)
        hidden = two_ref[two, :]
        for k in range(TASKS):
            d_gates[k].append(jnp.sum(parts[k] * hidden, axis=0, keepdims=True))
        d_hidden = gates[0, e : e + 1, :] * parts[0] + gates[1, e : e + 1, :] * parts[1]
        d_two = d_hidden * slope_two_ref[two, :]
        sum_bias[pl.ds(H1 + e * EXP_H2, EXP_H2), :] += fold(d_two)
        d_two = d_two.astype(bf16)
        sum_second[one, :] += dot_nt(hidden_ref[one, :], d_two)
        d_one = dot(second_ref[one, :], d_two) * slope_ref[one, :]
        sum_bias[one, :] += fold(d_one)
        d_ref[one, :] = d_one.astype(bf16)
    d_gates = jnp.stack([jnp.concatenate(rows_of, axis=0) for rows_of in d_gates])
    centered = d_gates - jnp.sum(gates * d_gates, axis=1, keepdims=True)
    d_ref[pl.ds(H1, GATES), :] = (gates * centered).reshape(GATES, rows).astype(bf16)
    sum_first[...] += dot(d_ref[...], inputs)

    if last:

        @pl.when(step == pl.num_programs(0) - 1)
        def _():
            place = place_ref[0]
            width = sum_first.shape[1]
            for e in range(EXPERTS):
                one = pl.ds(e * EXP_H1, EXP_H1)
                slot = e ^ place
                packed_ref[slot & 1, slot >> 1, :, :width] = sum_first[one, :].astype(bf16)
                packed_ref[slot & 1, slot >> 1, :, width:] = sum_second[one, :].astype(bf16)
            gate_out_ref[...] = sum_first[pl.ds(H1, GATES), :]
            small_ref[:TOWER * TASKS, :TOWER] = sum_tower[:EXP_H2, :TOWER]
            small_ref[:TOWER * TASKS, TOWER:] = sum_tower[EXP_H2:, TOWER:]
            ones = jnp.ones((8, LANES), f32)
            lines = dot_nt(ones, sum_bias[...], lax.Precision.HIGHEST)
            for row in range((H1 + H2) // LANES):
                small_ref[pl.ds(LANES + row, 1), :] = lines[:1, row * LANES : (row + 1) * LANES]
            at = LANES + (H1 + H2) // LANES
            for k in range(3):
                line = dot_nt(ones, sum_top[k], lax.Precision.HIGHEST)
                small_ref[pl.ds(at + k, 1), :] = line[:1, :]
            small_ref[at + 3 :, :] = jnp.zeros((small_ref.shape[0] - at - 3, LANES), f32)


def back_kernel(d_ref, first_ref, gate_ref, own_ref, *others):
    turned = dot(first_ref[...], d_ref[:H1, :]) + dot(gate_ref[...], d_ref[H1:, :])
    grads = turned.T
    width = own_ref.shape[1]
    own_ref[...] = grads[:, :width]
    for s, ref in enumerate(others):
        ref[...] = grads[:, (s + 1) * width : (s + 2) * width].astype(bf16)


def update_kernel(
    place_ref,
    grads_ref,
    first_w,
    first_m,
    first_v,
    second_w,
    second_m,
    second_v,
    second_a,
    first_w_out,
    first_m_out,
    first_v_out,
    second_w_out,
    second_m_out,
    second_v_out,
    second_a_out,
):
    grads = grads_ref[0].astype(f32)
    width = first_w.shape[0]
    new = adamw(first_w[...], first_m[...], first_v[...], grads[:, :width].T)
    first_w_out[...], first_m_out[...], first_v_out[...] = new
    new = adamw(second_w[...], second_m[...], second_v[...], grads[:, width:])
    second_w_out[...], second_m_out[...], second_v_out[...] = new
    second_a_out[...] = blend(second_a[...], new[0])


def on_device(
    inputs,
    labels,
    user_ids,
    first_weight,
    first_mean,
    first_square,
    gate_weight,
    gate_mean,
    gate_square,
    second_weight,
    second_mean,
    second_square,
    tower_weight,
    tower_mean,
    tower_square,
    head_weight,
    head_mean,
    head_square,
    biases,
    bias_mean,
    bias_square,
    second_average,
    tower_average,
    head_average,
):
    nfield, nbatch = lax.axis_size("field"), lax.axis_size("batch")
    field, batch = lax.axis_index("field"), lax.axis_index("batch")
    rows_dev, columns = inputs.shape
    rows = rows_dev // nfield
    chunk = rows // CHUNKS
    users_total = rows_dev * nbatch // USER_ROWS
    place = (batch % GROUP).astype(jnp.int32)
    place_arg = place.reshape(1)

    def shift(value, by):
        return lax.ppermute(value, "field", [(i, (i + by) % nfield) for i in range(nfield)])

    def cross(value, mask):
        return lax.ppermute(value, "batch", [(i, i ^ mask) for i in range(nbatch)])

    def sum_field(value):
        hop = 1
        while hop < nfield:
            value = value + lax.ppermute(value, "field", [(i, i ^ hop) for i in range(nfield)])
            hop *= 2
        return value

    def sum_batch(value):
        hop = 1
        while hop < nbatch:
            value = value + cross(value, hop)
            hop *= 2
        return value

    smem = pl.BlockSpec(memory_space=pltpu.SMEM)
    whole = pl.BlockSpec(memory_space=pltpu.VMEM)

    first_low = first_weight.astype(bf16)
    gate_low = gate_weight.astype(bf16)
    piece = lax.dynamic_slice_in_dim(first_low, place * EXP_H1, EXP_H1, 1)
    bundle = jnp.concatenate([piece] + [shift(piece, s) for s in range(1, nfield)], axis=0)
    gate_t = gate_low.T
    gate_t = jnp.concatenate([gate_t] + [shift(gate_t, s) for s in range(1, nfield)], axis=1)
    even = [bundle] + [cross(bundle, 2 * j) for j in range(1, GROUP // 2)]
    odd = [cross(part, 1) for part in even]
    slots = [part for pair in zip(even, odd) for part in pair]

    ids = user_ids.reshape(1, rows)
    counts = pl.pallas_call(
        count_kernel,
        out_shape=jax.ShapeDtypeStruct((users_total // LANES, LANES), f32),
        in_specs=[whole],
        out_specs=whole,
        compiler_params=params(),
        name="user_counts",
    )(ids)
    counts = sum_field(sum_batch(counts))
    row_weight = pl.pallas_call(
        functools.partial(weight_kernel, loss_scale * users_total),
        out_shape=jax.ShapeDtypeStruct((1, rows), f32),
        in_specs=[whole] * 2,
        out_specs=whole,
        compiler_params=params(),
        name="row_weights",
    )(ids, counts)

    first_all, turned_all = pl.pallas_call(
        prepare_kernel,
        out_shape=(
            jax.ShapeDtypeStruct((nfield * columns, H1), bf16),
            jax.ShapeDtypeStruct((H1, nfield * columns), bf16),
        ),
        in_specs=[smem] + [whole] * GROUP,
        out_specs=(whole, whole),
        compiler_params=params(),
        name="prepare_first",
    )(place_arg, *slots)

    second_low = second_weight.astype(bf16)
    second_t = second_low.reshape(EXPERTS, EXP_H1, EXP_H2).transpose(0, 2, 1).reshape(H2, EXP_H1)
    tower_low = tower_weight.astype(bf16)
    none = jnp.zeros((EXP_H2, TOWER), bf16)
    tower_bwd = jnp.concatenate(
        [
            jnp.concatenate([tower_low[:, :TOWER], none], axis=1),
            jnp.concatenate([none, tower_low[:, TOWER:]], axis=1),
        ],
        axis=0,
    )
    tower_fwd = tower_bwd.T
    bias_one = jnp.broadcast_to(biases[:H1, None], (H1, LANES))
    bias_two = jnp.broadcast_to(biases[H1 : H1 + H2, None], (H2, LANES))
    top = jnp.stack(
        [
            biases[H1 + H2 : H1 + H2 + LANES],
            head_weight,
            jnp.pad(biases[H1 + H2 + LANES :], (0, LANES - TASKS)),
        ]
    )
    bias_top = jnp.broadcast_to(top[:, :, None], (3, LANES, LANES))
    labels_t = labels.T

    def chunk_rows(c, s):
        start = (field + s) % nfield * rows + c * chunk
        return lax.dynamic_slice_in_dim(inputs, start, chunk, 0)

    arrived = []
    for c in range(CHUNKS):
        arrived.append(
            [chunk_rows(c, 0)] + [shift(chunk_rows(c, s), s) for s in range(1, nfield)]
        )

    sum_shapes = [
        jax.ShapeDtypeStruct((H1 + GATES, nfield * columns), f32),
        jax.ShapeDtypeStruct((H1, EXP_H2), f32),
        jax.ShapeDtypeStruct((TASKS * EXP_H2, TASKS * TOWER), f32),
        jax.ShapeDtypeStruct((H1 + H2, LANES), f32),
        jax.ShapeDtypeStruct((3, LANES, LANES), f32),
    ]

    def full(shape):
        return pl.BlockSpec(shape, lambda i: (0,) * len(shape))

    def run_layers(c, sums):
        last = c == CHUNKS - 1
        x_spec = pl.BlockSpec((SUB_ROWS, columns), lambda i: (i, 0))
        at = c * chunk // SUB_ROWS
        operands = [
            turned_all,
            gate_t,
            second_low,
            second_t,
            tower_fwd,
            tower_bwd,
            bias_one,
            bias_two,
            bias_top,
        ] + list(sums or [])
        out_shape = [
            jax.ShapeDtypeStruct((H1 + GATES, chunk), bf16),
            jax.ShapeDtypeStruct((TASKS, chunk), f32),
        ]
        out_specs = [
            pl.BlockSpec((H1 + GATES, SUB_ROWS), lambda i: (0, i)),
            pl.BlockSpec((TASKS, SUB_ROWS), lambda i: (0, i)),
        ]
        scratch = [
            pltpu.VMEM((H1, SUB_ROWS), bf16),
            pltpu.VMEM((H1, SUB_ROWS), f32),
            pltpu.VMEM((H2, SUB_ROWS), f32),
            pltpu.VMEM((H2, SUB_ROWS), f32),
        ]
        if last:
            more = [
                jax.ShapeDtypeStruct((2, GROUP // 2, EXP_H1, nfield * columns + EXP_H2), bf16),
                jax.ShapeDtypeStruct((GATES, nfield * columns), f32),
                jax.ShapeDtypeStruct((LANES + 32, LANES), f32),
            ]
            scratch = [pltpu.VMEM(s.shape, s.dtype) for s in sum_shapes] + scratch
        else:
            more = sum_shapes
        out_shape += more
        out_specs += [full(s.shape) for s in more]
        return pl.pallas_call(
            functools.partial(layers_kernel, last, sums is not None),
            grid=(chunk // SUB_ROWS,),
            out_shape=out_shape,
            in_specs=[smem]
            + [x_spec] * nfield
            + [
                pl.BlockSpec((TASKS, SUB_ROWS), lambda i: (0, i + at)),
                pl.BlockSpec((1, SUB_ROWS), lambda i: (0, i + at)),
            ]
            + [full(o.shape) for o in operands],
            out_specs=out_specs,
            scratch_shapes=scratch,
            compiler_params=params(),
            cost_estimate=cost(2 * chunk * 4e6, 20e6),
            name="layers",
        )(place_arg, *arrived[c], labels_t, row_weight, *operands)

    gate_all = gate_t.T

    def run_back(d_chunk):
        block = pl.BlockSpec((SUB_ROWS, columns), lambda i: (i, 0))
        return pl.pallas_call(
            back_kernel,
            grid=(chunk // SUB_ROWS,),
            out_shape=[jax.ShapeDtypeStruct((chunk, columns), f32)]
            + [jax.ShapeDtypeStruct((chunk, columns), bf16)] * (nfield - 1),
            in_specs=[
                pl.BlockSpec((H1 + GATES, SUB_ROWS), lambda i: (0, i)),
                full(first_all.shape),
                full(gate_all.shape),
            ],
            out_specs=[block] * nfield,
            compiler_params=params(),
            cost_estimate=cost(2 * chunk * 1e6, 8e6),
            name="input_gradients",
        )(d_chunk, first_all, gate_all)

    sums = None
    probs = []
    input_grad = jnp.zeros((rows_dev, columns), f32)
    returned = []
    for c in range(CHUNKS):
        d_chunk, prob, *sums = run_layers(c, sums)
        probs.append(prob)
        own, *others = run_back(d_chunk)
        returned.append([own] + [shift(o, -(s + 1)) for s, o in enumerate(others)])
    packed, gate_grad, small = sums

    kept = packed[0].astype(f32) + cross(packed[1], 1).astype(f32)
    kept_low = kept.astype(bf16)
    total = kept[0]
    for j in range(1, GROUP // 2):
        total = total + cross(kept_low[j], 2 * j).astype(f32)
    hop = GROUP
    while hop < nbatch:
        low = total.astype(bf16)
        total = low.astype(f32) + cross(low, hop).astype(f32)
        hop *= 2
    total = total.astype(bf16)
    width = nfield * columns

    def for_field(s):
        return jnp.concatenate([total[:, s * columns : (s + 1) * columns], total[:, width:]], axis=1)

    terms = [for_field(0)] + [shift(for_field(s), -s) for s in range(1, nfield)]
    terms = [t.astype(f32) for t in terms]
    odd_field = field % 2 == 1
    near = jnp.where(odd_field, terms[3], terms[1])
    far = jnp.where(odd_field, terms[1], terms[3])
    done = ((terms[0] + near) + (terms[2] + far)).astype(bf16)
    even = [done] + [cross(done, 2 * j) for j in range(1, GROUP // 2)]
    odd = [cross(part, 1) for part in even]
    grads = jnp.stack([part for pair in zip(even, odd) for part in pair])

    def row_block(j, place_ref):
        return (place_ref[0] ^ j, 0)

    def column_block(j, place_ref):
        return (0, place_ref[0] ^ j)

    first_spec = pl.BlockSpec((columns, EXP_H1), column_block)
    second_spec = pl.BlockSpec((EXP_H1, EXP_H2), row_block)
    updated = pl.pallas_call(
        update_kernel,
        grid_spec=pltpu.PrefetchScalarGridSpec(
            num_scalar_prefetch=1,
            grid=(EXPERTS,),
            in_specs=[pl.BlockSpec((1, EXP_H1, columns + EXP_H2), lambda j, place_ref: (j, 0, 0))]
            + [first_spec] * 3
            + [second_spec] * 4,
            out_specs=[first_spec] * 3 + [second_spec] * 4,
        ),
        out_shape=[jax.ShapeDtypeStruct((columns, H1), f32)] * 3
        + [jax.ShapeDtypeStruct((H1, EXP_H2), f32)] * 4,
        compiler_params=params(),
        cost_estimate=cost(1e6, 15e6),
        name="update_layers",
    )(
        place_arg,
        grads,
        first_weight,
        first_mean,
        first_square,
        second_weight,
        second_mean,
        second_square,
        second_average,
    )
    new_first, new_second, avg_second = updated[:3], updated[3:6], updated[6]

    gate_grad = jnp.concatenate(
        [gate_grad[:, s * columns : (s + 1) * columns] for s in range(nfield)], axis=0
    )
    both = sum_batch(jnp.concatenate([small, gate_grad], axis=0))
    small = sum_field(both[: small.shape[0]])
    gate_grad = both[small.shape[0] :]
    terms = [gate_grad[s * GATES : (s + 1) * GATES] for s in range(nfield)]
    gate_grad = terms[0]
    for s in range(1, nfield):
        gate_grad = gate_grad + shift(terms[s], -s)
    g_tower = small[:LANES]
    lines = (H1 + H2) // LANES
    g_head = small[LANES + lines + 1]
    g_bias = jnp.concatenate(
        [small[LANES : LANES + lines + 1].reshape(-1), small[LANES + lines + 2, :TASKS]]
    )
    new_gate = adamw(gate_weight, gate_mean, gate_square, gate_grad.T)
    new_tower = adamw(tower_weight, tower_mean, tower_square, g_tower)
    avg_tower = blend(tower_average, new_tower[0])
    new_head = adamw(head_weight, head_mean, head_square, g_head)
    avg_head = blend(head_average, new_head[0])
    new_bias = adamw(biases, bias_mean, bias_square, g_bias)

    for c in range(CHUNKS):
        for s in range(nfield):
            start = (field + s) % nfield * rows + c * chunk
            input_grad = lax.dynamic_update_slice_in_dim(
                input_grad, returned[c][s].astype(f32), start, 0
            )
    predicted = jnp.concatenate(probs, axis=1).T
    return (
        predicted,
        input_grad,
        *new_first,
        *new_gate,
        *new_second,
        *new_tower,
        *new_head,
        *new_bias,
        avg_second,
        avg_tower,
        avg_head,
    )


def solution(mesh):
    fields, copied = P("field", None), P()
    rows = P(("batch", "field"), None)
    in_specs = (
        (P("batch", "field"), rows, P(("batch", "field"))) + (fields,) * 6 + (copied,) * 15
    )
    out_specs = (rows, P("batch", "field")) + (fields,) * 6 + (copied,) * 15
    return jax.shard_map(
        on_device, mesh=mesh, in_specs=in_specs, out_specs=out_specs, check_vma=False
    )
```

```python
import functools

import jax
import jax.numpy as jnp
from jax import lax
from jax.experimental import pallas as pl
from jax.experimental.pallas import tpu as pltpu
from jax.sharding import PartitionSpec as P

EXPERTS = 8
EXP_H1 = 256
EXP_H2 = 128
TASKS = 2
TOWER = 64
USER_ROWS = 4
STEP = 10
H1 = 2048
H2 = 1024
GATES = TASKS * EXPERTS
LANES = 128
GROUP = 8
QUADS = GROUP // 2
CHUNKS = (4, 6, 6)
RETURNS = (3, 7, 6)
MIB = 1024 * 1024
LAYERS_MIB = 32
FIELDS = 4
BIG = (FIELDS + 1) * EXP_H1
TOWER_ROWS, LINE_ROWS, GATE_ROWS = 32, 16, 16
SMALL = TOWER_ROWS + LINE_ROWS + GATE_ROWS
PIECE = BIG + SMALL

beta_one = 0.9
beta_two = 0.999
learn_rate = 0.1
decay_rate = 0.01
adam_eps = 1e-08
average_rate = 0.8
loss_scale = 512.0

LAYERS_COST = 1e3
BACK_COST = 1e3

f32 = jnp.float32
bf16 = jnp.bfloat16
smem = pl.BlockSpec(memory_space=pltpu.SMEM)
vmem = pl.BlockSpec(memory_space=pltpu.VMEM)
anywhere = pl.BlockSpec(memory_space=pl.ANY)


def sigmoid(values):
    return 0.5 * jnp.tanh(0.5 * values) + 0.5


def dot(left, right):
    return jnp.dot(left, right, preferred_element_type=f32)


def dot_nt(left, right, precision=None):
    return lax.dot_general(
        left, right, (((1,), (1,)), ((), ())), precision=precision, preferred_element_type=f32
    )


def adamw(weight, moment, square, gradient):
    new_moment = beta_one * moment + (1.0 - beta_one) * gradient
    new_square = beta_two * square + (1.0 - beta_two) * gradient * gradient
    moment_hat = new_moment / (1.0 - beta_one**STEP)
    square_hat = new_square / (1.0 - beta_two**STEP)
    new_weight = weight - learn_rate * (
        moment_hat / (jnp.sqrt(square_hat) + adam_eps) + decay_rate * weight
    )
    return (new_weight, new_moment, new_square)


def blend(average, weight):
    return average_rate * average + (1.0 - average_rate) * weight


def params(mib=8):
    return pltpu.CompilerParams(vmem_limit_bytes=mib * MIB)


def cost(flops, nbytes):
    return pl.CostEstimate(flops=int(flops), bytes_accessed=int(nbytes), transcendentals=0)


def shaped(shape, dtype):
    return jax.ShapeDtypeStruct(shape, dtype)


def aligned(index, size):
    return pl.ds(pl.multiple_of(index * size, size), size)


def call(kernel, name, out_shape, in_specs, operands, flops=1e6, nbytes=1e6, deps=(), mib=8):
    def body(*refs):
        given = len(operands)
        kernel(*refs[:given], *refs[given + len(deps) :])

    return pl.pallas_call(
        body,
        out_shape=out_shape,
        in_specs=list(in_specs) + [anywhere] * len(deps),
        out_specs=jax.tree.map(lambda _: vmem, out_shape),
        compiler_params=params(mib),
        cost_estimate=cost(flops, nbytes),
        name=name,
    )(*operands, *deps)


def once_there(name, values, deps):
    return pl.pallas_call(
        lambda *refs: None,
        out_shape=[shaped(v.shape, v.dtype) for v in values],
        in_specs=[anywhere] * (len(values) + len(deps)),
        out_specs=[anywhere] * len(values),
        input_output_aliases={i: i for i in range(len(values))},
        compiler_params=params(),
        cost_estimate=cost(1, 1),
        name=name,
    )(*values, *deps)


def piece_kernel(place_ref, first_ref, gate_ref, ids_ref, send_ref):
    send_ref[:EXP_H1, :] = (0.5 * first_ref[...]).T.astype(bf16)
    at = EXP_H1 + GATES
    send_ref[EXP_H1:at, :] = gate_ref[...].astype(bf16)
    ids, lines = ids_ref[...], ids_ref.shape[0]
    send_ref[at : at + lines, :] = (ids % 256).astype(f32).astype(bf16)
    send_ref[at + lines :, :] = (ids // 256).astype(f32).astype(bf16)


def count_kernel(digits_ref, counts_ref):
    lines = digits_ref.shape[1] // 2
    width = digits_ref.shape[2]
    high = lax.broadcasted_iota(jnp.int32, (counts_ref.shape[1], width), 0).astype(f32)
    low = lax.broadcasted_iota(jnp.int32, (LANES, width), 0).astype(f32)
    total = jnp.zeros(counts_ref.shape, f32)
    for q in range(QUADS):
        digits = digits_ref[q].astype(f32)
        ids = digits[:lines] + 256.0 * digits[lines:]
        ids_high = jnp.floor(ids * (1.0 / LANES))
        ids_low = ids - LANES * ids_high
        for r in range(lines):
            one_high = jnp.where(high == ids_high[r : r + 1], 1.0, 0.0).astype(bf16)
            one_low = jnp.where(low == ids_low[r : r + 1], 1.0, 0.0).astype(bf16)
            total = total + dot_nt(one_low, one_high)
    counts_ref[...] = total


def prepare_kernel(second_ref, tower_ref, head_ref, bias_ref, *outs):
    second_low, second_t, tower_fwd, tower_bwd, bias_one, bias_two, bias_top = outs
    second_low[...] = (0.5 * second_ref[...]).astype(bf16)
    for e in range(EXPERTS):
        block = 0.5 * second_ref[pl.ds(e * EXP_H1, EXP_H1), :]
        second_t[pl.ds(e * EXP_H2, EXP_H2), :] = block.T.astype(bf16)
    tower = tower_ref[...]
    none = jnp.zeros((EXP_H2, TOWER), f32)
    left = jnp.concatenate([tower[:, :TOWER], none], axis=1)
    right = jnp.concatenate([none, tower[:, TOWER:]], axis=1)
    tower_bwd[...] = jnp.concatenate([left, right], axis=0).astype(bf16)
    tower_fwd[...] = jnp.concatenate([left.T, right.T], axis=1).astype(bf16)

    def column(row):
        return jnp.broadcast_to(row, (LANES, LANES)).T

    for r in range(H1 // LANES):
        bias_one[pl.ds(r * LANES, LANES), :] = 0.5 * column(bias_ref[:, r * LANES : (r + 1) * LANES])
    for r in range(H2 // LANES):
        at = H1 + r * LANES
        bias_two[pl.ds(r * LANES, LANES), :] = 0.5 * column(bias_ref[:, at : at + LANES])
    at = H1 + H2
    bias_top[0] = column(bias_ref[:, at : at + LANES])
    bias_top[1] = column(head_ref[...])
    bias_top[2] = column(bias_ref[:, at + LANES : at + 2 * LANES])


def join_fields_kernel(*refs):
    sent, (bundle_ref, gate_ref) = refs[:FIELDS], refs[FIELDS:]
    width = sent[0].shape[1]
    for s, ref in enumerate(sent):
        at = slice(s * width, (s + 1) * width)
        bundle_ref[:EXP_H1, at] = ref[:EXP_H1, :]
        gate_ref[:, at] = ref[EXP_H1 : EXP_H1 + GATES, :]
        bundle_ref[EXP_H1:, at] = ref[EXP_H1 + GATES :, :]


def join_quads_kernel(*refs):
    bundles, (stack_ref, digits_ref) = refs[:QUADS], refs[QUADS:]
    for q, ref in enumerate(bundles):
        stack_ref[q] = ref[:EXP_H1, :]
        digits_ref[q] = ref[EXP_H1:, :]


def rows_kernel(starts, place_ref, inputs_ref, *refs):
    outs, sems = refs[:-1], refs[-1]
    rows = inputs_ref.shape[0] // FIELDS
    copies = []
    for i, out in enumerate(outs):
        chunk, s = divmod(i, FIELDS)
        at = pl.ds(lax.rem(place_ref[1] + s, FIELDS) * rows + starts[chunk], out.shape[0])
        copies.append(pltpu.make_async_copy(inputs_ref.at[at, :], out, sems.at[i]))
        copies[-1].start()
    for copy in copies:
        copy.wait()


def turn_kernel(stack_ref, out_ref):
    for q in range(QUADS):
        out_ref[:, q * EXP_H1 : (q + 1) * EXP_H1] = stack_ref[q].T


NSUM = 5


def layers_kernel(last, with_sums, ndeps, scale, low_row, place_ref, *refs):
    xs, refs = refs[:FIELDS], refs[FIELDS:]
    ids_ref, labels_ref, own_ref, other_ref, gate_ref, counts_a, counts_b, refs = *refs[:7], refs[7:]
    second_ref, second_t_ref, tower_fwd_ref, tower_bwd_ref, bias_one_ref, bias_two_ref, bias_top_ref = refs[:7]
    refs = refs[7:]
    given = [None] * NSUM
    if with_sums:
        given, refs = refs[:NSUM], refs[NSUM:]
    refs = refs[ndeps:]
    d_ref, prob_ref, refs = refs[0], refs[1], refs[2:]
    sums, refs = refs[:NSUM], refs[NSUM:]
    if last:
        keep_ref, send_ref, refs = refs[0], refs[1], refs[2:]
    sum_first, sum_second, sum_tower, sum_bias, sum_top = sums
    hidden_ref, slope_ref, two_ref, slope_two_ref, gates_ref, d_gates_ref = refs
    rows = prob_ref.shape[1]
    mine = slice(low_row, low_row + rows)
    place = place_ref[0]

    def add(which, at, value):
        sums[which][at] = value if given[which] is None else given[which][at] + value

    def fold(values):
        out = values[:, :LANES]
        for at in range(LANES, values.shape[1], LANES):
            out = out + values[:, at : at + LANES]
        return out

    def wide(values):
        return jnp.concatenate([values] * (rows // LANES), axis=1)

    def silu_of_twice(half):
        swing = jnp.tanh(half)
        above = 1.0 + swing
        value = half * above
        return value, above + value * (1.0 - swing)

    ids = ids_ref[:, mine]
    counts = counts_a[...] + counts_b[...]
    present = jnp.sum(jnp.where(counts > 0.0, 1.0, 0.0), keepdims=True)
    high = lax.broadcasted_iota(jnp.int32, (counts.shape[1], rows), 0)
    low = lax.broadcasted_iota(jnp.int32, (LANES, rows), 0)
    one_high = jnp.where(high == ids // LANES, 1.0, 0.0).astype(bf16)
    top_digit = jnp.floor(counts * (1.0 / 65536.0))
    counts = counts - 65536.0 * top_digit
    mid_digit = jnp.floor(counts * (1.0 / 256.0))
    low_digit = counts - 256.0 * mid_digit
    found = dot(low_digit.astype(bf16), one_high)
    found = found + 256.0 * dot(mid_digit.astype(bf16), one_high)
    found = found + 65536.0 * dot(top_digit.astype(bf16), one_high)
    found = jnp.sum(jnp.where(low == ids % LANES, found, 0.0), axis=0, keepdims=True)
    row_weight = scale / (present * found)

    inputs = jnp.concatenate([x[...] for x in xs], axis=1)
    turned_in = inputs.T
    logits = dot(gate_ref[...], turned_in).reshape(TASKS, EXPERTS, rows)
    shifted = jnp.exp(logits - jnp.max(logits, axis=1, keepdims=True))
    gates = shifted / jnp.sum(shifted, axis=1, keepdims=True)
    gates_ref[...] = gates.reshape(GATES, rows)
    slots = [(c, q) for c in range(2) for q in range(QUADS)]
    mixed = [jnp.zeros((EXP_H2, rows), f32) for _ in range(TASKS)]
    for t, (c, q) in enumerate(slots):
        e = place ^ (2 * q + c)
        one, two = pl.ds(t * EXP_H1, EXP_H1), pl.ds(t * EXP_H2, EXP_H2)
        weight = (other_ref if c else own_ref)[q]
        half_one = dot(weight, turned_in) + wide(bias_one_ref[aligned(e, EXP_H1), :])
        hidden, slope_ref[one, :] = silu_of_twice(half_one)
        hidden_low = hidden.astype(bf16)
        hidden_ref[one, :] = hidden_low
        half_two = dot(second_t_ref[aligned(e, EXP_H2), :], hidden_low)
        half_two = half_two + wide(bias_two_ref[aligned(e, EXP_H2), :])
        hidden, slope_two_ref[two, :] = silu_of_twice(half_two)
        two_ref[two, :] = hidden
        for k in range(TASKS):
            mixed[k] = mixed[k] + gates_ref[pl.ds(k * EXPERTS + e, 1), :] * hidden
    mixed_low = jnp.concatenate(mixed, axis=0).astype(bf16)
    pre_tower = dot(tower_fwd_ref[...], mixed_low) + wide(bias_top_ref[0])
    logistic = sigmoid(pre_tower)
    upper = pre_tower * logistic
    slope_tower = logistic + upper * (1.0 - logistic)
    head = wide(bias_top_ref[1])
    logit = jnp.sum((upper * head).reshape(TASKS, TOWER, rows), axis=1)
    logit = logit + wide(bias_top_ref[2])[:TASKS, :]
    prob = 1.0 / (1.0 + jnp.exp(-logit))
    prob_ref[...] = prob
    d_logit = row_weight * (prob - labels_ref[:, mine].astype(f32))
    d_wide = jnp.broadcast_to(d_logit[:, None, :], (TASKS, TOWER, rows)).reshape(LANES, rows)
    d_tower = (d_wide * head * slope_tower).astype(bf16)
    add(4, 0, fold(d_tower.astype(f32)))
    add(4, 1, fold(d_wide * upper))
    low_rows = jnp.zeros((LANES - TASKS, LANES), f32)
    add(4, 2, jnp.concatenate([fold(d_logit), low_rows], axis=0))
    add(2, ..., dot_nt(mixed_low, d_tower))
    d_mixed = dot(tower_bwd_ref[...], d_tower)
    parts = [d_mixed[k * EXP_H2 : (k + 1) * EXP_H2, :] for k in range(TASKS)]
    for t, (c, q) in enumerate(slots):
        e = place ^ (2 * q + c)
        one, two = pl.ds(t * EXP_H1, EXP_H1), pl.ds(t * EXP_H2, EXP_H2)
        hidden = two_ref[two, :]
        d_hidden = jnp.zeros((EXP_H2, rows), f32)
        for k in range(TASKS):
            at = pl.ds(k * EXPERTS + e, 1)
            d_gates_ref[at, :] = jnp.sum(parts[k] * hidden, axis=0, keepdims=True)
            d_hidden = d_hidden + gates_ref[at, :] * parts[k]
        d_two = d_hidden * slope_two_ref[two, :]
        at = pl.ds(pl.multiple_of(H1 + e * EXP_H2, EXP_H2), EXP_H2)
        add(3, (at, slice(None)), fold(d_two))
        d_two = d_two.astype(bf16)
        add(1, (two, slice(None)), dot_nt(d_two, hidden_ref[one, :]))
        d_one = dot(second_ref[aligned(e, EXP_H1), :], d_two) * slope_ref[one, :]
        add(3, (aligned(e, EXP_H1), slice(None)), fold(d_one))
        d_ref[one, :] = d_one.astype(bf16)
    d_gates = d_gates_ref[...].reshape(TASKS, EXPERTS, rows)
    centered = d_gates - jnp.sum(gates * d_gates, axis=1, keepdims=True)
    d_ref[pl.ds(H1, GATES), :] = (gates * centered).reshape(GATES, rows).astype(bf16)
    add(0, ..., dot(d_ref[...], inputs))

    if last:
        for t, (c, q) in enumerate(slots):
            one, two = pl.ds(t * EXP_H1, EXP_H1), pl.ds(t * EXP_H2, EXP_H2)
            out = send_ref if c else keep_ref
            for s in range(FIELDS):
                at = pl.ds(q * BIG + s * EXP_H1, EXP_H1)
                out[at, :] = (0.5 * sum_first[one, s * LANES : (s + 1) * LANES]).astype(bf16)
            out[pl.ds(q * BIG + FIELDS * EXP_H1, EXP_H1), :] = (0.5 * sum_second[two, :]).T.astype(bf16)
        ones = jnp.ones((8, LANES), f32)
        bias = dot_nt(0.5 * ones, sum_bias[...], lax.Precision.HIGHEST)[:1, :]
        lines = [bias[:, r * LANES : (r + 1) * LANES] for r in range((H1 + H2) // LANES)]
        lines += [dot_nt(ones, sum_top[k], lax.Precision.HIGHEST)[:1, :] for k in range(3)]
        lines += [jnp.zeros((1, LANES), f32)] * (8 * QUADS - len(lines))
        none = jnp.zeros((8, LANES), f32)
        for out in (keep_ref, send_ref):
            at = QUADS * BIG
            for q in range(QUADS):
                block = sum_tower[pl.ds(q * TOWER_ROWS, TOWER_ROWS), :TOWER]
                below = sum_tower[pl.ds(EXP_H2 + q * TOWER_ROWS, TOWER_ROWS), TOWER:]
                out[pl.ds(at, TOWER_ROWS), :] = jnp.concatenate([block, below], axis=1).astype(bf16)
                at += TOWER_ROWS
                block = jnp.concatenate(lines[8 * q : 8 * q + 8] + [none], axis=0)
                out[pl.ds(at, LINE_ROWS), :] = block.astype(bf16)
                at += LINE_ROWS
                block = sum_first[pl.ds(H1, GATES), q * LANES : (q + 1) * LANES]
                out[pl.ds(at, GATE_ROWS), :] = block.astype(bf16)
                at += GATE_ROWS


def back_kernel(spans, *refs):
    d_refs, refs = refs[: len(spans)], refs[len(spans) :]
    own_ref, other_ref, gate_ref, out_own = refs[:4]
    half, at = H1 // 2, 0
    for (low, high), d_ref in zip(spans, d_refs):
        here = slice(low, high)
        turned = dot(own_ref[...], d_ref[:half, here]) + dot(other_ref[...], d_ref[half:H1, here])
        turned = turned + dot(gate_ref[...], d_ref[H1:, here])
        grads = turned.T
        width, rows = out_own.shape[1], pl.ds(at, high - low)
        out_own[rows, :] = grads[:, :width]
        for s, ref in enumerate(refs[-FIELDS + 1 :]):
            ref[rows, :] = grads[:, (s + 1) * width : (s + 2) * width].astype(bf16)
        at += high - low


def add_cores_kernel(place_ref, keep_ref, got_ref, *outs):
    quad = place_ref[0] >> 1

    def total(at):
        return (keep_ref[at, :].astype(f32) + got_ref[at, :].astype(f32)).astype(bf16)

    for q, out in enumerate(outs):
        out[:BIG, :] = total(pl.ds(q * BIG, BIG))
        start = pl.multiple_of(QUADS * BIG + (quad ^ q) * SMALL, SMALL)
        out[BIG:, :] = total(pl.ds(start, SMALL))


def add_quads_kernel(place_ref, *refs):
    parts, outs = refs[:QUADS], refs[QUADS:]
    quad = place_ref[0] >> 1

    def total(at):
        a, b, c, d = [ref[at, :].astype(f32) for ref in parts]
        return ((a + b) + (c + d)).astype(bf16)

    second = total(pl.ds(FIELDS * EXP_H1, EXP_H1))
    small = total(pl.ds(BIG, TOWER_ROWS + LINE_ROWS))
    gate = total(pl.ds(PIECE - GATE_ROWS, GATE_ROWS))
    for s, out in enumerate(outs):
        out[:EXP_H1, :] = total(pl.ds(s * EXP_H1, EXP_H1))
        out[EXP_H1 : 2 * EXP_H1, :] = second
        out[2 * EXP_H1 : 2 * EXP_H1 + TOWER_ROWS + LINE_ROWS, :] = small
        out[2 * EXP_H1 + TOWER_ROWS + LINE_ROWS :, :] = jnp.where(quad == s, gate, jnp.zeros_like(gate))


def add_fields_kernel(place_ref, *refs):
    parts, out = refs[:FIELDS], refs[FIELDS]
    odd = place_ref[1] % 2 == 1
    a, b, c, d = [ref[...].astype(f32) for ref in parts]
    out[...] = ((a + jnp.where(odd, d, b)) + (c + jnp.where(odd, b, d))).astype(bf16)


def join_done_kernel(place_ref, *refs):
    parts, (stack_ref, tower_ref, lines_ref, gate_ref) = refs[:QUADS], refs[QUADS:]
    quad = place_ref[0] >> 1
    for q, ref in enumerate(parts):
        stack_ref[q] = ref[: 2 * EXP_H1, :]
        at = 2 * EXP_H1
        tower_ref[aligned(quad ^ q, TOWER_ROWS), :] = ref[at : at + TOWER_ROWS, :].astype(f32)
        at += TOWER_ROWS
        lines_ref[aligned(quad ^ q, LINE_ROWS), :] = ref[at : at + LINE_ROWS, :].astype(f32)
    a, b, c, d = [ref[2 * EXP_H1 + TOWER_ROWS + LINE_ROWS :, :].astype(f32) for ref in parts]
    gate_ref[...] = (a + b) + (c + d)


def assemble_kernel(start, place_ref, *refs):
    parts, (out_ref, wide_ref, sems) = refs[:FIELDS], refs[-3:]
    rows, size = out_ref.shape[0] // FIELDS, wide_ref.shape[1]
    copies = []
    for s, part in enumerate(parts):
        at = pl.ds(lax.rem(place_ref[1] + s, FIELDS) * rows + start, size)
        if s:
            wide_ref[s - 1] = part[...].astype(f32)
        source = wide_ref.at[s - 1] if s else part
        copies.append(pltpu.make_async_copy(source, out_ref.at[at, :], sems.at[s]))
        copies[-1].start()
    for copy in copies:
        copy.wait()


def update_kernel(core, place_ref, grads_ref, *refs):
    first_w, first_m, first_v, second_w, second_m, second_v, second_a = refs[:7]
    outs = refs[-7:]
    expert = place_ref[0] ^ (2 * pl.program_id(0) + core)
    at = aligned(expert, EXP_H1)
    grads = grads_ref[pl.program_id(0)].astype(f32)
    new = adamw(first_w[:, at], first_m[:, at], first_v[:, at], grads[:EXP_H1].T)
    outs[0][...], outs[1][...], outs[2][...] = new
    new = adamw(second_w[at, :], second_m[at, :], second_v[at, :], grads[EXP_H1:])
    outs[3][...], outs[4][...], outs[5][...] = new
    outs[6][...] = blend(second_a[at, :], new[0])


def on_device(
    inputs,
    labels,
    user_ids,
    first_weight,
    first_mean,
    first_square,
    gate_weight,
    gate_mean,
    gate_square,
    second_weight,
    second_mean,
    second_square,
    tower_weight,
    tower_mean,
    tower_square,
    head_weight,
    head_mean,
    head_square,
    biases,
    bias_mean,
    bias_square,
    second_average,
    tower_average,
    head_average,
):
    nfield, nbatch = lax.axis_size("field"), lax.axis_size("batch")
    field, batch = lax.axis_index("field"), lax.axis_index("batch")
    rows_dev, columns = inputs.shape
    rows = rows_dev // nfield
    width = nfield * columns
    users_total = rows_dev * nbatch // USER_ROWS
    place = jnp.stack([batch % GROUP, field]).astype(jnp.int32)

    def shift(value, by):
        return lax.ppermute(value, "field", [(i, (i + by) % nfield) for i in range(nfield)])

    def cross(value, mask):
        return lax.ppermute(value, "batch", [(i, i ^ mask) for i in range(nbatch)])

    def from_fields(value):
        return [value] + [shift(value, s) for s in range(1, nfield)]

    def from_quads(value):
        return [value] + [cross(value, 2 * q) for q in range(1, QUADS)]

    starts = [0]
    for part in CHUNKS:
        starts.append(starts[-1] + part * rows // 16)
    nchunks = len(CHUNKS)

    ids = user_ids.reshape(1, rows)
    labels_t = labels.T
    expert_block = pl.BlockSpec((columns, EXP_H1), lambda i, place_ref: (0, place_ref[0]))
    high = users_total // LANES
    lines = 2 * rows // LANES
    sent = pl.pallas_call(
        piece_kernel,
        grid_spec=pltpu.PrefetchScalarGridSpec(
            num_scalar_prefetch=1, grid=(1,), in_specs=[expert_block, vmem, vmem], out_specs=vmem
        ),
        out_shape=shaped((EXP_H1 + GATES + lines, columns), bf16),
        compiler_params=params(),
        cost_estimate=cost(1e6, 1e5),
        name="first_piece",
    )(place, first_weight, gate_weight.T, user_ids.reshape(rows // LANES, LANES))
    prepared = call(
        prepare_kernel,
        "prepare_weights",
        [
            shaped((H1, EXP_H2), bf16),
            shaped((H2, EXP_H1), bf16),
            shaped((TASKS * TOWER, TASKS * EXP_H2), bf16),
            shaped((TASKS * EXP_H2, TASKS * TOWER), bf16),
            shaped((H1, LANES), f32),
            shaped((H2, LANES), f32),
            shaped((3, LANES, LANES), f32),
        ],
        [vmem] * 4,
        [
            second_weight,
            tower_weight,
            head_weight.reshape(1, LANES),
            jnp.pad(biases, (0, LANES - TASKS)).reshape(1, -1),
        ],
    )
    sliced = pl.pallas_call(
        functools.partial(rows_kernel, starts),
        out_shape=[shaped((b - a, columns), bf16) for a, b in zip(starts, starts[1:]) for _ in range(nfield)],
        in_specs=[smem, anywhere],
        out_specs=[anywhere] * (nchunks * nfield),
        scratch_shapes=[pltpu.SemaphoreType.DMA((nchunks * nfield,))],
        compiler_params=params(),
        cost_estimate=cost(1e3, 1e3),
        name="own_rows",
    )(place, inputs)

    def exchange_rows(c, deps):
        mine, *others = sliced[c * nfield : (c + 1) * nfield]
        if deps:
            others = once_there("rows_to_send", others, deps)
        return [mine] + [shift(o, s + 1) for s, o in enumerate(others)]

    arrived = [exchange_rows(0, [])]
    bundle, gate_t = call(
        join_fields_kernel,
        "join_fields",
        [shaped((EXP_H1 + lines, width), bf16), shaped((GATES, width), bf16)],
        [vmem] * FIELDS,
        from_fields(sent),
        deps=[prepared[0], *arrived[0][1:]],
    )
    arrived.append(exchange_rows(1, [gate_t]))
    own, digits = call(
        join_quads_kernel,
        "join_quads",
        [shaped((QUADS, EXP_H1, width), bf16), shaped((QUADS, lines, width), bf16)],
        [vmem] * QUADS,
        from_quads(bundle),
        deps=arrived[1][1:],
    )
    arrived.append(exchange_rows(2, [digits]))
    counts = call(count_kernel, "user_counts", shaped((LANES, high), f32), [vmem], [digits])
    hop = GROUP
    while hop < nbatch:
        counts = counts + cross(counts, hop)
        hop *= 2
    counts_other = cross(counts, 1)
    other = cross(own, 1)
    turned_own = call(turn_kernel, "turn_first", shaped((width, H1 // 2), bf16), [vmem], [own])
    turned_other = cross(turned_own, 1)

    sum_shapes = [
        shaped((H1 + GATES, width), f32),
        shaped((H2, EXP_H1), f32),
        shaped((TASKS * EXP_H2, TASKS * TOWER), f32),
        shaped((H1 + H2, LANES), f32),
        shaped((3, LANES, LANES), f32),
    ]

    def run_layers(c, sums, deps):
        last = c == nchunks - 1
        low, chunk = starts[c], starts[c + 1] - starts[c]
        operands = [*arrived[c], ids, labels_t, own, other, gate_t, counts, counts_other, *prepared]
        out_shape = [shaped((H1 + GATES, chunk), bf16), shaped((TASKS, chunk), f32)] + sum_shapes
        if last:
            out_shape += [shaped((QUADS * PIECE, LANES), bf16)] * 2

        def once(shape):
            return pl.BlockSpec(shape, lambda i: (0,) * len(shape), pipeline_mode=pl.Buffered(1))

        return pl.pallas_call(
            functools.partial(layers_kernel, last, bool(sums), len(deps), loss_scale * users_total, low),
            grid=(1,),
            out_shape=out_shape,
            in_specs=[smem]
            + [once(o.shape) for o in operands]
            + [vmem] * len(sums)
            + [anywhere] * len(deps),
            out_specs=[once(o.shape) for o in out_shape[:2]]
            + [vmem] * NSUM
            + [once(o.shape) for o in out_shape[2 + NSUM :]],
            input_output_aliases={1 + len(operands) + i: 2 + i for i in range(len(sums))},
            scratch_shapes=[
                pltpu.VMEM((H1, chunk), bf16),
                pltpu.VMEM((H1, chunk), f32),
                pltpu.VMEM((H2, chunk), f32),
                pltpu.VMEM((H2, chunk), f32),
                pltpu.VMEM((GATES, chunk), f32),
                pltpu.VMEM((GATES, chunk), f32),
            ],
            compiler_params=params(LAYERS_MIB),
            cost_estimate=cost(LAYERS_COST * chunk, 1e3),
            name="layers",
        )(place, *operands, *sums, *deps)

    gate_all = gate_t.T

    bounds = [0]
    for part in RETURNS:
        bounds.append(bounds[-1] + part * rows // 16)

    def give_back(i, deps):
        spans, taken = [], []
        for c in range(nchunks):
            low, high = max(bounds[i], starts[c]), min(bounds[i + 1], starts[c + 1])
            if low < high:
                spans.append((low - starts[c], high - starts[c]))
                taken.append(d_chunks[c])
        size = bounds[i + 1] - bounds[i]
        mine, *others = call(
            functools.partial(back_kernel, spans),
            "input_gradients",
            [shaped((size, columns), f32)] + [shaped((size, columns), bf16)] * (nfield - 1),
            [vmem] * (len(taken) + 3),
            [*taken, turned_own, turned_other, gate_all],
            flops=BACK_COST * size,
            deps=deps,
            mib=12,
        )
        return [mine] + [shift(o, -(s + 1)) for s, o in enumerate(others)]

    sums, probs, d_chunks, returned = [], [], [], []
    for c in range(nchunks):
        if c == nchunks - 1:
            returned.append(give_back(0, []))
        d_chunk, prob, *sums = run_layers(c, sums, [r[0] for r in returned])
        probs.append(prob)
        d_chunks.append(d_chunk)
    keep, send = sums[NSUM:]
    returned.append(give_back(1, [keep]))
    (send,) = once_there("gradients_to_send", [send], returned[0][1:])

    pieces = call(
        add_cores_kernel,
        "add_cores",
        [shaped((PIECE, LANES), bf16)] * QUADS,
        [smem, vmem, vmem],
        [place, keep, cross(send, 1)],
        deps=returned[1][:1],
    )
    parts = [pieces[0]] + [cross(pieces[q], 2 * q) for q in range(1, QUADS)]
    hop = GROUP
    while hop < nbatch:
        parts = [(p.astype(f32) + cross(p, hop).astype(f32)).astype(bf16) for p in parts]
        hop *= 2
    blocks = call(
        add_quads_kernel,
        "add_quads",
        [shaped((2 * EXP_H1 + SMALL, LANES), bf16)] * nfield,
        [smem] + [vmem] * QUADS,
        [place] + parts,
        deps=returned[1][1:],
    )
    returned.append(give_back(2, [blocks[0]]))
    done = call(
        add_fields_kernel,
        "add_fields",
        shaped((2 * EXP_H1 + SMALL, LANES), bf16),
        [smem] + [vmem] * nfield,
        [place, blocks[0]] + [shift(blocks[s], -s) for s in range(1, nfield)],
        deps=returned[2][:1],
    )
    done_own, g_tower, lines, g_gate = call(
        join_done_kernel,
        "join_gradients",
        [
            shaped((QUADS, 2 * EXP_H1, LANES), bf16),
            shaped((LANES, LANES), f32),
            shaped((QUADS * LINE_ROWS, LANES), f32),
            shaped((GATES, columns), f32),
        ],
        [smem] + [vmem] * QUADS,
        [place] + from_quads(done),
    )
    done_other = cross(done_own, 1)

    def run_update(core, grads, before):
        first_spec = pl.BlockSpec((columns, EXP_H1), lambda q, place_ref: (0, place_ref[0] ^ (2 * q + core)))
        second_spec = pl.BlockSpec((EXP_H1, EXP_H2), lambda q, place_ref: (place_ref[0] ^ (2 * q + core), 0))
        operands = [
            grads,
            first_weight,
            first_mean,
            first_square,
            second_weight,
            second_mean,
            second_square,
            second_average,
        ]
        specs = [first_spec] * 3 + [second_spec] * 4
        before = list(before or [])
        return pl.pallas_call(
            functools.partial(update_kernel, core),
            grid_spec=pltpu.PrefetchScalarGridSpec(
                num_scalar_prefetch=1,
                grid=(QUADS,),
                in_specs=[vmem] * len(operands) + [anywhere] * len(before),
                out_specs=specs,
            ),
            out_shape=[shaped((columns, H1), f32)] * 3 + [shaped((H1, EXP_H2), f32)] * 4,
            input_output_aliases={1 + len(operands) + i: i for i in range(len(before))},
            compiler_params=params(),
            cost_estimate=cost(1e6, 8e6),
            name="update_layers",
        )(place, *operands, *before)

    updated_half = run_update(0, done_own, None)
    updated = run_update(1, done_other, updated_half)
    new_first, new_second, avg_second = updated[:3], updated[3:6], updated[6]

    lines = lines.reshape(QUADS, LINE_ROWS, LANES)[:, :8].reshape(8 * QUADS, LANES)
    at = (H1 + H2) // LANES
    g_head = lines[at + 1]
    g_bias = jnp.concatenate([lines[: at + 1].reshape(-1), lines[at + 2, :TASKS]])
    new_gate = adamw(gate_weight, gate_mean, gate_square, g_gate.T)
    new_tower = adamw(tower_weight, tower_mean, tower_square, g_tower)
    avg_tower = blend(tower_average, new_tower[0])
    new_head = adamw(head_weight, head_mean, head_square, g_head)
    avg_head = blend(head_average, new_head[0])
    new_bias = adamw(biases, bias_mean, bias_square, g_bias)

    input_grad = []
    for i, part in enumerate(returned):
        deps = [updated[0]]
        input_grad = pl.pallas_call(
            functools.partial(assemble_kernel, bounds[i]),
            out_shape=[shaped((rows_dev, columns), f32)],
            in_specs=[smem, anywhere] + [vmem] * (nfield - 1) + [anywhere] * (len(input_grad) + len(deps)),
            out_specs=[anywhere],
            input_output_aliases={1 + nfield: 0} if input_grad else {},
            scratch_shapes=[
                pltpu.VMEM((nfield - 1, bounds[i + 1] - bounds[i], columns), f32),
                pltpu.SemaphoreType.DMA((nfield,)),
            ],
            compiler_params=params(),
            cost_estimate=cost(1e3, 1e3),
            name="assemble_input_grad",
        )(place, *part, *input_grad, *deps)
    (input_grad,) = input_grad
    predicted = jnp.concatenate(probs, axis=1).T
    return (
        predicted,
        input_grad,
        *new_first,
        *new_gate,
        *new_second,
        *new_tower,
        *new_head,
        *new_bias,
        avg_second,
        avg_tower,
        avg_head,
    )


def solution(mesh):
    fields, copied = P("field", None), P()
    rows = P(("batch", "field"), None)
    in_specs = (
        (P("batch", "field"), rows, P(("batch", "field"))) + (fields,) * 6 + (copied,) * 15
    )
    out_specs = (rows, P("batch", "field")) + (fields,) * 6 + (copied,) * 15
    return jax.shard_map(
        on_device, mesh=mesh, in_specs=in_specs, out_specs=out_specs, check_vma=False
    )
```

```python
import functools

import jax
import jax.numpy as jnp
from jax import lax
from jax.experimental import pallas as pl
from jax.experimental.pallas import tpu as pltpu
from jax.sharding import PartitionSpec as P

EXPERTS = 8
EXP_H1 = 256
EXP_H2 = 128
TASKS = 2
TOWER = 64
USER_ROWS = 4
STEP = 10
H1 = 2048
H2 = 1024
GATES = TASKS * EXPERTS
LANES = 128
GROUP = 8
QUADS = GROUP // 2
CHUNKS = (4, 6, 6)
RETURNS = (4, 6, 6)
MIB = 1024 * 1024
LAYERS_MIB = 32
FIELDS = 4
BIG = (FIELDS + 1) * EXP_H1
TOWER_ROWS, LINE_ROWS, GATE_ROWS = 32, 16, 16
SMALL = TOWER_ROWS + LINE_ROWS + GATE_ROWS
PIECE = BIG + SMALL

beta_one = 0.9
beta_two = 0.999
learn_rate = 0.1
decay_rate = 0.01
adam_eps = 1e-08
average_rate = 0.8
loss_scale = 512.0

LAYERS_COST = 1e3
BACK_COST = 1e3

f32 = jnp.float32
bf16 = jnp.bfloat16
smem = pl.BlockSpec(memory_space=pltpu.SMEM)
vmem = pl.BlockSpec(memory_space=pltpu.VMEM)
anywhere = pl.BlockSpec(memory_space=pl.ANY)
hbm = pl.BlockSpec(memory_space=pltpu.HBM)


def sigmoid(values):
    return 0.5 * jnp.tanh(0.5 * values) + 0.5


def dot(left, right):
    return jnp.dot(left, right, preferred_element_type=f32)


def dot_nt(left, right, precision=None):
    return lax.dot_general(
        left, right, (((1,), (1,)), ((), ())), precision=precision, preferred_element_type=f32
    )


def adamw(weight, moment, square, gradient):
    new_moment = beta_one * moment + (1.0 - beta_one) * gradient
    new_square = beta_two * square + (1.0 - beta_two) * gradient * gradient
    moment_hat = new_moment / (1.0 - beta_one**STEP)
    square_hat = new_square / (1.0 - beta_two**STEP)
    new_weight = weight - learn_rate * (
        moment_hat / (jnp.sqrt(square_hat) + adam_eps) + decay_rate * weight
    )
    return (new_weight, new_moment, new_square)


def blend(average, weight):
    return average_rate * average + (1.0 - average_rate) * weight


def params(mib=8):
    return pltpu.CompilerParams(vmem_limit_bytes=mib * MIB)


def cost(flops, nbytes):
    return pl.CostEstimate(flops=int(flops), bytes_accessed=int(nbytes), transcendentals=0)


def shaped(shape, dtype):
    return jax.ShapeDtypeStruct(shape, dtype)


def aligned(index, size):
    return pl.ds(pl.multiple_of(index * size, size), size)


def call(kernel, name, out_shape, in_specs, operands, flops=1e6, nbytes=1e6, deps=(), mib=8):
    def body(*refs):
        given = len(operands)
        kernel(*refs[:given], *refs[given + len(deps) :])

    return pl.pallas_call(
        body,
        out_shape=out_shape,
        in_specs=list(in_specs) + [hbm] * len(deps),
        out_specs=jax.tree.map(lambda _: vmem, out_shape),
        compiler_params=params(mib),
        cost_estimate=cost(flops, nbytes),
        name=name,
    )(*operands, *deps)


def once_there(name, values, deps):
    return pl.pallas_call(
        lambda *refs: None,
        out_shape=[shaped(v.shape, v.dtype) for v in values],
        in_specs=[anywhere] * (len(values) + len(deps)),
        out_specs=[anywhere] * len(values),
        input_output_aliases={i: i for i in range(len(values))},
        compiler_params=params(),
        cost_estimate=cost(1, 1),
        name=name,
    )(*values, *deps)


def piece_kernel(place_ref, first_ref, gate_ref, ids_ref, send_ref):
    send_ref[:EXP_H1, :] = (0.5 * first_ref[...]).T.astype(bf16)
    at = EXP_H1 + GATES
    send_ref[EXP_H1:at, :] = gate_ref[...].astype(bf16)
    ids, lines = ids_ref[...], ids_ref.shape[0]
    send_ref[at : at + lines, :] = (ids % 256).astype(f32).astype(bf16)
    send_ref[at + lines :, :] = (ids // 256).astype(f32).astype(bf16)


def count_kernel(digits_ref, counts_ref):
    lines = digits_ref.shape[1] // 2
    width = digits_ref.shape[2]
    high = lax.broadcasted_iota(jnp.int32, (counts_ref.shape[1], width), 0).astype(f32)
    low = lax.broadcasted_iota(jnp.int32, (LANES, width), 0).astype(f32)
    total = jnp.zeros(counts_ref.shape, f32)
    for q in range(QUADS):
        digits = digits_ref[q].astype(f32)
        ids = digits[:lines] + 256.0 * digits[lines:]
        ids_high = jnp.floor(ids * (1.0 / LANES))
        ids_low = ids - LANES * ids_high
        for r in range(lines):
            one_high = jnp.where(high == ids_high[r : r + 1], 1.0, 0.0).astype(bf16)
            one_low = jnp.where(low == ids_low[r : r + 1], 1.0, 0.0).astype(bf16)
            total = total + dot_nt(one_low, one_high)
    counts_ref[...] = total


LOW_TURNED = H1
LOW_TOWERS = 2 * H1
LOW_ROWS = LOW_TOWERS + 2 * TASKS * EXP_H2
WIDE_TWO = H1
WIDE_TOP = H1 + H2
WIDE_ROWS = WIDE_TOP + 3 * LANES


def prepare_kernel(second_ref, tower_ref, head_ref, bias_ref, ids_ref, labels_ref, low_ref, wide_ref, marks_ref):
    low_ref[:H1, :] = (0.5 * second_ref[...]).astype(bf16)
    for block in range(H1 // LANES):
        turned = (0.5 * second_ref[pl.ds(block * LANES, LANES), :]).T
        low_ref[pl.ds(LOW_TURNED + block * LANES, LANES), :] = turned.astype(bf16)
    tower = tower_ref[...]
    none = jnp.zeros((EXP_H2, TOWER), f32)
    left = jnp.concatenate([tower[:, :TOWER], none], axis=1)
    right = jnp.concatenate([none, tower[:, TOWER:]], axis=1)
    for i, block in enumerate((left, right, left.T, right.T)):
        low_ref[pl.ds(LOW_TOWERS + i * LANES, LANES), :] = block.astype(bf16)

    def column(row):
        return jnp.broadcast_to(row, (LANES, LANES)).T

    for r in range((H1 + H2) // LANES):
        wide_ref[pl.ds(r * LANES, LANES), :] = 0.5 * column(bias_ref[:, r * LANES : (r + 1) * LANES])
    at = H1 + H2
    wide_ref[pl.ds(WIDE_TOP, LANES), :] = column(bias_ref[:, at : at + LANES])
    wide_ref[pl.ds(WIDE_TOP + LANES, LANES), :] = column(head_ref[...])
    wide_ref[pl.ds(WIDE_TOP + 2 * LANES, LANES), :] = column(bias_ref[:, at + LANES : at + 2 * LANES])
    marks_ref[:1, :] = ids_ref[...]
    marks_ref[1:, :] = labels_ref[...]


def join_fields_kernel(*refs):
    sent, (bundle_ref, gate_ref) = refs[:FIELDS], refs[FIELDS:]
    width = sent[0].shape[1]
    for s, ref in enumerate(sent):
        at = slice(s * width, (s + 1) * width)
        bundle_ref[:EXP_H1, at] = ref[:EXP_H1, :]
        gate_ref[:, at] = ref[EXP_H1 : EXP_H1 + GATES, :]
        bundle_ref[EXP_H1:, at] = ref[EXP_H1 + GATES :, :]


def join_quads_kernel(*refs):
    bundles, refs = refs[:QUADS], refs[QUADS:]
    rows, gate_ref, (stack_ref, digits_ref, joined_ref, gate_out) = refs[:FIELDS], refs[FIELDS], refs[FIELDS + 1 :]
    for q, ref in enumerate(bundles):
        stack_ref[q] = ref[:EXP_H1, :]
        digits_ref[q] = ref[EXP_H1:, :]
    width = rows[0].shape[1]
    for s, ref in enumerate(rows):
        joined_ref[:, s * width : (s + 1) * width] = ref[...]
    gate_out[...] = gate_ref[...]


def rows_kernel(starts, place_ref, inputs_ref, *refs):
    outs, sems = refs[-1 - len(starts) * FIELDS : -1], refs[-1]
    rows = inputs_ref.shape[0] // FIELDS
    copies = []
    for i, out in enumerate(outs):
        chunk, s = divmod(i, FIELDS)
        at = pl.ds(lax.rem(place_ref[1] + s, FIELDS) * rows + starts[chunk], out.shape[0])
        copies.append(pltpu.make_async_copy(inputs_ref.at[at, :], out, sems.at[i]))
        copies[-1].start()
    for copy in copies:
        copy.wait()


def turn_kernel(stack_ref, out_ref):
    for q in range(QUADS):
        out_ref[:, q * EXP_H1 : (q + 1) * EXP_H1] = stack_ref[q].T


NSUM = 5


def layers_kernel(last, with_sums, ndeps, scale, low_row, nrows, place_ref, *refs):
    xs, refs = refs[:nrows], refs[nrows:]
    marks_ref, own_ref, other_ref, gate_ref, counts_a, counts_b, low_ref, wide_ref = refs[:8]
    refs = refs[8:]
    given = [None] * NSUM
    if with_sums:
        given, refs = refs[:NSUM], refs[NSUM:]
    refs = refs[ndeps:]
    d_ref, prob_ref, refs = refs[0], refs[1], refs[2:]
    sums, refs = refs[:NSUM], refs[NSUM:]
    if last:
        keep_ref, send_ref, refs = refs[0], refs[1], refs[2:]
    sum_first, sum_second, sum_tower, sum_bias, sum_top = sums
    hidden_ref, slope_ref, two_ref, slope_two_ref, gates_ref, d_gates_ref = refs
    rows = prob_ref.shape[1]
    mine = slice(low_row, low_row + rows)
    place = place_ref[0]

    def add(which, at, value):
        sums[which][at] = value if given[which] is None else given[which][at] + value

    def fold(values):
        out = values[:, :LANES]
        for at in range(LANES, values.shape[1], LANES):
            out = out + values[:, at : at + LANES]
        return out

    def wide(values):
        return jnp.concatenate([values] * (rows // LANES), axis=1)

    def silu_of_twice(half):
        swing = jnp.tanh(half)
        above = 1.0 + swing
        value = half * above
        return value, above + value * (1.0 - swing)

    ids = marks_ref[:1, mine]
    counts = counts_a[...] + counts_b[...]
    present = jnp.sum(jnp.where(counts > 0.0, 1.0, 0.0), keepdims=True)
    high = lax.broadcasted_iota(jnp.int32, (counts.shape[1], rows), 0)
    low = lax.broadcasted_iota(jnp.int32, (LANES, rows), 0)
    one_high = jnp.where(high == ids // LANES, 1.0, 0.0).astype(bf16)
    top_digit = jnp.floor(counts * (1.0 / 65536.0))
    counts = counts - 65536.0 * top_digit
    mid_digit = jnp.floor(counts * (1.0 / 256.0))
    low_digit = counts - 256.0 * mid_digit
    found = dot(low_digit.astype(bf16), one_high)
    found = found + 256.0 * dot(mid_digit.astype(bf16), one_high)
    found = found + 65536.0 * dot(top_digit.astype(bf16), one_high)
    found = jnp.sum(jnp.where(low == ids % LANES, found, 0.0), axis=0, keepdims=True)
    row_weight = scale / (present * found)

    inputs = jnp.concatenate([x[...] for x in xs], axis=1) if nrows > 1 else xs[0][...]
    turned_in = inputs.T
    logits = dot(gate_ref[...], turned_in).reshape(TASKS, EXPERTS, rows)
    shifted = jnp.exp(logits - jnp.max(logits, axis=1, keepdims=True))
    gates = shifted / jnp.sum(shifted, axis=1, keepdims=True)
    gates_ref[...] = gates.reshape(GATES, rows)
    slots = [(c, q) for c in range(2) for q in range(QUADS)]
    mixed = [jnp.zeros((EXP_H2, rows), f32) for _ in range(TASKS)]
    for t, (c, q) in enumerate(slots):
        e = place ^ (2 * q + c)
        one, two = pl.ds(t * EXP_H1, EXP_H1), pl.ds(t * EXP_H2, EXP_H2)
        weight = (other_ref if c else own_ref)[q]
        half_one = dot(weight, turned_in) + wide(wide_ref[aligned(e, EXP_H1), :])
        hidden, slope_ref[one, :] = silu_of_twice(half_one)
        hidden_low = hidden.astype(bf16)
        hidden_ref[one, :] = hidden_low
        at = pl.multiple_of(LOW_TURNED + e * EXP_H1, EXP_H1)
        turned = jnp.concatenate([low_ref[pl.ds(at, LANES), :], low_ref[pl.ds(at + LANES, LANES), :]], axis=1)
        at = pl.multiple_of(WIDE_TWO + e * EXP_H2, EXP_H2)
        half_two = dot(turned, hidden_low) + wide(wide_ref[pl.ds(at, EXP_H2), :])
        hidden, slope_two_ref[two, :] = silu_of_twice(half_two)
        two_ref[two, :] = hidden
        for k in range(TASKS):
            mixed[k] = mixed[k] + gates_ref[pl.ds(k * EXPERTS + e, 1), :] * hidden
    mixed_low = jnp.concatenate(mixed, axis=0).astype(bf16)
    at = LOW_TOWERS + TASKS * EXP_H2
    tower_fwd = jnp.concatenate([low_ref[at : at + LANES, :], low_ref[at + LANES :, :]], axis=1)
    tops = [wide_ref[WIDE_TOP + k * LANES : WIDE_TOP + (k + 1) * LANES, :] for k in range(3)]
    pre_tower = dot(tower_fwd, mixed_low) + wide(tops[0])
    logistic = sigmoid(pre_tower)
    upper = pre_tower * logistic
    slope_tower = logistic + upper * (1.0 - logistic)
    head = wide(tops[1])
    logit = jnp.sum((upper * head).reshape(TASKS, TOWER, rows), axis=1)
    logit = logit + wide(tops[2][:TASKS, :])
    prob = 1.0 / (1.0 + jnp.exp(-logit))
    prob_ref[...] = prob
    d_logit = row_weight * (prob - marks_ref[1:, mine].astype(f32))
    d_wide = jnp.broadcast_to(d_logit[:, None, :], (TASKS, TOWER, rows)).reshape(LANES, rows)
    d_tower = (d_wide * head * slope_tower).astype(bf16)
    add(4, 0, fold(d_tower.astype(f32)))
    add(4, 1, fold(d_wide * upper))
    low_rows = jnp.zeros((LANES - TASKS, LANES), f32)
    add(4, 2, jnp.concatenate([fold(d_logit), low_rows], axis=0))
    add(2, ..., dot_nt(mixed_low, d_tower))
    d_mixed = dot(low_ref[LOW_TOWERS : LOW_TOWERS + TASKS * EXP_H2, :], d_tower)
    parts = [d_mixed[k * EXP_H2 : (k + 1) * EXP_H2, :] for k in range(TASKS)]
    for t, (c, q) in enumerate(slots):
        e = place ^ (2 * q + c)
        one, two = pl.ds(t * EXP_H1, EXP_H1), pl.ds(t * EXP_H2, EXP_H2)
        hidden = two_ref[two, :]
        d_hidden = jnp.zeros((EXP_H2, rows), f32)
        for k in range(TASKS):
            at = pl.ds(k * EXPERTS + e, 1)
            d_gates_ref[at, :] = jnp.sum(parts[k] * hidden, axis=0, keepdims=True)
            d_hidden = d_hidden + gates_ref[at, :] * parts[k]
        d_two = d_hidden * slope_two_ref[two, :]
        at = pl.ds(pl.multiple_of(H1 + e * EXP_H2, EXP_H2), EXP_H2)
        add(3, (at, slice(None)), fold(d_two))
        d_two = d_two.astype(bf16)
        add(1, (two, slice(None)), dot_nt(d_two, hidden_ref[one, :]))
        d_one = dot(low_ref[aligned(e, EXP_H1), :], d_two) * slope_ref[one, :]
        add(3, (aligned(e, EXP_H1), slice(None)), fold(d_one))
        d_ref[one, :] = d_one.astype(bf16)
    d_gates = d_gates_ref[...].reshape(TASKS, EXPERTS, rows)
    centered = d_gates - jnp.sum(gates * d_gates, axis=1, keepdims=True)
    d_ref[pl.ds(H1, GATES), :] = (gates * centered).reshape(GATES, rows).astype(bf16)
    add(0, ..., dot(d_ref[...], inputs))

    if last:
        for t, (c, q) in enumerate(slots):
            one, two = pl.ds(t * EXP_H1, EXP_H1), pl.ds(t * EXP_H2, EXP_H2)
            out = send_ref if c else keep_ref
            for s in range(FIELDS):
                at = pl.ds(q * BIG + s * EXP_H1, EXP_H1)
                out[at, :] = (0.5 * sum_first[one, s * LANES : (s + 1) * LANES]).astype(bf16)
            out[pl.ds(q * BIG + FIELDS * EXP_H1, EXP_H1), :] = (0.5 * sum_second[two, :]).T.astype(bf16)
        ones = jnp.ones((8, LANES), f32)
        bias = dot_nt(0.5 * ones, sum_bias[...], lax.Precision.HIGHEST)[:1, :]
        lines = [bias[:, r * LANES : (r + 1) * LANES] for r in range((H1 + H2) // LANES)]
        lines += [dot_nt(ones, sum_top[k], lax.Precision.HIGHEST)[:1, :] for k in range(3)]
        lines += [jnp.zeros((1, LANES), f32)] * (8 * QUADS - len(lines))
        for out in (keep_ref, send_ref):
            at = QUADS * BIG
            for q in range(QUADS):
                block = sum_tower[pl.ds(q * TOWER_ROWS, TOWER_ROWS), :TOWER]
                below = sum_tower[pl.ds(EXP_H2 + q * TOWER_ROWS, TOWER_ROWS), TOWER:]
                out[pl.ds(at, TOWER_ROWS), :] = jnp.concatenate([block, below], axis=1).astype(bf16)
                at += TOWER_ROWS
                out[pl.ds(at, LINE_ROWS), :] = two_parts(jnp.concatenate(lines[8 * q : 8 * q + 8], axis=0))
                at += LINE_ROWS
                block = sum_first[pl.ds(H1, GATES), q * LANES : (q + 1) * LANES]
                out[pl.ds(at, GATE_ROWS), :] = block.astype(bf16)
                at += GATE_ROWS


def back_kernel(spans, *refs):
    d_refs, refs = refs[: len(spans)], refs[len(spans) :]
    own_ref, other_ref, gate_ref, out_own = refs[:4]
    half, at = H1 // 2, 0
    for (low, high), d_ref in zip(spans, d_refs):
        here = slice(low, high)
        turned = dot(own_ref[...], d_ref[:half, here]) + dot(other_ref[...], d_ref[half:H1, here])
        turned = turned + dot(gate_ref[...], d_ref[H1:, here])
        grads = turned.T
        width, rows = out_own.shape[1], pl.ds(at, high - low)
        out_own[rows, :] = grads[:, :width]
        for s, ref in enumerate(refs[-FIELDS + 1 :]):
            ref[rows, :] = grads[:, (s + 1) * width : (s + 2) * width].astype(bf16)
        at += high - low


def two_parts(lines):
    low = lines.astype(bf16)
    return jnp.concatenate([low.astype(f32), lines - low.astype(f32)], axis=0).astype(bf16)


def whole(parts):
    half = parts.shape[0] // 2
    return parts[:half] + parts[half:]


def add_cores_kernel(place_ref, keep_ref, got_ref, *outs):
    quad = place_ref[0] >> 1

    def both(at):
        return keep_ref[at, :].astype(f32), got_ref[at, :].astype(f32)

    for q, out in enumerate(outs):
        a, b = both(pl.ds(q * BIG, BIG))
        out[:BIG, :] = (a + b).astype(bf16)
        a, b = both(pl.ds(pl.multiple_of(QUADS * BIG + (quad ^ q) * SMALL, SMALL), SMALL))
        out[BIG:, :] = (a + b).astype(bf16)
        lines = slice(TOWER_ROWS, TOWER_ROWS + LINE_ROWS)
        out[BIG + TOWER_ROWS : BIG + TOWER_ROWS + LINE_ROWS, :] = two_parts(whole(a[lines]) + whole(b[lines]))


def add_quads_kernel(place_ref, *refs):
    parts, outs = refs[:QUADS], refs[QUADS:]
    quad, field = place_ref[0] >> 1, place_ref[1]

    def four(at):
        return [ref[at, :].astype(f32) for ref in parts]

    def total(at):
        a, b, c, d = four(at)
        return ((a + b) + (c + d)).astype(bf16)

    second = total(pl.ds(FIELDS * EXP_H1, EXP_H1))
    tower = total(pl.ds(BIG, TOWER_ROWS))
    a, b, c, d = [whole(v) for v in four(pl.ds(BIG + TOWER_ROWS, LINE_ROWS))]
    lines = two_parts((a + b) + (c + d))
    gate = total(pl.ds(PIECE - GATE_ROWS, GATE_ROWS))
    for s, out in enumerate(outs):
        out[:EXP_H1, :] = total(pl.ds(s * EXP_H1, EXP_H1))
        out[EXP_H1 : 2 * EXP_H1, :] = second
        at = 2 * EXP_H1
        out[at : at + TOWER_ROWS, :] = tower
        at += TOWER_ROWS
        out[at : at + LINE_ROWS, :] = lines
        out[at + LINE_ROWS :, :] = jnp.where(quad == s, gate, jnp.zeros_like(gate))


def add_fields_kernel(place_ref, *refs):
    parts, out = refs[:FIELDS], refs[FIELDS]
    odd = place_ref[1] % 2 == 1
    a, b, c, d = [ref[...].astype(f32) for ref in parts]

    def total(a, b, c, d):
        return (a + jnp.where(odd, d, b)) + (c + jnp.where(odd, b, d))

    out[...] = total(a, b, c, d).astype(bf16)
    lines = slice(2 * EXP_H1 + TOWER_ROWS, 2 * EXP_H1 + TOWER_ROWS + LINE_ROWS)
    out[lines, :] = two_parts(total(*[whole(v[lines]) for v in (a, b, c, d)]))


def join_done_kernel(place_ref, *refs):
    parts, (stack_ref, tower_ref, lines_ref, gate_ref) = refs[:QUADS], refs[QUADS:]
    quad = place_ref[0] >> 1
    for q, ref in enumerate(parts):
        stack_ref[q] = ref[: 2 * EXP_H1, :]
        at = 2 * EXP_H1
        tower_ref[aligned(quad ^ q, TOWER_ROWS), :] = ref[at : at + TOWER_ROWS, :].astype(f32)
        at += TOWER_ROWS
        lines_ref[aligned(quad ^ q, 8), :] = whole(ref[at : at + LINE_ROWS, :].astype(f32))
    a, b, c, d = [ref[2 * EXP_H1 + TOWER_ROWS + LINE_ROWS :, :].astype(f32) for ref in parts]
    gate_ref[...] = (a + b) + (c + d)


def assemble_kernel(start, place_ref, *refs):
    parts, (out_ref, wide_ref, sems) = refs[:FIELDS], refs[-3:]
    rows, size = out_ref.shape[0] // FIELDS, wide_ref.shape[1]
    copies = []
    for s, part in enumerate(parts):
        at = pl.ds(lax.rem(place_ref[1] + s, FIELDS) * rows + start, size)
        if s:
            wide_ref[s - 1] = part[...].astype(f32)
        source = wide_ref.at[s - 1] if s else part
        copies.append(pltpu.make_async_copy(source, out_ref.at[at, :], sems.at[s]))
        copies[-1].start()
    for copy in copies:
        copy.wait()


def update_kernel(core, place_ref, grads_ref, *refs):
    first_w, first_m, first_v, second_w, second_m, second_v, second_a = refs[:7]
    outs = refs[-8:]
    outs[7][...] = jnp.zeros((8, LANES), f32)
    expert = place_ref[0] ^ (2 * pl.program_id(0) + core)
    at = aligned(expert, EXP_H1)
    grads = grads_ref[pl.program_id(0)].astype(f32)
    new = adamw(first_w[:, at], first_m[:, at], first_v[:, at], grads[:EXP_H1].T)
    outs[0][...], outs[1][...], outs[2][...] = new
    new = adamw(second_w[at, :], second_m[at, :], second_v[at, :], grads[EXP_H1:])
    outs[3][...], outs[4][...], outs[5][...] = new
    outs[6][...] = blend(second_a[at, :], new[0])


def on_device(
    inputs,
    labels,
    user_ids,
    first_weight,
    first_mean,
    first_square,
    gate_weight,
    gate_mean,
    gate_square,
    second_weight,
    second_mean,
    second_square,
    tower_weight,
    tower_mean,
    tower_square,
    head_weight,
    head_mean,
    head_square,
    biases,
    bias_mean,
    bias_square,
    second_average,
    tower_average,
    head_average,
):
    nfield, nbatch = lax.axis_size("field"), lax.axis_size("batch")
    field, batch = lax.axis_index("field"), lax.axis_index("batch")
    rows_dev, columns = inputs.shape
    rows = rows_dev // nfield
    width = nfield * columns
    users_total = rows_dev * nbatch // USER_ROWS
    place = jnp.stack([batch % GROUP, field]).astype(jnp.int32)

    def shift(value, by):
        return lax.ppermute(value, "field", [(i, (i + by) % nfield) for i in range(nfield)])

    def cross(value, mask):
        return lax.ppermute(value, "batch", [(i, i ^ mask) for i in range(nbatch)])

    def from_fields(value):
        return [value] + [shift(value, s) for s in range(1, nfield)]

    def from_quads(value):
        return [value] + [cross(value, 2 * q) for q in range(1, QUADS)]

    starts = [0]
    for part in CHUNKS:
        starts.append(starts[-1] + part * rows // 16)
    nchunks = len(CHUNKS)

    ids = user_ids.reshape(1, rows)
    labels_t = labels.T
    expert_block = pl.BlockSpec((columns, EXP_H1), lambda i, place_ref: (0, place_ref[0]))
    high = users_total // LANES
    lines = 2 * rows // LANES
    sent = pl.pallas_call(
        piece_kernel,
        grid_spec=pltpu.PrefetchScalarGridSpec(
            num_scalar_prefetch=1, grid=(1,), in_specs=[expert_block, vmem, vmem], out_specs=vmem
        ),
        out_shape=shaped((EXP_H1 + GATES + lines, columns), bf16),
        compiler_params=params(),
        cost_estimate=cost(1e6, 1e5),
        name="first_piece",
    )(place, first_weight, gate_weight.T, user_ids.reshape(rows // LANES, LANES))
    def own_rows(low, high, deps):
        count = (high - low) * nfield
        return pl.pallas_call(
            functools.partial(rows_kernel, starts[low:high]),
            out_shape=[shaped((starts[c + 1] - starts[c], columns), bf16) for c in range(low, high) for _ in range(nfield)],
            in_specs=[smem, anywhere] + [anywhere] * len(deps),
            out_specs=[anywhere] * count,
            scratch_shapes=[pltpu.SemaphoreType.DMA((count,))],
            compiler_params=params(),
            cost_estimate=cost(1e3, 1e3),
            name="own_rows",
        )(place, inputs, *deps)

    def exchange_rows(mine, *others):
        return [mine] + [shift(o, s + 1) for s, o in enumerate(others)]

    arrived = [exchange_rows(*own_rows(0, 1, []))]
    later_rows = own_rows(1, nchunks, [sent])
    prepared = call(
        prepare_kernel,
        "prepare_weights",
        [shaped((LOW_ROWS, LANES), bf16), shaped((WIDE_ROWS, LANES), f32), shaped((1 + TASKS, rows), jnp.int32)],
        [vmem] * 6,
        [
            second_weight,
            tower_weight,
            head_weight.reshape(1, LANES),
            jnp.pad(biases, (0, LANES - TASKS)).reshape(1, -1),
            ids,
            labels_t,
        ],
    )
    bundle, gate_t = call(
        join_fields_kernel,
        "join_fields",
        [shaped((EXP_H1 + lines, width), bf16), shaped((GATES, width), bf16)],
        [vmem] * FIELDS,
        from_fields(sent),
        deps=[later_rows[0], prepared[0], *arrived[0][1:]],
    )
    mine, *others = later_rows[:nfield]
    arrived.append(exchange_rows(mine, *once_there("rows_to_send", others, [gate_t])))
    own, digits, joined, gate_t = call(
        join_quads_kernel,
        "join_quads",
        [
            shaped((QUADS, EXP_H1, width), bf16),
            shaped((QUADS, lines, width), bf16),
            shaped((starts[1], width), bf16),
            shaped((GATES, width), bf16),
        ],
        [vmem] * (QUADS + FIELDS + 1),
        [*from_quads(bundle), *arrived[0], gate_t],
        deps=arrived[1][1:],
    )
    arrived[0] = [joined]
    mine, *others = later_rows[nfield:]
    arrived.append(exchange_rows(mine, *once_there("rows_to_send", others, [digits])))
    counts = call(count_kernel, "user_counts", shaped((LANES, high), f32), [vmem], [digits])
    hop = GROUP
    while hop < nbatch:
        counts = counts + cross(counts, hop)
        hop *= 2
    counts_other = cross(counts, 1)
    other = cross(own, 1)
    turned_own = call(turn_kernel, "turn_first", shaped((width, H1 // 2), bf16), [vmem], [own])
    turned_other = cross(turned_own, 1)

    sum_shapes = [
        shaped((H1 + GATES, width), f32),
        shaped((H2, EXP_H1), f32),
        shaped((TASKS * EXP_H2, TASKS * TOWER), f32),
        shaped((H1 + H2, LANES), f32),
        shaped((3, LANES, LANES), f32),
    ]

    def run_layers(c, sums, deps):
        last = c == nchunks - 1
        low, chunk = starts[c], starts[c + 1] - starts[c]
        low_weights, wide_biases, marks = prepared
        operands = [*arrived[c], marks, own, other, gate_t, counts, counts_other, low_weights, wide_biases]
        out_shape = [shaped((H1 + GATES, chunk), bf16), shaped((TASKS, chunk), f32)] + sum_shapes
        if last:
            out_shape += [shaped((QUADS * PIECE, LANES), bf16)] * 2

        def once(shape):
            return pl.BlockSpec(shape, lambda i: (0,) * len(shape), pipeline_mode=pl.Buffered(1))

        return pl.pallas_call(
            functools.partial(layers_kernel, last, bool(sums), len(deps), loss_scale * users_total, low, len(arrived[c])),
            grid=(1,),
            out_shape=out_shape,
            in_specs=[smem]
            + [once(o.shape) for o in operands]
            + [vmem] * len(sums)
            + [hbm] * len(deps),
            out_specs=[once(o.shape) for o in out_shape[:2]]
            + [vmem] * NSUM
            + [once(o.shape) for o in out_shape[2 + NSUM :]],
            input_output_aliases={1 + len(operands) + i: 2 + i for i in range(len(sums))},
            scratch_shapes=[
                pltpu.VMEM((H1, chunk), bf16),
                pltpu.VMEM((H1, chunk), f32),
                pltpu.VMEM((H2, chunk), f32),
                pltpu.VMEM((H2, chunk), f32),
                pltpu.VMEM((GATES, chunk), f32),
                pltpu.VMEM((GATES, chunk), f32),
            ],
            compiler_params=params(LAYERS_MIB),
            cost_estimate=cost(LAYERS_COST * chunk, 1e3),
            name="layers",
        )(place, *operands, *sums, *deps)

    gate_all = gate_t.T

    bounds = [0]
    for part in RETURNS:
        bounds.append(bounds[-1] + part * rows // 16)

    def give_back(i, deps):
        spans, taken = [], []
        for c in range(nchunks):
            low, high = max(bounds[i], starts[c]), min(bounds[i + 1], starts[c + 1])
            if low < high:
                spans.append((low - starts[c], high - starts[c]))
                taken.append(d_chunks[c])
        size = bounds[i + 1] - bounds[i]
        mine, *others = call(
            functools.partial(back_kernel, spans),
            "input_gradients",
            [shaped((size, columns), f32)] + [shaped((size, columns), bf16)] * (nfield - 1),
            [vmem] * (len(taken) + 3),
            [*taken, turned_own, turned_other, gate_all],
            flops=BACK_COST * size,
            deps=deps,
            mib=12,
        )
        return [mine] + [shift(o, -(s + 1)) for s, o in enumerate(others)]

    sums, probs, d_chunks, returned = [], [], [], []
    for c in range(nchunks):
        if c == nchunks - 1:
            returned.append(give_back(0, []))
        d_chunk, prob, *sums = run_layers(c, sums, [r[0] for r in returned])
        probs.append(prob)
        d_chunks.append(d_chunk)
    keep, send = sums[NSUM:]
    returned.append(give_back(1, [keep]))
    (send,) = once_there("gradients_to_send", [send], returned[0][1:])

    pieces = call(
        add_cores_kernel,
        "add_cores",
        [shaped((PIECE, LANES), bf16)] * QUADS,
        [smem, vmem, vmem],
        [place, keep, cross(send, 1)],
        deps=returned[1][:1],
    )
    parts = [pieces[0]] + [cross(pieces[q], 2 * q) for q in range(1, QUADS)]
    hop = GROUP
    while hop < nbatch:
        parts = [(p.astype(f32) + cross(p, hop).astype(f32)).astype(bf16) for p in parts]
        hop *= 2
    blocks = call(
        add_quads_kernel,
        "add_quads",
        [shaped((2 * EXP_H1 + SMALL, LANES), bf16)] * nfield,
        [smem] + [vmem] * QUADS,
        [place] + parts,
        deps=returned[1][1:],
    )
    returned.append(give_back(2, [blocks[0]]))
    def assemble(i, before, deps):
        return pl.pallas_call(
            functools.partial(assemble_kernel, bounds[i]),
            out_shape=[shaped((rows_dev, columns), f32)],
            in_specs=[smem, anywhere] + [vmem] * (nfield - 1) + [hbm] * (len(before) + len(deps)),
            out_specs=[hbm],
            input_output_aliases={1 + nfield: 0} if before else {},
            scratch_shapes=[
                pltpu.VMEM((nfield - 1, bounds[i + 1] - bounds[i], columns), f32),
                pltpu.SemaphoreType.DMA((nfield,)),
            ],
            compiler_params=params(),
            cost_estimate=cost(1e3, 1e3),
            name="assemble_input_grad",
        )(place, *returned[i], *before, *deps)

    input_grad = assemble(0, [], [blocks[0]])
    input_grad = assemble(1, input_grad, [blocks[0]])
    done = call(
        add_fields_kernel,
        "add_fields",
        shaped((2 * EXP_H1 + SMALL, LANES), bf16),
        [smem] + [vmem] * nfield,
        [place, blocks[0]] + [shift(blocks[s], -s) for s in range(1, nfield)],
        deps=[returned[2][0], *input_grad],
    )
    done_own, g_tower, lines, g_gate = call(
        join_done_kernel,
        "join_gradients",
        [
            shaped((QUADS, 2 * EXP_H1, LANES), bf16),
            shaped((LANES, LANES), f32),
            shaped((8 * QUADS, LANES), f32),
            shaped((GATES, columns), f32),
        ],
        [smem] + [vmem] * QUADS,
        [place] + from_quads(done),
    )
    done_other = cross(done_own, 1)

    def run_update(core, grads, before):
        first_spec = pl.BlockSpec((columns, EXP_H1), lambda q, place_ref: (0, place_ref[0] ^ (2 * q + core)))
        second_spec = pl.BlockSpec((EXP_H1, EXP_H2), lambda q, place_ref: (place_ref[0] ^ (2 * q + core), 0))
        operands = [
            grads,
            first_weight,
            first_mean,
            first_square,
            second_weight,
            second_mean,
            second_square,
            second_average,
        ]
        specs = [first_spec] * 3 + [second_spec] * 4
        before = list(before or [])[:7]
        return pl.pallas_call(
            functools.partial(update_kernel, core),
            grid_spec=pltpu.PrefetchScalarGridSpec(
                num_scalar_prefetch=1,
                grid=(QUADS,),
                in_specs=[vmem] * len(operands) + [anywhere] * len(before),
                out_specs=specs + [pl.BlockSpec((8, LANES), lambda q, place_ref: (0, 0))],
            ),
            out_shape=[shaped((columns, H1), f32)] * 3
            + [shaped((H1, EXP_H2), f32)] * 4
            + [shaped((8, LANES), f32)],
            input_output_aliases={1 + len(operands) + i: i for i in range(len(before))},
            compiler_params=params(),
            cost_estimate=cost(1e6, 8e6),
            name="update_layers",
        )(place, *operands, *before)

    updated_half = run_update(0, done_own, None)
    updated = run_update(1, done_other, updated_half)
    new_first, new_second, avg_second = updated[:3], updated[3:6], updated[6]

    at = (H1 + H2) // LANES
    g_head = lines[at + 1]
    g_bias = jnp.concatenate([lines[: at + 1].reshape(-1), lines[at + 2, :TASKS]])
    new_gate = adamw(gate_weight, gate_mean, gate_square, g_gate.T)
    new_tower = adamw(tower_weight, tower_mean, tower_square, g_tower)
    avg_tower = blend(tower_average, new_tower[0])
    new_head = adamw(head_weight, head_mean, head_square, g_head)
    avg_head = blend(head_average, new_head[0])
    new_bias = adamw(biases, bias_mean, bias_square, g_bias)

    (input_grad,) = assemble(2, input_grad, [updated[7]])
    predicted = jnp.concatenate(probs, axis=1).T
    return (
        predicted,
        input_grad,
        *new_first,
        *new_gate,
        *new_second,
        *new_tower,
        *new_head,
        *new_bias,
        avg_second,
        avg_tower,
        avg_head,
    )


def solution(mesh):
    fields, copied = P("field", None), P()
    rows = P(("batch", "field"), None)
    in_specs = (
        (P("batch", "field"), rows, P(("batch", "field"))) + (fields,) * 6 + (copied,) * 15
    )
    out_specs = (rows, P("batch", "field")) + (fields,) * 6 + (copied,) * 15
    return jax.shard_map(
        on_device, mesh=mesh, in_specs=in_specs, out_specs=out_specs, check_vma=False
    )
```

```python
import functools

import jax
import jax.numpy as jnp
from jax import lax
from jax.experimental import pallas as pl
from jax.experimental.pallas import tpu as pltpu
from jax.sharding import PartitionSpec as P

EXPERTS = 8
EXP_H1 = 256
EXP_H2 = 128
TASKS = 2
TOWER = 64
USER_ROWS = 4
STEP = 10
H1 = 2048
H2 = 1024
GATES = TASKS * EXPERTS
LANES = 128
GROUP = 8
QUADS = GROUP // 2
CHUNKS = (4, 6, 6)
RETURNS = (4, 6, 6)
MIB = 1024 * 1024
LAYERS_MIB = 32
FIELDS = 4
BIG = (FIELDS + 1) * EXP_H1
TOWER_ROWS, LINE_ROWS, GATE_ROWS = 32, 16, 16
SMALL = TOWER_ROWS + LINE_ROWS + GATE_ROWS
PIECE = BIG + SMALL

beta_one = 0.9
beta_two = 0.999
learn_rate = 0.1
decay_rate = 0.01
adam_eps = 1e-08
average_rate = 0.8
loss_scale = 512.0

LAYERS_COST = 1e7
BACK_COST = 1e3

f32 = jnp.float32
bf16 = jnp.bfloat16
smem = pl.BlockSpec(memory_space=pltpu.SMEM)
vmem = pl.BlockSpec(memory_space=pltpu.VMEM)
anywhere = pl.BlockSpec(memory_space=pl.ANY)
hbm = pl.BlockSpec(memory_space=pltpu.HBM)


def sigmoid(values):
    return 0.5 * jnp.tanh(0.5 * values) + 0.5


def dot(left, right):
    return jnp.dot(left, right, preferred_element_type=f32)


def dot_nt(left, right, precision=None):
    return lax.dot_general(
        left, right, (((1,), (1,)), ((), ())), precision=precision, preferred_element_type=f32
    )


def adamw(weight, moment, square, gradient):
    new_moment = beta_one * moment + (1.0 - beta_one) * gradient
    new_square = beta_two * square + (1.0 - beta_two) * gradient * gradient
    moment_hat = new_moment / (1.0 - beta_one**STEP)
    square_hat = new_square / (1.0 - beta_two**STEP)
    new_weight = weight - learn_rate * (
        moment_hat / (jnp.sqrt(square_hat) + adam_eps) + decay_rate * weight
    )
    return (new_weight, new_moment, new_square)


def blend(average, weight):
    return average_rate * average + (1.0 - average_rate) * weight


def params(mib=8):
    return pltpu.CompilerParams(vmem_limit_bytes=mib * MIB)


def cost(flops, nbytes):
    return pl.CostEstimate(flops=int(flops), bytes_accessed=int(nbytes), transcendentals=0)


def shaped(shape, dtype):
    return jax.ShapeDtypeStruct(shape, dtype)


def aligned(index, size):
    return pl.ds(pl.multiple_of(index * size, size), size)


def call(kernel, name, out_shape, in_specs, operands, flops=1e6, nbytes=1e6, deps=(), mib=8):
    def body(*refs):
        given = len(operands)
        kernel(*refs[:given], *refs[given + len(deps) :])

    return pl.pallas_call(
        body,
        out_shape=out_shape,
        in_specs=list(in_specs) + [hbm] * len(deps),
        out_specs=jax.tree.map(lambda _: vmem, out_shape),
        compiler_params=params(mib),
        cost_estimate=cost(flops, nbytes),
        name=name,
    )(*operands, *deps)


def once_there(name, values, deps):
    return pl.pallas_call(
        lambda *refs: None,
        out_shape=[shaped(v.shape, v.dtype) for v in values],
        in_specs=[hbm] * (len(values) + len(deps)),
        out_specs=[hbm] * len(values),
        input_output_aliases={i: i for i in range(len(values))},
        compiler_params=params(),
        cost_estimate=cost(1, 1),
        name=name,
    )(*values, *deps)


def piece_kernel(place_ref, first_ref, gate_ref, ids_ref, send_ref):
    send_ref[:EXP_H1, :] = (0.5 * first_ref[...]).T.astype(bf16)
    at = EXP_H1 + GATES
    send_ref[EXP_H1:at, :] = gate_ref[...].astype(bf16)
    ids, lines = ids_ref[...], ids_ref.shape[0]
    send_ref[at : at + lines, :] = (ids % 256).astype(f32).astype(bf16)
    send_ref[at + lines :, :] = (ids // 256).astype(f32).astype(bf16)


def count_kernel(digits_ref, counts_ref):
    lines = digits_ref.shape[1] // 2
    width = digits_ref.shape[2]
    high = lax.broadcasted_iota(jnp.int32, (counts_ref.shape[1], width), 0).astype(f32)
    low = lax.broadcasted_iota(jnp.int32, (LANES, width), 0).astype(f32)
    total = jnp.zeros(counts_ref.shape, f32)
    for q in range(QUADS):
        digits = digits_ref[q].astype(f32)
        ids = digits[:lines] + 256.0 * digits[lines:]
        ids_high = jnp.floor(ids * (1.0 / LANES))
        ids_low = ids - LANES * ids_high
        for r in range(lines):
            one_high = jnp.where(high == ids_high[r : r + 1], 1.0, 0.0).astype(bf16)
            one_low = jnp.where(low == ids_low[r : r + 1], 1.0, 0.0).astype(bf16)
            total = total + dot_nt(one_low, one_high)
    counts_ref[...] = total


LOW_TURNED = H1
LOW_TOWERS = 2 * H1
LOW_ROWS = LOW_TOWERS + 2 * TASKS * EXP_H2
WIDE_TWO = H1
WIDE_TOP = H1 + H2
WIDE_ROWS = WIDE_TOP + 3 * LANES


def prepare_kernel(second_ref, tower_ref, head_ref, bias_ref, ids_ref, labels_ref, low_ref, wide_ref, marks_ref):
    low_ref[:H1, :] = (0.5 * second_ref[...]).astype(bf16)
    for block in range(H1 // LANES):
        turned = (0.5 * second_ref[pl.ds(block * LANES, LANES), :]).T
        low_ref[pl.ds(LOW_TURNED + block * LANES, LANES), :] = turned.astype(bf16)
    tower = tower_ref[...]
    none = jnp.zeros((EXP_H2, TOWER), f32)
    left = jnp.concatenate([tower[:, :TOWER], none], axis=1)
    right = jnp.concatenate([none, tower[:, TOWER:]], axis=1)
    for i, block in enumerate((left, right, left.T, right.T)):
        low_ref[pl.ds(LOW_TOWERS + i * LANES, LANES), :] = block.astype(bf16)

    def column(row):
        return jnp.broadcast_to(row, (LANES, LANES)).T

    for r in range((H1 + H2) // LANES):
        wide_ref[pl.ds(r * LANES, LANES), :] = 0.5 * column(bias_ref[:, r * LANES : (r + 1) * LANES])
    at = H1 + H2
    wide_ref[pl.ds(WIDE_TOP, LANES), :] = column(bias_ref[:, at : at + LANES])
    wide_ref[pl.ds(WIDE_TOP + LANES, LANES), :] = column(head_ref[...])
    wide_ref[pl.ds(WIDE_TOP + 2 * LANES, LANES), :] = column(bias_ref[:, at + LANES : at + 2 * LANES])
    marks_ref[:1, :] = ids_ref[...]
    marks_ref[1:, :] = labels_ref[...]


def join_fields_kernel(*refs):
    sent, (bundle_ref, gate_ref) = refs[:FIELDS], refs[FIELDS:]
    width = sent[0].shape[1]
    for s, ref in enumerate(sent):
        at = slice(s * width, (s + 1) * width)
        bundle_ref[:EXP_H1, at] = ref[:EXP_H1, :]
        gate_ref[:, at] = ref[EXP_H1 : EXP_H1 + GATES, :]
        bundle_ref[EXP_H1:, at] = ref[EXP_H1 + GATES :, :]


def join_quads_kernel(*refs):
    bundles, refs = refs[:QUADS], refs[QUADS:]
    rows, gate_ref, (stack_ref, digits_ref, joined_ref, gate_out) = refs[:FIELDS], refs[FIELDS], refs[FIELDS + 1 :]
    for q, ref in enumerate(bundles):
        stack_ref[q] = ref[:EXP_H1, :]
        digits_ref[q] = ref[EXP_H1:, :]
    width = rows[0].shape[1]
    for s, ref in enumerate(rows):
        joined_ref[:, s * width : (s + 1) * width] = ref[...]
    gate_out[...] = gate_ref[...]


def rows_kernel(starts, place_ref, inputs_ref, *refs):
    outs, sems = refs[-1 - len(starts) * FIELDS : -1], refs[-1]
    rows = inputs_ref.shape[0] // FIELDS
    copies = []
    for i, out in enumerate(outs):
        chunk, s = divmod(i, FIELDS)
        at = pl.ds(lax.rem(place_ref[1] + s, FIELDS) * rows + starts[chunk], out.shape[0])
        copies.append(pltpu.make_async_copy(inputs_ref.at[at, :], out, sems.at[i]))
        copies[-1].start()
    for copy in copies:
        copy.wait()


def turn_kernel(stack_ref, gate_ref, out_ref, gate_out):
    gate_out[...] = gate_ref[...].T
    for q in range(QUADS):
        out_ref[:, q * EXP_H1 : (q + 1) * EXP_H1] = stack_ref[q].T


NSUM = 5


def layers_kernel(last, with_sums, ndeps, scale, low_row, nrows, place_ref, *refs):
    xs, refs = refs[:nrows], refs[nrows:]
    marks_ref, own_ref, other_ref, gate_ref, counts_a, counts_b, low_ref, wide_ref = refs[:8]
    refs = refs[8:]
    given = [None] * NSUM
    if with_sums:
        given, refs = refs[:NSUM], refs[NSUM:]
    refs = refs[ndeps:]
    d_ref, prob_ref, refs = refs[0], refs[1], refs[2:]
    sums, refs = refs[:NSUM], refs[NSUM:]
    if last:
        keep_ref, send_ref, refs = refs[0], refs[1], refs[2:]
    sum_first, sum_second, sum_tower, sum_bias, sum_top = sums
    hidden_ref, slope_ref, two_ref, slope_two_ref, gates_ref, d_gates_ref = refs
    rows = prob_ref.shape[1]
    mine = slice(low_row, low_row + rows)
    place = place_ref[0]

    def add(which, at, value):
        sums[which][at] = value if given[which] is None else given[which][at] + value

    def fold(values):
        out = values[:, :LANES]
        for at in range(LANES, values.shape[1], LANES):
            out = out + values[:, at : at + LANES]
        return out

    def wide(values):
        return jnp.concatenate([values] * (rows // LANES), axis=1)

    def silu_of_twice(half):
        swing = jnp.tanh(half)
        above = 1.0 + swing
        value = half * above
        return value, above + value * (1.0 - swing)

    ids = marks_ref[:1, mine]
    counts = counts_a[...] + counts_b[...]
    present = jnp.sum(jnp.where(counts > 0.0, 1.0, 0.0), keepdims=True)
    high = lax.broadcasted_iota(jnp.int32, (counts.shape[1], rows), 0)
    low = lax.broadcasted_iota(jnp.int32, (LANES, rows), 0)
    one_high = jnp.where(high == ids // LANES, 1.0, 0.0).astype(bf16)
    top_digit = jnp.floor(counts * (1.0 / 65536.0))
    counts = counts - 65536.0 * top_digit
    mid_digit = jnp.floor(counts * (1.0 / 256.0))
    low_digit = counts - 256.0 * mid_digit
    found = dot(low_digit.astype(bf16), one_high)
    found = found + 256.0 * dot(mid_digit.astype(bf16), one_high)
    found = found + 65536.0 * dot(top_digit.astype(bf16), one_high)
    found = jnp.sum(jnp.where(low == ids % LANES, found, 0.0), axis=0, keepdims=True)
    row_weight = scale / (present * found)

    inputs = jnp.concatenate([x[...] for x in xs], axis=1) if nrows > 1 else xs[0][...]
    turned_in = inputs.T
    logits = dot(gate_ref[...], turned_in).reshape(TASKS, EXPERTS, rows)
    shifted = jnp.exp(logits - jnp.max(logits, axis=1, keepdims=True))
    gates = shifted / jnp.sum(shifted, axis=1, keepdims=True)
    gates_ref[...] = gates.reshape(GATES, rows)
    slots = [(c, q) for c in range(2) for q in range(QUADS)]
    mixed = [jnp.zeros((EXP_H2, rows), f32) for _ in range(TASKS)]
    for t, (c, q) in enumerate(slots):
        e = place ^ (2 * q + c)
        one, two = pl.ds(t * EXP_H1, EXP_H1), pl.ds(t * EXP_H2, EXP_H2)
        weight = (other_ref if c else own_ref)[q]
        half_one = dot(weight, turned_in) + wide(wide_ref[aligned(e, EXP_H1), :])
        hidden, slope_ref[one, :] = silu_of_twice(half_one)
        hidden_low = hidden.astype(bf16)
        hidden_ref[one, :] = hidden_low
        at = pl.multiple_of(LOW_TURNED + e * EXP_H1, EXP_H1)
        turned = jnp.concatenate([low_ref[pl.ds(at, LANES), :], low_ref[pl.ds(at + LANES, LANES), :]], axis=1)
        at = pl.multiple_of(WIDE_TWO + e * EXP_H2, EXP_H2)
        half_two = dot(turned, hidden_low) + wide(wide_ref[pl.ds(at, EXP_H2), :])
        hidden, slope_two_ref[two, :] = silu_of_twice(half_two)
        two_ref[two, :] = hidden
        for k in range(TASKS):
            mixed[k] = mixed[k] + gates_ref[pl.ds(k * EXPERTS + e, 1), :] * hidden
    mixed_low = jnp.concatenate(mixed, axis=0).astype(bf16)
    at = LOW_TOWERS + TASKS * EXP_H2
    tower_fwd = jnp.concatenate([low_ref[at : at + LANES, :], low_ref[at + LANES :, :]], axis=1)
    tops = [wide_ref[WIDE_TOP + k * LANES : WIDE_TOP + (k + 1) * LANES, :] for k in range(3)]
    pre_tower = dot(tower_fwd, mixed_low) + wide(tops[0])
    logistic = sigmoid(pre_tower)
    upper = pre_tower * logistic
    slope_tower = logistic + upper * (1.0 - logistic)
    head = wide(tops[1])
    logit = jnp.sum((upper * head).reshape(TASKS, TOWER, rows), axis=1)
    logit = logit + wide(tops[2][:TASKS, :])
    prob = 1.0 / (1.0 + jnp.exp(-logit))
    prob_ref[...] = prob
    d_logit = row_weight * (prob - marks_ref[1:, mine].astype(f32))
    d_wide = jnp.broadcast_to(d_logit[:, None, :], (TASKS, TOWER, rows)).reshape(LANES, rows)
    d_tower = (d_wide * head * slope_tower).astype(bf16)
    add(4, 0, fold(d_tower.astype(f32)))
    add(4, 1, fold(d_wide * upper))
    low_rows = jnp.zeros((LANES - TASKS, LANES), f32)
    add(4, 2, jnp.concatenate([fold(d_logit), low_rows], axis=0))
    add(2, ..., dot_nt(mixed_low, d_tower))
    d_mixed = dot(low_ref[LOW_TOWERS : LOW_TOWERS + TASKS * EXP_H2, :], d_tower)
    parts = [d_mixed[k * EXP_H2 : (k + 1) * EXP_H2, :] for k in range(TASKS)]
    for t, (c, q) in enumerate(slots):
        e = place ^ (2 * q + c)
        one, two = pl.ds(t * EXP_H1, EXP_H1), pl.ds(t * EXP_H2, EXP_H2)
        hidden = two_ref[two, :]
        d_hidden = jnp.zeros((EXP_H2, rows), f32)
        for k in range(TASKS):
            at = pl.ds(k * EXPERTS + e, 1)
            d_gates_ref[at, :] = jnp.sum(parts[k] * hidden, axis=0, keepdims=True)
            d_hidden = d_hidden + gates_ref[at, :] * parts[k]
        d_two = d_hidden * slope_two_ref[two, :]
        at = pl.ds(pl.multiple_of(H1 + e * EXP_H2, EXP_H2), EXP_H2)
        add(3, (at, slice(None)), fold(d_two))
        d_two = d_two.astype(bf16)
        add(1, (two, slice(None)), dot_nt(d_two, hidden_ref[one, :]))
        d_one = dot(low_ref[aligned(e, EXP_H1), :], d_two) * slope_ref[one, :]
        add(3, (aligned(e, EXP_H1), slice(None)), fold(d_one))
        d_ref[one, :] = d_one.astype(bf16)
    d_gates = d_gates_ref[...].reshape(TASKS, EXPERTS, rows)
    centered = d_gates - jnp.sum(gates * d_gates, axis=1, keepdims=True)
    d_ref[pl.ds(H1, GATES), :] = (gates * centered).reshape(GATES, rows).astype(bf16)
    add(0, ..., dot(d_ref[...], inputs))

    if last:
        for t, (c, q) in enumerate(slots):
            one, two = pl.ds(t * EXP_H1, EXP_H1), pl.ds(t * EXP_H2, EXP_H2)
            out = send_ref if c else keep_ref
            for s in range(FIELDS):
                at = pl.ds(q * BIG + s * EXP_H1, EXP_H1)
                out[at, :] = (0.5 * sum_first[one, s * LANES : (s + 1) * LANES]).astype(bf16)
            out[pl.ds(q * BIG + FIELDS * EXP_H1, EXP_H1), :] = (0.5 * sum_second[two, :]).T.astype(bf16)
        ones = jnp.ones((8, LANES), f32)
        bias = dot_nt(0.5 * ones, sum_bias[...], lax.Precision.HIGHEST)[:1, :]
        lines = [bias[:, r * LANES : (r + 1) * LANES] for r in range((H1 + H2) // LANES)]
        lines += [dot_nt(ones, sum_top[k], lax.Precision.HIGHEST)[:1, :] for k in range(3)]
        lines += [jnp.zeros((1, LANES), f32)] * (8 * QUADS - len(lines))
        for out in (keep_ref, send_ref):
            at = QUADS * BIG
            for q in range(QUADS):
                block = sum_tower[pl.ds(q * TOWER_ROWS, TOWER_ROWS), :TOWER]
                below = sum_tower[pl.ds(EXP_H2 + q * TOWER_ROWS, TOWER_ROWS), TOWER:]
                out[pl.ds(at, TOWER_ROWS), :] = jnp.concatenate([block, below], axis=1).astype(bf16)
                at += TOWER_ROWS
                out[pl.ds(at, LINE_ROWS), :] = two_parts(jnp.concatenate(lines[8 * q : 8 * q + 8], axis=0))
                at += LINE_ROWS
                block = sum_first[pl.ds(H1, GATES), q * LANES : (q + 1) * LANES]
                out[pl.ds(at, GATE_ROWS), :] = block.astype(bf16)
                at += GATE_ROWS


def back_kernel(spans, *refs):
    d_refs, refs = refs[: len(spans)], refs[len(spans) :]
    own_ref, other_ref, gate_ref, out_own = refs[:4]
    half, at = H1 // 2, 0
    for (low, high), d_ref in zip(spans, d_refs):
        here = slice(low, high)
        turned = dot(own_ref[...], d_ref[:half, here]) + dot(other_ref[...], d_ref[half:H1, here])
        turned = turned + dot(gate_ref[...], d_ref[H1:, here])
        grads = turned.T
        width, rows = out_own.shape[1], pl.ds(at, high - low)
        out_own[rows, :] = grads[:, :width]
        for s, ref in enumerate(refs[-FIELDS + 1 :]):
            ref[rows, :] = grads[:, (s + 1) * width : (s + 2) * width].astype(bf16)
        at += high - low


def two_parts(lines):
    low = lines.astype(bf16)
    return jnp.concatenate([low.astype(f32), lines - low.astype(f32)], axis=0).astype(bf16)


def whole(parts):
    half = parts.shape[0] // 2
    return parts[:half] + parts[half:]


def add_cores_kernel(place_ref, keep_ref, got_ref, *outs):
    quad = place_ref[0] >> 1

    def both(at):
        return keep_ref[at, :].astype(f32), got_ref[at, :].astype(f32)

    for q, out in enumerate(outs):
        a, b = both(pl.ds(q * BIG, BIG))
        out[:BIG, :] = (a + b).astype(bf16)
        a, b = both(pl.ds(pl.multiple_of(QUADS * BIG + (quad ^ q) * SMALL, SMALL), SMALL))
        out[BIG:, :] = (a + b).astype(bf16)
        lines = slice(TOWER_ROWS, TOWER_ROWS + LINE_ROWS)
        out[BIG + TOWER_ROWS : BIG + TOWER_ROWS + LINE_ROWS, :] = two_parts(whole(a[lines]) + whole(b[lines]))


def add_quads_kernel(place_ref, *refs):
    parts, outs = refs[:QUADS], refs[QUADS:]
    quad, field = place_ref[0] >> 1, place_ref[1]

    def four(at):
        return [ref[at, :].astype(f32) for ref in parts]

    def total(at):
        a, b, c, d = four(at)
        return ((a + b) + (c + d)).astype(bf16)

    second = total(pl.ds(FIELDS * EXP_H1, EXP_H1))
    tower = total(pl.ds(BIG, TOWER_ROWS))
    a, b, c, d = [whole(v) for v in four(pl.ds(BIG + TOWER_ROWS, LINE_ROWS))]
    lines = two_parts((a + b) + (c + d))
    gate = total(pl.ds(PIECE - GATE_ROWS, GATE_ROWS))
    for s, out in enumerate(outs):
        out[:EXP_H1, :] = total(pl.ds(s * EXP_H1, EXP_H1))
        out[EXP_H1 : 2 * EXP_H1, :] = second
        at = 2 * EXP_H1
        out[at : at + TOWER_ROWS, :] = tower
        at += TOWER_ROWS
        out[at : at + LINE_ROWS, :] = lines
        out[at + LINE_ROWS :, :] = jnp.where(quad == s, gate, jnp.zeros_like(gate))


def add_fields_kernel(place_ref, *refs):
    parts, out = refs[:FIELDS], refs[FIELDS]
    odd = place_ref[1] % 2 == 1
    a, b, c, d = [ref[...].astype(f32) for ref in parts]

    def total(a, b, c, d):
        return (a + jnp.where(odd, d, b)) + (c + jnp.where(odd, b, d))

    out[...] = total(a, b, c, d).astype(bf16)
    lines = slice(2 * EXP_H1 + TOWER_ROWS, 2 * EXP_H1 + TOWER_ROWS + LINE_ROWS)
    out[lines, :] = two_parts(total(*[whole(v[lines]) for v in (a, b, c, d)]))


def join_done_kernel(place_ref, *refs):
    parts, (stack_ref, tower_ref, lines_ref, gate_ref) = refs[:QUADS], refs[QUADS:]
    quad = place_ref[0] >> 1
    for q, ref in enumerate(parts):
        stack_ref[q] = ref[: 2 * EXP_H1, :]
        at = 2 * EXP_H1
        tower_ref[aligned(quad ^ q, TOWER_ROWS), :] = ref[at : at + TOWER_ROWS, :].astype(f32)
        at += TOWER_ROWS
        lines_ref[aligned(quad ^ q, 8), :] = whole(ref[at : at + LINE_ROWS, :].astype(f32))
    a, b, c, d = [ref[2 * EXP_H1 + TOWER_ROWS + LINE_ROWS :, :].astype(f32) for ref in parts]
    gate_ref[...] = (a + b) + (c + d)


def assemble_kernel(start, place_ref, *refs):
    parts, (out_ref, wide_ref, sems) = refs[:FIELDS], refs[-3:]
    rows, size = out_ref.shape[0] // FIELDS, wide_ref.shape[1]
    copies = []
    for s, part in enumerate(parts):
        at = pl.ds(lax.rem(place_ref[1] + s, FIELDS) * rows + start, size)
        if s:
            wide_ref[s - 1] = part[...].astype(f32)
        source = wide_ref.at[s - 1] if s else part
        copies.append(pltpu.make_async_copy(source, out_ref.at[at, :], sems.at[s]))
        copies[-1].start()
    for copy in copies:
        copy.wait()


def update_kernel(core, place_ref, grads_ref, *refs):
    first_w, first_m, first_v, second_w, second_m, second_v, second_a = refs[:7]
    outs = refs[-8:]
    outs[7][...] = jnp.zeros((8, LANES), f32)
    expert = place_ref[0] ^ (2 * pl.program_id(0) + core)
    at = aligned(expert, EXP_H1)
    grads = grads_ref[pl.program_id(0)].astype(f32)
    new = adamw(first_w[:, at], first_m[:, at], first_v[:, at], grads[:EXP_H1].T)
    outs[0][...], outs[1][...], outs[2][...] = new
    new = adamw(second_w[at, :], second_m[at, :], second_v[at, :], grads[EXP_H1:])
    outs[3][...], outs[4][...], outs[5][...] = new
    outs[6][...] = blend(second_a[at, :], new[0])


def on_device(
    inputs,
    labels,
    user_ids,
    first_weight,
    first_mean,
    first_square,
    gate_weight,
    gate_mean,
    gate_square,
    second_weight,
    second_mean,
    second_square,
    tower_weight,
    tower_mean,
    tower_square,
    head_weight,
    head_mean,
    head_square,
    biases,
    bias_mean,
    bias_square,
    second_average,
    tower_average,
    head_average,
):
    nfield, nbatch = lax.axis_size("field"), lax.axis_size("batch")
    field, batch = lax.axis_index("field"), lax.axis_index("batch")
    rows_dev, columns = inputs.shape
    rows = rows_dev // nfield
    width = nfield * columns
    users_total = rows_dev * nbatch // USER_ROWS
    place = jnp.stack([batch % GROUP, field]).astype(jnp.int32)

    def shift(value, by):
        return lax.ppermute(value, "field", [(i, (i + by) % nfield) for i in range(nfield)])

    def cross(value, mask):
        return lax.ppermute(value, "batch", [(i, i ^ mask) for i in range(nbatch)])

    def from_fields(value):
        return [value] + [shift(value, s) for s in range(1, nfield)]

    def from_quads(value):
        return [value] + [cross(value, 2 * q) for q in range(1, QUADS)]

    starts = [0]
    for part in CHUNKS:
        starts.append(starts[-1] + part * rows // 16)
    nchunks = len(CHUNKS)

    ids = user_ids.reshape(1, rows)
    labels_t = labels.T
    expert_block = pl.BlockSpec((columns, EXP_H1), lambda i, place_ref: (0, place_ref[0]))
    high = users_total // LANES
    lines = 2 * rows // LANES
    sent = pl.pallas_call(
        piece_kernel,
        grid_spec=pltpu.PrefetchScalarGridSpec(
            num_scalar_prefetch=1, grid=(1,), in_specs=[expert_block, vmem, vmem], out_specs=vmem
        ),
        out_shape=shaped((EXP_H1 + GATES + lines, columns), bf16),
        compiler_params=params(),
        cost_estimate=cost(1e6, 1e5),
        name="first_piece",
    )(place, first_weight, gate_weight.T, user_ids.reshape(rows // LANES, LANES))
    def own_rows(low, high, deps):
        count = (high - low) * nfield
        return pl.pallas_call(
            functools.partial(rows_kernel, starts[low:high]),
            out_shape=[shaped((starts[c + 1] - starts[c], columns), bf16) for c in range(low, high) for _ in range(nfield)],
            in_specs=[smem, anywhere] + [anywhere] * len(deps),
            out_specs=[hbm] * count,
            scratch_shapes=[pltpu.SemaphoreType.DMA((count,))],
            compiler_params=params(),
            cost_estimate=cost(1e3, 1e3),
            name="own_rows",
        )(place, inputs, *deps)

    def exchange_rows(mine, *others):
        return [mine] + [shift(o, s + 1) for s, o in enumerate(others)]

    def exchange_rows_after(deps, rows_of):
        mine, *others = rows_of
        return exchange_rows(mine, *once_there("rows_to_send", others, deps))

    chunk_rows = own_rows(0, nchunks, [])
    chunk_rows = [chunk_rows[c * nfield : (c + 1) * nfield] for c in range(nchunks)]
    prepared = call(
        prepare_kernel,
        "prepare_weights",
        [shaped((LOW_ROWS, LANES), bf16), shaped((WIDE_ROWS, LANES), f32), shaped((1 + TASKS, rows), jnp.int32)],
        [vmem] * 6,
        [
            second_weight,
            tower_weight,
            head_weight.reshape(1, LANES),
            jnp.pad(biases, (0, LANES - TASKS)).reshape(1, -1),
            ids,
            labels_t,
        ],
    )
    bundle, gate_t = call(
        join_fields_kernel,
        "join_fields",
        [shaped((EXP_H1 + lines, width), bf16), shaped((GATES, width), bf16)],
        [vmem] * FIELDS,
        from_fields(sent),
        deps=[chunk_rows[0][0], prepared[0]],
    )
    arrived = [exchange_rows_after([gate_t], chunk_rows[0])]
    own, digits, joined, gate_t = call(
        join_quads_kernel,
        "join_quads",
        [
            shaped((QUADS, EXP_H1, width), bf16),
            shaped((QUADS, lines, width), bf16),
            shaped((starts[1], width), bf16),
            shaped((GATES, width), bf16),
        ],
        [vmem] * (QUADS + FIELDS + 1),
        [*from_quads(bundle), *arrived[0], gate_t],
    )
    arrived[0] = [joined]
    arrived.append(exchange_rows_after([digits], chunk_rows[1]))
    counts = call(count_kernel, "user_counts", shaped((LANES, high), f32), [vmem], [digits])
    hop = GROUP
    while hop < nbatch:
        counts = counts + cross(counts, hop)
        hop *= 2
    counts_other = cross(counts, 1)
    other = cross(own, 1)
    turned_own, gate_all = call(
        turn_kernel,
        "turn_first",
        [shaped((width, H1 // 2), bf16), shaped((width, GATES), bf16)],
        [vmem] * 2,
        [own, gate_t],
    )
    turned_other = cross(turned_own, 1)

    sum_shapes = [
        shaped((H1 + GATES, width), f32),
        shaped((H2, EXP_H1), f32),
        shaped((TASKS * EXP_H2, TASKS * TOWER), f32),
        shaped((H1 + H2, LANES), f32),
        shaped((3, LANES, LANES), f32),
    ]

    def run_layers(c, sums, deps):
        last = c == nchunks - 1
        low, chunk = starts[c], starts[c + 1] - starts[c]
        low_weights, wide_biases, marks = prepared
        operands = [*arrived[c], marks, own, other, gate_t, counts, counts_other, low_weights, wide_biases]
        out_shape = [shaped((H1 + GATES, chunk), bf16), shaped((TASKS, chunk), f32)] + sum_shapes
        if last:
            out_shape += [shaped((QUADS * PIECE, LANES), bf16)] * 2

        def once(shape):
            return pl.BlockSpec(shape, lambda i: (0,) * len(shape), pipeline_mode=pl.Buffered(1))

        return pl.pallas_call(
            functools.partial(layers_kernel, last, bool(sums), len(deps), loss_scale * users_total, low, len(arrived[c])),
            grid=(1,),
            out_shape=out_shape,
            in_specs=[smem]
            + [once(o.shape) for o in operands]
            + [vmem] * len(sums)
            + [hbm] * len(deps),
            out_specs=[once(o.shape) for o in out_shape[:2]]
            + [vmem] * NSUM
            + [once(o.shape) for o in out_shape[2 + NSUM :]],
            input_output_aliases={1 + len(operands) + i: 2 + i for i in range(len(sums))},
            scratch_shapes=[
                pltpu.VMEM((H1, chunk), bf16),
                pltpu.VMEM((H1, chunk), f32),
                pltpu.VMEM((H2, chunk), f32),
                pltpu.VMEM((H2, chunk), f32),
                pltpu.VMEM((GATES, chunk), f32),
                pltpu.VMEM((GATES, chunk), f32),
            ],
            compiler_params=params(LAYERS_MIB),
            cost_estimate=cost(LAYERS_COST * chunk, 1e3),
            name="layers",
        )(place, *operands, *sums, *deps)


    bounds = [0]
    for part in RETURNS:
        bounds.append(bounds[-1] + part * rows // 16)

    def give_back(i, deps):
        spans, taken = [], []
        for c in range(nchunks):
            low, high = max(bounds[i], starts[c]), min(bounds[i + 1], starts[c + 1])
            if low < high:
                spans.append((low - starts[c], high - starts[c]))
                taken.append(d_chunks[c])
        size = bounds[i + 1] - bounds[i]
        mine, *others = call(
            functools.partial(back_kernel, spans),
            "input_gradients",
            [shaped((size, columns), f32)] + [shaped((size, columns), bf16)] * (nfield - 1),
            [vmem] * (len(taken) + 3),
            [*taken, turned_own, turned_other, gate_all],
            flops=BACK_COST * size,
            deps=deps,
            mib=12,
        )
        return [mine] + [shift(o, -(s + 1)) for s, o in enumerate(others)]

    sums, probs, d_chunks, returned = [], [], [], []
    for c in range(nchunks):
        if c == nchunks - 1:
            returned.append(give_back(0, [probs[-1]]))
        d_chunk, prob, *sums = run_layers(c, sums, [r[0] for r in returned])
        probs.append(prob)
        d_chunks.append(d_chunk)
        if c + 2 < nchunks:
            arrived.append(exchange_rows_after([prob], chunk_rows[c + 2]))
    keep, send = sums[NSUM:]
    returned.append(give_back(1, [keep]))
    (send,) = once_there("gradients_to_send", [send], returned[0][1:])

    pieces = call(
        add_cores_kernel,
        "add_cores",
        [shaped((PIECE, LANES), bf16)] * QUADS,
        [smem, vmem, vmem],
        [place, keep, cross(send, 1)],
        deps=returned[1][:1],
    )
    parts = [pieces[0]] + [cross(pieces[q], 2 * q) for q in range(1, QUADS)]
    hop = GROUP
    while hop < nbatch:
        parts = [(p.astype(f32) + cross(p, hop).astype(f32)).astype(bf16) for p in parts]
        hop *= 2
    blocks = call(
        add_quads_kernel,
        "add_quads",
        [shaped((2 * EXP_H1 + SMALL, LANES), bf16)] * nfield,
        [smem] + [vmem] * QUADS,
        [place] + parts,
        deps=returned[1][1:],
    )
    returned.append(give_back(2, [blocks[0]]))
    def assemble(i, before, deps):
        return pl.pallas_call(
            functools.partial(assemble_kernel, bounds[i]),
            out_shape=[shaped((rows_dev, columns), f32)],
            in_specs=[smem, anywhere] + [vmem] * (nfield - 1) + [hbm] * (len(before) + len(deps)),
            out_specs=[hbm],
            input_output_aliases={1 + nfield: 0} if before else {},
            scratch_shapes=[
                pltpu.VMEM((nfield - 1, bounds[i + 1] - bounds[i], columns), f32),
                pltpu.SemaphoreType.DMA((nfield,)),
            ],
            compiler_params=params(),
            cost_estimate=cost(1e3, 1e3),
            name="assemble_input_grad",
        )(place, *returned[i], *before, *deps)

    input_grad = assemble(0, [], [blocks[0]])
    input_grad = assemble(1, input_grad, [blocks[0]])
    done = call(
        add_fields_kernel,
        "add_fields",
        shaped((2 * EXP_H1 + SMALL, LANES), bf16),
        [smem] + [vmem] * nfield,
        [place, blocks[0]] + [shift(blocks[s], -s) for s in range(1, nfield)],
        deps=[returned[2][0], *input_grad],
    )
    done_own, g_tower, lines, g_gate = call(
        join_done_kernel,
        "join_gradients",
        [
            shaped((QUADS, 2 * EXP_H1, LANES), bf16),
            shaped((LANES, LANES), f32),
            shaped((8 * QUADS, LANES), f32),
            shaped((GATES, columns), f32),
        ],
        [smem] + [vmem] * QUADS,
        [place] + from_quads(done),
    )
    done_other = cross(done_own, 1)

    def run_update(core, grads, before):
        first_spec = pl.BlockSpec((columns, EXP_H1), lambda q, place_ref: (0, place_ref[0] ^ (2 * q + core)))
        second_spec = pl.BlockSpec((EXP_H1, EXP_H2), lambda q, place_ref: (place_ref[0] ^ (2 * q + core), 0))
        operands = [
            grads,
            first_weight,
            first_mean,
            first_square,
            second_weight,
            second_mean,
            second_square,
            second_average,
        ]
        specs = [first_spec] * 3 + [second_spec] * 4
        before = list(before or [])[:7]
        return pl.pallas_call(
            functools.partial(update_kernel, core),
            grid_spec=pltpu.PrefetchScalarGridSpec(
                num_scalar_prefetch=1,
                grid=(QUADS,),
                in_specs=[vmem] * len(operands) + [anywhere] * len(before),
                out_specs=specs + [pl.BlockSpec((8, LANES), lambda q, place_ref: (0, 0))],
            ),
            out_shape=[shaped((columns, H1), f32)] * 3
            + [shaped((H1, EXP_H2), f32)] * 4
            + [shaped((8, LANES), f32)],
            input_output_aliases={1 + len(operands) + i: i for i in range(len(before))},
            compiler_params=params(),
            cost_estimate=cost(1e6, 8e6),
            name="update_layers",
        )(place, *operands, *before)

    updated_half = run_update(0, done_own, None)
    updated = run_update(1, done_other, updated_half)
    new_first, new_second, avg_second = updated[:3], updated[3:6], updated[6]

    at = (H1 + H2) // LANES
    g_head = lines[at + 1]
    g_bias = jnp.concatenate([lines[: at + 1].reshape(-1), lines[at + 2, :TASKS]])
    new_gate = adamw(gate_weight, gate_mean, gate_square, g_gate.T)
    new_tower = adamw(tower_weight, tower_mean, tower_square, g_tower)
    avg_tower = blend(tower_average, new_tower[0])
    new_head = adamw(head_weight, head_mean, head_square, g_head)
    avg_head = blend(head_average, new_head[0])
    new_bias = adamw(biases, bias_mean, bias_square, g_bias)

    (input_grad,) = assemble(2, input_grad, [updated[7]])
    predicted = jnp.concatenate(probs, axis=1).T
    return (
        predicted,
        input_grad,
        *new_first,
        *new_gate,
        *new_second,
        *new_tower,
        *new_head,
        *new_bias,
        avg_second,
        avg_tower,
        avg_head,
    )


def solution(mesh):
    fields, copied = P("field", None), P()
    rows = P(("batch", "field"), None)
    in_specs = (
        (P("batch", "field"), rows, P(("batch", "field"))) + (fields,) * 6 + (copied,) * 15
    )
    out_specs = (rows, P("batch", "field")) + (fields,) * 6 + (copied,) * 15
    return jax.shard_map(
        on_device, mesh=mesh, in_specs=in_specs, out_specs=out_specs, check_vma=False
    )
```

```python
import functools

import jax
import jax.numpy as jnp
from jax import lax
from jax.experimental import pallas as pl
from jax.experimental.pallas import tpu as pltpu
from jax.sharding import PartitionSpec as P

EXPERTS = 8
EXP_H1 = 256
EXP_H2 = 128
TASKS = 2
TOWER = 64
USER_ROWS = 4
STEP = 10
H1 = 2048
H2 = 1024
GATES = TASKS * EXPERTS
LANES = 128
GROUP = 8
QUADS = GROUP // 2
CHUNKS = (8, 12, 12)
RETURNS = (10, 11, 11)
MIB = 1024 * 1024
LAYERS_MIB = 32
FIELDS = 4
BIG = (FIELDS + 1) * EXP_H1
TOWER_ROWS, LINE_ROWS, GATE_ROWS = 32, 16, 16
SMALL = TOWER_ROWS + LINE_ROWS + GATE_ROWS
PIECE = BIG + SMALL

beta_one = 0.9
beta_two = 0.999
learn_rate = 0.1
decay_rate = 0.01
adam_eps = 1e-08
average_rate = 0.8
loss_scale = 512.0

LAYERS_COST = 1e7
BACK_COST = 1e3

f32 = jnp.float32
bf16 = jnp.bfloat16
smem = pl.BlockSpec(memory_space=pltpu.SMEM)
vmem = pl.BlockSpec(memory_space=pltpu.VMEM)
anywhere = pl.BlockSpec(memory_space=pl.ANY)
hbm = pl.BlockSpec(memory_space=pltpu.HBM)


def sigmoid(values):
    return 0.5 * jnp.tanh(0.5 * values) + 0.5


def dot(left, right):
    return jnp.dot(left, right, preferred_element_type=f32)


def dot_nt(left, right, precision=None):
    return lax.dot_general(
        left, right, (((1,), (1,)), ((), ())), precision=precision, preferred_element_type=f32
    )


def adamw(weight, moment, square, gradient):
    new_moment = beta_one * moment + (1.0 - beta_one) * gradient
    new_square = beta_two * square + (1.0 - beta_two) * gradient * gradient
    moment_hat = new_moment / (1.0 - beta_one**STEP)
    square_hat = new_square / (1.0 - beta_two**STEP)
    new_weight = weight - learn_rate * (
        moment_hat / (jnp.sqrt(square_hat) + adam_eps) + decay_rate * weight
    )
    return (new_weight, new_moment, new_square)


def blend(average, weight):
    return average_rate * average + (1.0 - average_rate) * weight


def params(mib=8):
    return pltpu.CompilerParams(vmem_limit_bytes=mib * MIB)


def cost(flops, nbytes):
    return pl.CostEstimate(flops=int(flops), bytes_accessed=int(nbytes), transcendentals=0)


def shaped(shape, dtype):
    return jax.ShapeDtypeStruct(shape, dtype)


def aligned(index, size):
    return pl.ds(pl.multiple_of(index * size, size), size)


def call(kernel, name, out_shape, in_specs, operands, flops=1e6, nbytes=1e6, deps=(), mib=8):
    def body(*refs):
        given = len(operands)
        kernel(*refs[:given], *refs[given + len(deps) :])

    return pl.pallas_call(
        body,
        out_shape=out_shape,
        in_specs=list(in_specs) + [hbm] * len(deps),
        out_specs=jax.tree.map(lambda _: vmem, out_shape),
        compiler_params=params(mib),
        cost_estimate=cost(flops, nbytes),
        name=name,
    )(*operands, *deps)


def once_there(name, values, deps):
    return pl.pallas_call(
        lambda *refs: None,
        out_shape=[shaped(v.shape, v.dtype) for v in values],
        in_specs=[hbm] * (len(values) + len(deps)),
        out_specs=[hbm] * len(values),
        input_output_aliases={i: i for i in range(len(values))},
        compiler_params=params(),
        cost_estimate=cost(1, 1),
        name=name,
    )(*values, *deps)


def piece_kernel(place_ref, first_ref, gate_ref, ids_ref, send_ref):
    send_ref[:EXP_H1, :] = (0.5 * first_ref[...]).T.astype(bf16)
    at = EXP_H1 + GATES
    send_ref[EXP_H1:at, :] = gate_ref[...].astype(bf16)
    ids, lines = ids_ref[...], ids_ref.shape[0]
    send_ref[at : at + lines, :] = (ids % 256).astype(f32).astype(bf16)
    send_ref[at + lines :, :] = (ids // 256).astype(f32).astype(bf16)


def count_kernel(digits_ref, counts_ref):
    lines = digits_ref.shape[1] // 2
    width = digits_ref.shape[2]
    high = lax.broadcasted_iota(jnp.int32, (counts_ref.shape[1], width), 0).astype(f32)
    low = lax.broadcasted_iota(jnp.int32, (LANES, width), 0).astype(f32)
    total = jnp.zeros(counts_ref.shape, f32)
    for q in range(QUADS):
        digits = digits_ref[q].astype(f32)
        ids = digits[:lines] + 256.0 * digits[lines:]
        ids_high = jnp.floor(ids * (1.0 / LANES))
        ids_low = ids - LANES * ids_high
        for r in range(lines):
            one_high = jnp.where(high == ids_high[r : r + 1], 1.0, 0.0).astype(bf16)
            one_low = jnp.where(low == ids_low[r : r + 1], 1.0, 0.0).astype(bf16)
            total = total + dot_nt(one_low, one_high)
    counts_ref[...] = total


LOW_TURNED = H1
LOW_TOWERS = 2 * H1
LOW_ROWS = LOW_TOWERS + 2 * TASKS * EXP_H2
WIDE_TWO = H1
WIDE_TOP = H1 + H2
WIDE_ROWS = WIDE_TOP + 3 * LANES


def prepare_kernel(second_ref, tower_ref, head_ref, bias_ref, ids_ref, labels_ref, low_ref, wide_ref, marks_ref):
    low_ref[:H1, :] = (0.5 * second_ref[...]).astype(bf16)
    for block in range(H1 // LANES):
        turned = (0.5 * second_ref[pl.ds(block * LANES, LANES), :]).T
        low_ref[pl.ds(LOW_TURNED + block * LANES, LANES), :] = turned.astype(bf16)
    tower = tower_ref[...]
    none = jnp.zeros((EXP_H2, TOWER), f32)
    left = jnp.concatenate([tower[:, :TOWER], none], axis=1)
    right = jnp.concatenate([none, tower[:, TOWER:]], axis=1)
    for i, block in enumerate((left, right, left.T, right.T)):
        low_ref[pl.ds(LOW_TOWERS + i * LANES, LANES), :] = block.astype(bf16)

    def column(row):
        return jnp.broadcast_to(row, (LANES, LANES)).T

    for r in range((H1 + H2) // LANES):
        wide_ref[pl.ds(r * LANES, LANES), :] = 0.5 * column(bias_ref[:, r * LANES : (r + 1) * LANES])
    at = H1 + H2
    wide_ref[pl.ds(WIDE_TOP, LANES), :] = column(bias_ref[:, at : at + LANES])
    wide_ref[pl.ds(WIDE_TOP + LANES, LANES), :] = column(head_ref[...])
    wide_ref[pl.ds(WIDE_TOP + 2 * LANES, LANES), :] = column(bias_ref[:, at + LANES : at + 2 * LANES])
    marks_ref[:1, :] = ids_ref[...]
    marks_ref[1:, :] = labels_ref[...]


def join_fields_kernel(*refs):
    sent, (bundle_ref, gate_ref) = refs[:FIELDS], refs[FIELDS:]
    width = sent[0].shape[1]
    for s, ref in enumerate(sent):
        at = slice(s * width, (s + 1) * width)
        bundle_ref[:EXP_H1, at] = ref[:EXP_H1, :]
        gate_ref[:, at] = ref[EXP_H1 : EXP_H1 + GATES, :]
        bundle_ref[EXP_H1:, at] = ref[EXP_H1 + GATES :, :]


def join_quads_kernel(*refs):
    bundles, refs = refs[:QUADS], refs[QUADS:]
    rows, gate_ref, (stack_ref, digits_ref, joined_ref, gate_out) = refs[:FIELDS], refs[FIELDS], refs[FIELDS + 1 :]
    for q, ref in enumerate(bundles):
        stack_ref[q] = ref[:EXP_H1, :]
        digits_ref[q] = ref[EXP_H1:, :]
    width = rows[0].shape[1]
    for s, ref in enumerate(rows):
        joined_ref[:, s * width : (s + 1) * width] = ref[...]
    gate_out[...] = gate_ref[...]


def rows_kernel(starts, place_ref, inputs_ref, *refs):
    outs, sems = refs[-1 - len(starts) * FIELDS : -1], refs[-1]
    rows = inputs_ref.shape[0] // FIELDS
    copies = []
    for i, out in enumerate(outs):
        chunk, s = divmod(i, FIELDS)
        at = pl.ds(lax.rem(place_ref[1] + s, FIELDS) * rows + starts[chunk], out.shape[0])
        copies.append(pltpu.make_async_copy(inputs_ref.at[at, :], out, sems.at[i]))
        copies[-1].start()
    for copy in copies:
        copy.wait()


def turn_kernel(stack_ref, gate_ref, out_ref, gate_out):
    gate_out[...] = gate_ref[...].T
    for q in range(QUADS):
        out_ref[:, q * EXP_H1 : (q + 1) * EXP_H1] = stack_ref[q].T


NSUM = 5


def layers_kernel(last, with_sums, ndeps, scale, low_row, nrows, place_ref, *refs):
    xs, refs = refs[:nrows], refs[nrows:]
    marks_ref, own_ref, other_ref, gate_ref, counts_a, counts_b, low_ref, wide_ref = refs[:8]
    refs = refs[8:]
    given = [None] * NSUM
    if with_sums:
        given, refs = refs[:NSUM], refs[NSUM:]
    refs = refs[ndeps:]
    d_ref, prob_ref, refs = refs[0], refs[1], refs[2:]
    sums, refs = refs[:NSUM], refs[NSUM:]
    if last:
        keep_ref, send_ref, refs = refs[0], refs[1], refs[2:]
    sum_first, sum_second, sum_tower, sum_bias, sum_top = sums
    hidden_ref, slope_ref, two_ref, slope_two_ref, gates_ref, d_gates_ref = refs
    rows = prob_ref.shape[1]
    mine = slice(low_row, low_row + rows)
    place = place_ref[0]

    def add(which, at, value):
        sums[which][at] = value if given[which] is None else given[which][at] + value

    def fold(values):
        out = values[:, :LANES]
        for at in range(LANES, values.shape[1], LANES):
            out = out + values[:, at : at + LANES]
        return out

    def wide(values):
        return jnp.concatenate([values] * (rows // LANES), axis=1)

    def silu_of_twice(half):
        swing = jnp.tanh(half)
        above = 1.0 + swing
        value = half * above
        return value, above + value * (1.0 - swing)

    ids = marks_ref[:1, mine]
    counts = counts_a[...] + counts_b[...]
    present = jnp.sum(jnp.where(counts > 0.0, 1.0, 0.0), keepdims=True)
    high = lax.broadcasted_iota(jnp.int32, (counts.shape[1], rows), 0)
    low = lax.broadcasted_iota(jnp.int32, (LANES, rows), 0)
    one_high = jnp.where(high == ids // LANES, 1.0, 0.0).astype(bf16)
    top_digit = jnp.floor(counts * (1.0 / 65536.0))
    counts = counts - 65536.0 * top_digit
    mid_digit = jnp.floor(counts * (1.0 / 256.0))
    low_digit = counts - 256.0 * mid_digit
    found = dot(low_digit.astype(bf16), one_high)
    found = found + 256.0 * dot(mid_digit.astype(bf16), one_high)
    found = found + 65536.0 * dot(top_digit.astype(bf16), one_high)
    found = jnp.sum(jnp.where(low == ids % LANES, found, 0.0), axis=0, keepdims=True)
    row_weight = scale / (present * found)

    inputs = jnp.concatenate([x[...] for x in xs], axis=1) if nrows > 1 else xs[0][...]
    turned_in = inputs.T
    logits = dot(gate_ref[...], turned_in).reshape(TASKS, EXPERTS, rows)
    shifted = jnp.exp(logits - jnp.max(logits, axis=1, keepdims=True))
    gates = shifted / jnp.sum(shifted, axis=1, keepdims=True)
    gates_ref[...] = gates.reshape(GATES, rows)
    slots = [(c, q) for c in range(2) for q in range(QUADS)]
    mixed = [jnp.zeros((EXP_H2, rows), f32) for _ in range(TASKS)]
    for t, (c, q) in enumerate(slots):
        e = place ^ (2 * q + c)
        one, two = pl.ds(t * EXP_H1, EXP_H1), pl.ds(t * EXP_H2, EXP_H2)
        weight = (other_ref if c else own_ref)[q]
        half_one = dot(weight, turned_in) + wide(wide_ref[aligned(e, EXP_H1), :])
        hidden, slope_ref[one, :] = silu_of_twice(half_one)
        hidden_low = hidden.astype(bf16)
        hidden_ref[one, :] = hidden_low
        at = pl.multiple_of(LOW_TURNED + e * EXP_H1, EXP_H1)
        turned = jnp.concatenate([low_ref[pl.ds(at, LANES), :], low_ref[pl.ds(at + LANES, LANES), :]], axis=1)
        at = pl.multiple_of(WIDE_TWO + e * EXP_H2, EXP_H2)
        half_two = dot(turned, hidden_low) + wide(wide_ref[pl.ds(at, EXP_H2), :])
        hidden, slope_two_ref[two, :] = silu_of_twice(half_two)
        two_ref[two, :] = hidden
        for k in range(TASKS):
            mixed[k] = mixed[k] + gates_ref[pl.ds(k * EXPERTS + e, 1), :] * hidden
    mixed_low = jnp.concatenate(mixed, axis=0).astype(bf16)
    at = LOW_TOWERS + TASKS * EXP_H2
    tower_fwd = jnp.concatenate([low_ref[at : at + LANES, :], low_ref[at + LANES :, :]], axis=1)
    tops = [wide_ref[WIDE_TOP + k * LANES : WIDE_TOP + (k + 1) * LANES, :] for k in range(3)]
    pre_tower = dot(tower_fwd, mixed_low) + wide(tops[0])
    logistic = sigmoid(pre_tower)
    upper = pre_tower * logistic
    slope_tower = logistic + upper * (1.0 - logistic)
    head = wide(tops[1])
    logit = jnp.sum((upper * head).reshape(TASKS, TOWER, rows), axis=1)
    logit = logit + wide(tops[2][:TASKS, :])
    prob = 1.0 / (1.0 + jnp.exp(-logit))
    prob_ref[...] = prob
    d_logit = row_weight * (prob - marks_ref[1:, mine].astype(f32))
    d_wide = jnp.broadcast_to(d_logit[:, None, :], (TASKS, TOWER, rows)).reshape(LANES, rows)
    d_tower = (d_wide * head * slope_tower).astype(bf16)
    add(4, 0, fold(d_tower.astype(f32)))
    add(4, 1, fold(d_wide * upper))
    low_rows = jnp.zeros((LANES - TASKS, LANES), f32)
    add(4, 2, jnp.concatenate([fold(d_logit), low_rows], axis=0))
    add(2, ..., dot_nt(mixed_low, d_tower))
    d_mixed = dot(low_ref[LOW_TOWERS : LOW_TOWERS + TASKS * EXP_H2, :], d_tower)
    parts = [d_mixed[k * EXP_H2 : (k + 1) * EXP_H2, :] for k in range(TASKS)]
    for t, (c, q) in enumerate(slots):
        e = place ^ (2 * q + c)
        one, two = pl.ds(t * EXP_H1, EXP_H1), pl.ds(t * EXP_H2, EXP_H2)
        hidden = two_ref[two, :]
        d_hidden = jnp.zeros((EXP_H2, rows), f32)
        for k in range(TASKS):
            at = pl.ds(k * EXPERTS + e, 1)
            d_gates_ref[at, :] = jnp.sum(parts[k] * hidden, axis=0, keepdims=True)
            d_hidden = d_hidden + gates_ref[at, :] * parts[k]
        d_two = d_hidden * slope_two_ref[two, :]
        at = pl.ds(pl.multiple_of(H1 + e * EXP_H2, EXP_H2), EXP_H2)
        add(3, (at, slice(None)), fold(d_two))
        d_two = d_two.astype(bf16)
        add(1, (two, slice(None)), dot_nt(d_two, hidden_ref[one, :]))
        d_one = dot(low_ref[aligned(e, EXP_H1), :], d_two) * slope_ref[one, :]
        add(3, (aligned(e, EXP_H1), slice(None)), fold(d_one))
        d_ref[one, :] = d_one.astype(bf16)
    d_gates = d_gates_ref[...].reshape(TASKS, EXPERTS, rows)
    centered = d_gates - jnp.sum(gates * d_gates, axis=1, keepdims=True)
    d_ref[pl.ds(H1, GATES), :] = (gates * centered).reshape(GATES, rows).astype(bf16)
    add(0, ..., dot(d_ref[...], inputs))

    if last:
        for t, (c, q) in enumerate(slots):
            one, two = pl.ds(t * EXP_H1, EXP_H1), pl.ds(t * EXP_H2, EXP_H2)
            out = send_ref if c else keep_ref
            for s in range(FIELDS):
                at = pl.ds(q * BIG + s * EXP_H1, EXP_H1)
                out[at, :] = (0.5 * sum_first[one, s * LANES : (s + 1) * LANES]).astype(bf16)
            out[pl.ds(q * BIG + FIELDS * EXP_H1, EXP_H1), :] = (0.5 * sum_second[two, :]).T.astype(bf16)
        ones = jnp.ones((8, LANES), f32)
        bias = dot_nt(0.5 * ones, sum_bias[...], lax.Precision.HIGHEST)[:1, :]
        lines = [bias[:, r * LANES : (r + 1) * LANES] for r in range((H1 + H2) // LANES)]
        lines += [dot_nt(ones, sum_top[k], lax.Precision.HIGHEST)[:1, :] for k in range(3)]
        lines += [jnp.zeros((1, LANES), f32)] * (8 * QUADS - len(lines))
        for out in (keep_ref, send_ref):
            at = QUADS * BIG
            for q in range(QUADS):
                block = sum_tower[pl.ds(q * TOWER_ROWS, TOWER_ROWS), :TOWER]
                below = sum_tower[pl.ds(EXP_H2 + q * TOWER_ROWS, TOWER_ROWS), TOWER:]
                out[pl.ds(at, TOWER_ROWS), :] = jnp.concatenate([block, below], axis=1).astype(bf16)
                at += TOWER_ROWS
                out[pl.ds(at, LINE_ROWS), :] = two_parts(jnp.concatenate(lines[8 * q : 8 * q + 8], axis=0))
                at += LINE_ROWS
                block = sum_first[pl.ds(H1, GATES), q * LANES : (q + 1) * LANES]
                out[pl.ds(at, GATE_ROWS), :] = block.astype(bf16)
                at += GATE_ROWS


def back_kernel(spans, *refs):
    d_refs, refs = refs[: len(spans)], refs[len(spans) :]
    own_ref, other_ref, gate_ref, out_own = refs[:4]
    half, at = H1 // 2, 0
    for (low, high), d_ref in zip(spans, d_refs):
        here = slice(low, high)
        turned = dot(own_ref[...], d_ref[:half, here]) + dot(other_ref[...], d_ref[half:H1, here])
        turned = turned + dot(gate_ref[...], d_ref[H1:, here])
        grads = turned.T
        width, rows = out_own.shape[1], pl.ds(at, high - low)
        out_own[rows, :] = grads[:, :width]
        for s, ref in enumerate(refs[-FIELDS + 1 :]):
            ref[rows, :] = grads[:, (s + 1) * width : (s + 2) * width].astype(bf16)
        at += high - low


def two_parts(lines):
    low = lines.astype(bf16)
    return jnp.concatenate([low.astype(f32), lines - low.astype(f32)], axis=0).astype(bf16)


def whole(parts):
    half = parts.shape[0] // 2
    return parts[:half] + parts[half:]


def add_cores_kernel(place_ref, keep_ref, got_ref, *outs):
    quad = place_ref[0] >> 1

    def both(at):
        return keep_ref[at, :].astype(f32), got_ref[at, :].astype(f32)

    for q, out in enumerate(outs):
        a, b = both(pl.ds(q * BIG, BIG))
        out[:BIG, :] = (a + b).astype(bf16)
        a, b = both(pl.ds(pl.multiple_of(QUADS * BIG + (quad ^ q) * SMALL, SMALL), SMALL))
        out[BIG:, :] = (a + b).astype(bf16)
        lines = slice(TOWER_ROWS, TOWER_ROWS + LINE_ROWS)
        out[BIG + TOWER_ROWS : BIG + TOWER_ROWS + LINE_ROWS, :] = two_parts(whole(a[lines]) + whole(b[lines]))


def add_quads_kernel(place_ref, *refs):
    parts, outs = refs[:QUADS], refs[QUADS:]
    quad, field = place_ref[0] >> 1, place_ref[1]

    def four(at):
        return [ref[at, :].astype(f32) for ref in parts]

    def total(at):
        a, b, c, d = four(at)
        return ((a + b) + (c + d)).astype(bf16)

    second = total(pl.ds(FIELDS * EXP_H1, EXP_H1))
    tower = total(pl.ds(BIG, TOWER_ROWS))
    a, b, c, d = [whole(v) for v in four(pl.ds(BIG + TOWER_ROWS, LINE_ROWS))]
    lines = two_parts((a + b) + (c + d))
    gate = total(pl.ds(PIECE - GATE_ROWS, GATE_ROWS))
    for s, out in enumerate(outs):
        out[:EXP_H1, :] = total(pl.ds(s * EXP_H1, EXP_H1))
        out[EXP_H1 : 2 * EXP_H1, :] = second
        at = 2 * EXP_H1
        out[at : at + TOWER_ROWS, :] = tower
        at += TOWER_ROWS
        out[at : at + LINE_ROWS, :] = lines
        out[at + LINE_ROWS :, :] = jnp.where(quad == s, gate, jnp.zeros_like(gate))


def add_fields_kernel(place_ref, *refs):
    parts, out = refs[:FIELDS], refs[FIELDS]
    odd = place_ref[1] % 2 == 1
    a, b, c, d = [ref[...].astype(f32) for ref in parts]

    def total(a, b, c, d):
        return (a + jnp.where(odd, d, b)) + (c + jnp.where(odd, b, d))

    out[...] = total(a, b, c, d).astype(bf16)
    lines = slice(2 * EXP_H1 + TOWER_ROWS, 2 * EXP_H1 + TOWER_ROWS + LINE_ROWS)
    out[lines, :] = two_parts(total(*[whole(v[lines]) for v in (a, b, c, d)]))


def join_done_kernel(place_ref, *refs):
    parts, (stack_ref, tower_ref, lines_ref, gate_ref) = refs[:QUADS], refs[QUADS:]
    quad = place_ref[0] >> 1
    for q, ref in enumerate(parts):
        stack_ref[q] = ref[: 2 * EXP_H1, :]
        at = 2 * EXP_H1
        tower_ref[aligned(quad ^ q, TOWER_ROWS), :] = ref[at : at + TOWER_ROWS, :].astype(f32)
        at += TOWER_ROWS
        lines_ref[aligned(quad ^ q, 8), :] = whole(ref[at : at + LINE_ROWS, :].astype(f32))
    a, b, c, d = [ref[2 * EXP_H1 + TOWER_ROWS + LINE_ROWS :, :].astype(f32) for ref in parts]
    gate_ref[...] = (a + b) + (c + d)


def assemble_kernel(start, place_ref, *refs):
    parts, (out_ref, wide_ref, sems) = refs[:FIELDS], refs[-3:]
    rows, size = out_ref.shape[0] // FIELDS, wide_ref.shape[1]
    copies = []
    for s, part in enumerate(parts):
        at = pl.ds(lax.rem(place_ref[1] + s, FIELDS) * rows + start, size)
        if s:
            wide_ref[s - 1] = part[...].astype(f32)
        source = wide_ref.at[s - 1] if s else part
        copies.append(pltpu.make_async_copy(source, out_ref.at[at, :], sems.at[s]))
        copies[-1].start()
    for copy in copies:
        copy.wait()


def update_kernel(core, place_ref, grads_ref, *refs):
    first_w, first_m, first_v, second_w, second_m, second_v, second_a = refs[:7]
    outs = refs[-8:]
    outs[7][...] = jnp.zeros((8, LANES), f32)
    expert = place_ref[0] ^ (2 * pl.program_id(0) + core)
    at = aligned(expert, EXP_H1)
    grads = grads_ref[pl.program_id(0)].astype(f32)
    new = adamw(first_w[:, at], first_m[:, at], first_v[:, at], grads[:EXP_H1].T)
    outs[0][...], outs[1][...], outs[2][...] = new
    new = adamw(second_w[at, :], second_m[at, :], second_v[at, :], grads[EXP_H1:])
    outs[3][...], outs[4][...], outs[5][...] = new
    outs[6][...] = blend(second_a[at, :], new[0])


def on_device(
    inputs,
    labels,
    user_ids,
    first_weight,
    first_mean,
    first_square,
    gate_weight,
    gate_mean,
    gate_square,
    second_weight,
    second_mean,
    second_square,
    tower_weight,
    tower_mean,
    tower_square,
    head_weight,
    head_mean,
    head_square,
    biases,
    bias_mean,
    bias_square,
    second_average,
    tower_average,
    head_average,
):
    nfield, nbatch = lax.axis_size("field"), lax.axis_size("batch")
    field, batch = lax.axis_index("field"), lax.axis_index("batch")
    rows_dev, columns = inputs.shape
    rows = rows_dev // nfield
    width = nfield * columns
    users_total = rows_dev * nbatch // USER_ROWS
    place = jnp.stack([batch % GROUP, field]).astype(jnp.int32)

    def shift(value, by):
        return lax.ppermute(value, "field", [(i, (i + by) % nfield) for i in range(nfield)])

    def cross(value, mask):
        return lax.ppermute(value, "batch", [(i, i ^ mask) for i in range(nbatch)])

    def from_fields(value):
        return [value] + [shift(value, s) for s in range(1, nfield)]

    def from_quads(value):
        return [value] + [cross(value, 2 * q) for q in range(1, QUADS)]

    starts = [0]
    for part in CHUNKS:
        starts.append(starts[-1] + part * rows // 32)
    nchunks = len(CHUNKS)

    ids = user_ids.reshape(1, rows)
    labels_t = labels.T
    expert_block = pl.BlockSpec((columns, EXP_H1), lambda i, place_ref: (0, place_ref[0]))
    high = users_total // LANES
    lines = 2 * rows // LANES
    sent = pl.pallas_call(
        piece_kernel,
        grid_spec=pltpu.PrefetchScalarGridSpec(
            num_scalar_prefetch=1, grid=(1,), in_specs=[expert_block, vmem, vmem], out_specs=vmem
        ),
        out_shape=shaped((EXP_H1 + GATES + lines, columns), bf16),
        compiler_params=params(),
        cost_estimate=cost(1e6, 1e5),
        name="first_piece",
    )(place, first_weight, gate_weight.T, user_ids.reshape(rows // LANES, LANES))
    def own_rows(low, high, deps):
        count = (high - low) * nfield
        return pl.pallas_call(
            functools.partial(rows_kernel, starts[low:high]),
            out_shape=[shaped((starts[c + 1] - starts[c], columns), bf16) for c in range(low, high) for _ in range(nfield)],
            in_specs=[smem, anywhere] + [anywhere] * len(deps),
            out_specs=[hbm] * count,
            scratch_shapes=[pltpu.SemaphoreType.DMA((count,))],
            compiler_params=params(),
            cost_estimate=cost(1e3, 1e3),
            name="own_rows",
        )(place, inputs, *deps)

    def exchange_rows(mine, *others):
        return [mine] + [shift(o, s + 1) for s, o in enumerate(others)]

    def exchange_rows_after(deps, rows_of):
        mine, *others = rows_of
        return exchange_rows(mine, *once_there("rows_to_send", others, deps))

    chunk_rows = own_rows(0, nchunks, [])
    chunk_rows = [chunk_rows[c * nfield : (c + 1) * nfield] for c in range(nchunks)]
    prepared = call(
        prepare_kernel,
        "prepare_weights",
        [shaped((LOW_ROWS, LANES), bf16), shaped((WIDE_ROWS, LANES), f32), shaped((1 + TASKS, rows), jnp.int32)],
        [vmem] * 6,
        [
            second_weight,
            tower_weight,
            head_weight.reshape(1, LANES),
            jnp.pad(biases, (0, LANES - TASKS)).reshape(1, -1),
            ids,
            labels_t,
        ],
    )
    bundle, gate_t = call(
        join_fields_kernel,
        "join_fields",
        [shaped((EXP_H1 + lines, width), bf16), shaped((GATES, width), bf16)],
        [vmem] * FIELDS,
        from_fields(sent),
        deps=[chunk_rows[0][0], prepared[0]],
    )
    arrived = [exchange_rows_after([gate_t], chunk_rows[0])]
    own, digits, joined, gate_t = call(
        join_quads_kernel,
        "join_quads",
        [
            shaped((QUADS, EXP_H1, width), bf16),
            shaped((QUADS, lines, width), bf16),
            shaped((starts[1], width), bf16),
            shaped((GATES, width), bf16),
        ],
        [vmem] * (QUADS + FIELDS + 1),
        [*from_quads(bundle), *arrived[0], gate_t],
    )
    arrived[0] = [joined]
    arrived.append(exchange_rows_after([digits], chunk_rows[1]))
    counts = call(count_kernel, "user_counts", shaped((LANES, high), f32), [vmem], [digits])
    hop = GROUP
    while hop < nbatch:
        counts = counts + cross(counts, hop)
        hop *= 2
    counts_other = cross(counts, 1)
    other = cross(own, 1)
    turned_own, gate_all = call(
        turn_kernel,
        "turn_first",
        [shaped((width, H1 // 2), bf16), shaped((width, GATES), bf16)],
        [vmem] * 2,
        [own, gate_t],
    )
    turned_other = cross(turned_own, 1)

    sum_shapes = [
        shaped((H1 + GATES, width), f32),
        shaped((H2, EXP_H1), f32),
        shaped((TASKS * EXP_H2, TASKS * TOWER), f32),
        shaped((H1 + H2, LANES), f32),
        shaped((3, LANES, LANES), f32),
    ]

    def run_layers(c, sums, deps):
        last = c == nchunks - 1
        low, chunk = starts[c], starts[c + 1] - starts[c]
        low_weights, wide_biases, marks = prepared
        operands = [*arrived[c], marks, own, other, gate_t, counts, counts_other, low_weights, wide_biases]
        out_shape = [shaped((H1 + GATES, chunk), bf16), shaped((TASKS, chunk), f32)] + sum_shapes
        if last:
            out_shape += [shaped((QUADS * PIECE, LANES), bf16)] * 2

        def once(shape):
            return pl.BlockSpec(shape, lambda i: (0,) * len(shape), pipeline_mode=pl.Buffered(1))

        return pl.pallas_call(
            functools.partial(layers_kernel, last, bool(sums), len(deps), loss_scale * users_total, low, len(arrived[c])),
            grid=(1,),
            out_shape=out_shape,
            in_specs=[smem]
            + [once(o.shape) for o in operands]
            + [vmem] * len(sums)
            + [hbm] * len(deps),
            out_specs=[once(o.shape) for o in out_shape[:2]]
            + [vmem] * NSUM
            + [once(o.shape) for o in out_shape[2 + NSUM :]],
            input_output_aliases={1 + len(operands) + i: 2 + i for i in range(len(sums))},
            scratch_shapes=[
                pltpu.VMEM((H1, chunk), bf16),
                pltpu.VMEM((H1, chunk), f32),
                pltpu.VMEM((H2, chunk), f32),
                pltpu.VMEM((H2, chunk), f32),
                pltpu.VMEM((GATES, chunk), f32),
                pltpu.VMEM((GATES, chunk), f32),
            ],
            compiler_params=params(LAYERS_MIB),
            cost_estimate=cost(LAYERS_COST * chunk, 1e3),
            name="layers",
        )(place, *operands, *sums, *deps)


    bounds = [0]
    for part in RETURNS:
        bounds.append(bounds[-1] + part * rows // 32)

    def give_back(i, deps):
        spans, taken = [], []
        for c in range(nchunks):
            low, high = max(bounds[i], starts[c]), min(bounds[i + 1], starts[c + 1])
            if low < high:
                spans.append((low - starts[c], high - starts[c]))
                taken.append(d_chunks[c])
        size = bounds[i + 1] - bounds[i]
        mine, *others = call(
            functools.partial(back_kernel, spans),
            "input_gradients",
            [shaped((size, columns), f32)] + [shaped((size, columns), bf16)] * (nfield - 1),
            [vmem] * (len(taken) + 3),
            [*taken, turned_own, turned_other, gate_all],
            flops=BACK_COST * size,
            deps=deps,
            mib=12,
        )
        return [mine] + [shift(o, -(s + 1)) for s, o in enumerate(others)]

    sums, probs, d_chunks, returned = [], [], [], []
    for c in range(nchunks):
        if c == nchunks - 1:
            returned.append(give_back(0, [probs[-1]]))
        d_chunk, prob, *sums = run_layers(c, sums, [r[0] for r in returned])
        probs.append(prob)
        d_chunks.append(d_chunk)
        if c + 2 < nchunks:
            arrived.append(exchange_rows_after([prob], chunk_rows[c + 2]))
    keep, send = sums[NSUM:]
    returned.append(give_back(1, [keep]))
    (send,) = once_there("gradients_to_send", [send], returned[0][1:])

    pieces = call(
        add_cores_kernel,
        "add_cores",
        [shaped((PIECE, LANES), bf16)] * QUADS,
        [smem, vmem, vmem],
        [place, keep, cross(send, 1)],
        deps=returned[1][:1],
    )
    parts = [pieces[0]] + [cross(pieces[q], 2 * q) for q in range(1, QUADS)]
    hop = GROUP
    while hop < nbatch:
        parts = [(p.astype(f32) + cross(p, hop).astype(f32)).astype(bf16) for p in parts]
        hop *= 2
    blocks = call(
        add_quads_kernel,
        "add_quads",
        [shaped((2 * EXP_H1 + SMALL, LANES), bf16)] * nfield,
        [smem] + [vmem] * QUADS,
        [place] + parts,
        deps=returned[1][1:],
    )
    returned.append(give_back(2, [blocks[0]]))
    def assemble(i, before, deps):
        return pl.pallas_call(
            functools.partial(assemble_kernel, bounds[i]),
            out_shape=[shaped((rows_dev, columns), f32)],
            in_specs=[smem, anywhere] + [vmem] * (nfield - 1) + [hbm] * (len(before) + len(deps)),
            out_specs=[hbm],
            input_output_aliases={1 + nfield: 0} if before else {},
            scratch_shapes=[
                pltpu.VMEM((nfield - 1, bounds[i + 1] - bounds[i], columns), f32),
                pltpu.SemaphoreType.DMA((nfield,)),
            ],
            compiler_params=params(),
            cost_estimate=cost(1e3, 1e3),
            name="assemble_input_grad",
        )(place, *returned[i], *before, *deps)

    input_grad = assemble(0, [], [blocks[0]])
    input_grad = assemble(1, input_grad, [blocks[0]])
    done = call(
        add_fields_kernel,
        "add_fields",
        shaped((2 * EXP_H1 + SMALL, LANES), bf16),
        [smem] + [vmem] * nfield,
        [place, blocks[0]] + [shift(blocks[s], -s) for s in range(1, nfield)],
        deps=[returned[2][0], *input_grad],
    )
    done_own, g_tower, lines, g_gate = call(
        join_done_kernel,
        "join_gradients",
        [
            shaped((QUADS, 2 * EXP_H1, LANES), bf16),
            shaped((LANES, LANES), f32),
            shaped((8 * QUADS, LANES), f32),
            shaped((GATES, columns), f32),
        ],
        [smem] + [vmem] * QUADS,
        [place] + from_quads(done),
    )
    done_other = cross(done_own, 1)

    def run_update(core, grads, before):
        first_spec = pl.BlockSpec((columns, EXP_H1), lambda q, place_ref: (0, place_ref[0] ^ (2 * q + core)))
        second_spec = pl.BlockSpec((EXP_H1, EXP_H2), lambda q, place_ref: (place_ref[0] ^ (2 * q + core), 0))
        operands = [
            grads,
            first_weight,
            first_mean,
            first_square,
            second_weight,
            second_mean,
            second_square,
            second_average,
        ]
        specs = [first_spec] * 3 + [second_spec] * 4
        before = list(before or [])[:7]
        return pl.pallas_call(
            functools.partial(update_kernel, core),
            grid_spec=pltpu.PrefetchScalarGridSpec(
                num_scalar_prefetch=1,
                grid=(QUADS,),
                in_specs=[vmem] * len(operands) + [anywhere] * len(before),
                out_specs=specs + [pl.BlockSpec((8, LANES), lambda q, place_ref: (0, 0))],
            ),
            out_shape=[shaped((columns, H1), f32)] * 3
            + [shaped((H1, EXP_H2), f32)] * 4
            + [shaped((8, LANES), f32)],
            input_output_aliases={1 + len(operands) + i: i for i in range(len(before))},
            compiler_params=params(),
            cost_estimate=cost(1e6, 8e6),
            name="update_layers",
        )(place, *operands, *before)

    updated_half = run_update(0, done_own, None)
    updated = run_update(1, done_other, updated_half)
    new_first, new_second, avg_second = updated[:3], updated[3:6], updated[6]

    at = (H1 + H2) // LANES
    g_head = lines[at + 1]
    g_bias = jnp.concatenate([lines[: at + 1].reshape(-1), lines[at + 2, :TASKS]])
    new_gate = adamw(gate_weight, gate_mean, gate_square, g_gate.T)
    new_tower = adamw(tower_weight, tower_mean, tower_square, g_tower)
    avg_tower = blend(tower_average, new_tower[0])
    new_head = adamw(head_weight, head_mean, head_square, g_head)
    avg_head = blend(head_average, new_head[0])
    new_bias = adamw(biases, bias_mean, bias_square, g_bias)

    (input_grad,) = assemble(2, input_grad, [updated[7]])
    predicted = jnp.concatenate(probs, axis=1).T
    return (
        predicted,
        input_grad,
        *new_first,
        *new_gate,
        *new_second,
        *new_tower,
        *new_head,
        *new_bias,
        avg_second,
        avg_tower,
        avg_head,
    )


def solution(mesh):
    fields, copied = P("field", None), P()
    rows = P(("batch", "field"), None)
    in_specs = (
        (P("batch", "field"), rows, P(("batch", "field"))) + (fields,) * 6 + (copied,) * 15
    )
    out_specs = (rows, P("batch", "field")) + (fields,) * 6 + (copied,) * 15
    return jax.shard_map(
        on_device, mesh=mesh, in_specs=in_specs, out_specs=out_specs, check_vma=False
    )
```

```python
import functools

import jax
import jax.numpy as jnp
from jax import lax
from jax.experimental import pallas as pl
from jax.experimental.pallas import tpu as pltpu
from jax.sharding import PartitionSpec as P

EXPERTS = 8
EXP_H1 = 256
EXP_H2 = 128
TASKS = 2
TOWER = 64
USER_ROWS = 4
STEP = 10
H1 = 2048
H2 = 1024
GATES = TASKS * EXPERTS
LANES = 128
GROUP = 8
QUADS = GROUP // 2
CHUNKS = (8, 12, 12)
RETURNS = (12, 10, 10)
MIB = 1024 * 1024
LAYERS_MIB = 32
FIELDS = 4
BIG = (FIELDS + 1) * EXP_H1
TOWER_ROWS, LINE_ROWS, GATE_ROWS = 32, 16, 16
SMALL = TOWER_ROWS + LINE_ROWS + GATE_ROWS
PIECE = BIG + SMALL

beta_one = 0.9
beta_two = 0.999
learn_rate = 0.1
decay_rate = 0.01
adam_eps = 1e-08
average_rate = 0.8
loss_scale = 512.0

LAYERS_COST = 1e7
BACK_COST = 1e3

f32 = jnp.float32
bf16 = jnp.bfloat16
smem = pl.BlockSpec(memory_space=pltpu.SMEM)
vmem = pl.BlockSpec(memory_space=pltpu.VMEM)
anywhere = pl.BlockSpec(memory_space=pl.ANY)
hbm = pl.BlockSpec(memory_space=pltpu.HBM)


def sigmoid(values):
    return 0.5 * jnp.tanh(0.5 * values) + 0.5


def dot(left, right):
    return jnp.dot(left, right, preferred_element_type=f32)


def dot_nt(left, right, precision=None):
    return lax.dot_general(
        left, right, (((1,), (1,)), ((), ())), precision=precision, preferred_element_type=f32
    )


def adamw(weight, moment, square, gradient):
    new_moment = beta_one * moment + (1.0 - beta_one) * gradient
    new_square = beta_two * square + (1.0 - beta_two) * gradient * gradient
    moment_hat = new_moment / (1.0 - beta_one**STEP)
    square_hat = new_square / (1.0 - beta_two**STEP)
    new_weight = weight - learn_rate * (
        moment_hat / (jnp.sqrt(square_hat) + adam_eps) + decay_rate * weight
    )
    return (new_weight, new_moment, new_square)


def blend(average, weight):
    return average_rate * average + (1.0 - average_rate) * weight


def params(mib=8):
    return pltpu.CompilerParams(vmem_limit_bytes=mib * MIB)


def cost(flops, nbytes):
    return pl.CostEstimate(flops=int(flops), bytes_accessed=int(nbytes), transcendentals=0)


def shaped(shape, dtype):
    return jax.ShapeDtypeStruct(shape, dtype)


def aligned(index, size):
    return pl.ds(pl.multiple_of(index * size, size), size)


def call(kernel, name, out_shape, in_specs, operands, flops=1e6, nbytes=1e6, deps=(), mib=8):
    def body(*refs):
        given = len(operands)
        kernel(*refs[:given], *refs[given + len(deps) :])

    return pl.pallas_call(
        body,
        out_shape=out_shape,
        in_specs=list(in_specs) + [hbm] * len(deps),
        out_specs=jax.tree.map(lambda _: vmem, out_shape),
        compiler_params=params(mib),
        cost_estimate=cost(flops, nbytes),
        name=name,
    )(*operands, *deps)


def once_there(name, values, deps):
    return pl.pallas_call(
        lambda *refs: None,
        out_shape=[shaped(v.shape, v.dtype) for v in values],
        in_specs=[hbm] * (len(values) + len(deps)),
        out_specs=[hbm] * len(values),
        input_output_aliases={i: i for i in range(len(values))},
        compiler_params=params(),
        cost_estimate=cost(1, 1),
        name=name,
    )(*values, *deps)


def piece_kernel(place_ref, first_ref, gate_ref, ids_ref, send_ref):
    send_ref[:EXP_H1, :] = (0.5 * first_ref[...]).T.astype(bf16)
    at = EXP_H1 + GATES
    send_ref[EXP_H1:at, :] = gate_ref[...].astype(bf16)
    ids, lines = ids_ref[...], ids_ref.shape[0]
    send_ref[at : at + lines, :] = (ids % 256).astype(f32).astype(bf16)
    send_ref[at + lines :, :] = (ids // 256).astype(f32).astype(bf16)


def count_kernel(digits_ref, counts_ref):
    lines = digits_ref.shape[1] // 2
    width = digits_ref.shape[2]
    high = lax.broadcasted_iota(jnp.int32, (counts_ref.shape[1], width), 0).astype(f32)
    low = lax.broadcasted_iota(jnp.int32, (LANES, width), 0).astype(f32)
    total = jnp.zeros(counts_ref.shape, f32)
    for q in range(QUADS):
        digits = digits_ref[q].astype(f32)
        ids = digits[:lines] + 256.0 * digits[lines:]
        ids_high = jnp.floor(ids * (1.0 / LANES))
        ids_low = ids - LANES * ids_high
        for r in range(lines):
            one_high = jnp.where(high == ids_high[r : r + 1], 1.0, 0.0).astype(bf16)
            one_low = jnp.where(low == ids_low[r : r + 1], 1.0, 0.0).astype(bf16)
            total = total + dot_nt(one_low, one_high)
    counts_ref[...] = total


LOW_TURNED = H1
LOW_TOWERS = 2 * H1
LOW_ROWS = LOW_TOWERS + 2 * TASKS * EXP_H2
WIDE_TWO = H1
WIDE_TOP = H1 + H2
WIDE_ROWS = WIDE_TOP + 3 * LANES


def prepare_kernel(second_ref, tower_ref, head_ref, bias_ref, ids_ref, labels_ref, low_ref, wide_ref, marks_ref):
    low_ref[:H1, :] = (0.5 * second_ref[...]).astype(bf16)
    for block in range(H1 // LANES):
        turned = (0.5 * second_ref[pl.ds(block * LANES, LANES), :]).T
        low_ref[pl.ds(LOW_TURNED + block * LANES, LANES), :] = turned.astype(bf16)
    tower = tower_ref[...]
    none = jnp.zeros((EXP_H2, TOWER), f32)
    left = jnp.concatenate([tower[:, :TOWER], none], axis=1)
    right = jnp.concatenate([none, tower[:, TOWER:]], axis=1)
    for i, block in enumerate((left, right, left.T, right.T)):
        low_ref[pl.ds(LOW_TOWERS + i * LANES, LANES), :] = block.astype(bf16)

    def column(row):
        return jnp.broadcast_to(row, (LANES, LANES)).T

    for r in range((H1 + H2) // LANES):
        wide_ref[pl.ds(r * LANES, LANES), :] = 0.5 * column(bias_ref[:, r * LANES : (r + 1) * LANES])
    at = H1 + H2
    wide_ref[pl.ds(WIDE_TOP, LANES), :] = column(bias_ref[:, at : at + LANES])
    wide_ref[pl.ds(WIDE_TOP + LANES, LANES), :] = column(head_ref[...])
    wide_ref[pl.ds(WIDE_TOP + 2 * LANES, LANES), :] = column(bias_ref[:, at + LANES : at + 2 * LANES])
    marks_ref[:1, :] = ids_ref[...]
    marks_ref[1:, :] = labels_ref[...]


def join_fields_kernel(*refs):
    sent, (bundle_ref, gate_ref) = refs[:FIELDS], refs[FIELDS:]
    width = sent[0].shape[1]
    for s, ref in enumerate(sent):
        at = slice(s * width, (s + 1) * width)
        bundle_ref[:EXP_H1, at] = ref[:EXP_H1, :]
        gate_ref[:, at] = ref[EXP_H1 : EXP_H1 + GATES, :]
        bundle_ref[EXP_H1:, at] = ref[EXP_H1 + GATES :, :]


def join_quads_kernel(*refs):
    bundles, refs = refs[:QUADS], refs[QUADS:]
    rows, gate_ref, (stack_ref, digits_ref, joined_ref, gate_out) = refs[:FIELDS], refs[FIELDS], refs[FIELDS + 1 :]
    for q, ref in enumerate(bundles):
        stack_ref[q] = ref[:EXP_H1, :]
        digits_ref[q] = ref[EXP_H1:, :]
    width = rows[0].shape[1]
    for s, ref in enumerate(rows):
        joined_ref[:, s * width : (s + 1) * width] = ref[...]
    gate_out[...] = gate_ref[...]


def rows_kernel(starts, place_ref, inputs_ref, *refs):
    outs, sems = refs[-1 - len(starts) * FIELDS : -1], refs[-1]
    rows = inputs_ref.shape[0] // FIELDS
    copies = []
    for i, out in enumerate(outs):
        chunk, s = divmod(i, FIELDS)
        at = pl.ds(lax.rem(place_ref[1] + s, FIELDS) * rows + starts[chunk], out.shape[0])
        copies.append(pltpu.make_async_copy(inputs_ref.at[at, :], out, sems.at[i]))
        copies[-1].start()
    for copy in copies:
        copy.wait()


def turn_kernel(stack_ref, gate_ref, out_ref, gate_out):
    gate_out[...] = gate_ref[...].T
    for q in range(QUADS):
        out_ref[:, q * EXP_H1 : (q + 1) * EXP_H1] = stack_ref[q].T


NSUM = 5


def layers_kernel(last, with_sums, ndeps, scale, low_row, nrows, place_ref, *refs):
    xs, refs = refs[:nrows], refs[nrows:]
    marks_ref, own_ref, other_ref, gate_ref, counts_a, counts_b, low_ref, wide_ref = refs[:8]
    refs = refs[8:]
    given = [None] * NSUM
    if with_sums:
        given, refs = refs[:NSUM], refs[NSUM:]
    refs = refs[ndeps:]
    d_ref, prob_ref, refs = refs[0], refs[1], refs[2:]
    sums, refs = refs[:NSUM], refs[NSUM:]
    if last:
        keep_ref, send_ref, refs = refs[0], refs[1], refs[2:]
    sum_first, sum_second, sum_tower, sum_bias, sum_top = sums
    hidden_ref, slope_ref, two_ref, slope_two_ref, gates_ref, d_gates_ref = refs
    rows = prob_ref.shape[1]
    mine = slice(low_row, low_row + rows)
    place = place_ref[0]

    def add(which, at, value):
        sums[which][at] = value if given[which] is None else given[which][at] + value

    def fold(values):
        out = values[:, :LANES]
        for at in range(LANES, values.shape[1], LANES):
            out = out + values[:, at : at + LANES]
        return out

    def wide(values):
        return jnp.concatenate([values] * (rows // LANES), axis=1)

    def silu_of_twice(half):
        swing = jnp.tanh(half)
        above = 1.0 + swing
        value = half * above
        return value, above + value * (1.0 - swing)

    ids = marks_ref[:1, mine]
    counts = counts_a[...] + counts_b[...]
    present = jnp.sum(jnp.where(counts > 0.0, 1.0, 0.0), keepdims=True)
    high = lax.broadcasted_iota(jnp.int32, (counts.shape[1], rows), 0)
    low = lax.broadcasted_iota(jnp.int32, (LANES, rows), 0)
    one_high = jnp.where(high == ids // LANES, 1.0, 0.0).astype(bf16)
    top_digit = jnp.floor(counts * (1.0 / 65536.0))
    counts = counts - 65536.0 * top_digit
    mid_digit = jnp.floor(counts * (1.0 / 256.0))
    low_digit = counts - 256.0 * mid_digit
    found = dot(low_digit.astype(bf16), one_high)
    found = found + 256.0 * dot(mid_digit.astype(bf16), one_high)
    found = found + 65536.0 * dot(top_digit.astype(bf16), one_high)
    found = jnp.sum(jnp.where(low == ids % LANES, found, 0.0), axis=0, keepdims=True)
    row_weight = scale / (present * found)

    inputs = jnp.concatenate([x[...] for x in xs], axis=1) if nrows > 1 else xs[0][...]
    turned_in = inputs.T
    logits = dot(gate_ref[...], turned_in).reshape(TASKS, EXPERTS, rows)
    shifted = jnp.exp(logits - jnp.max(logits, axis=1, keepdims=True))
    gates = shifted / jnp.sum(shifted, axis=1, keepdims=True)
    gates_ref[...] = gates.reshape(GATES, rows)
    slots = [(c, q) for c in range(2) for q in range(QUADS)]
    mixed = [jnp.zeros((EXP_H2, rows), f32) for _ in range(TASKS)]
    for t, (c, q) in enumerate(slots):
        e = place ^ (2 * q + c)
        one, two = pl.ds(t * EXP_H1, EXP_H1), pl.ds(t * EXP_H2, EXP_H2)
        weight = (other_ref if c else own_ref)[q]
        half_one = dot(weight, turned_in) + wide(wide_ref[aligned(e, EXP_H1), :])
        hidden, slope_ref[one, :] = silu_of_twice(half_one)
        hidden_low = hidden.astype(bf16)
        hidden_ref[one, :] = hidden_low
        at = pl.multiple_of(LOW_TURNED + e * EXP_H1, EXP_H1)
        turned = jnp.concatenate([low_ref[pl.ds(at, LANES), :], low_ref[pl.ds(at + LANES, LANES), :]], axis=1)
        at = pl.multiple_of(WIDE_TWO + e * EXP_H2, EXP_H2)
        half_two = dot(turned, hidden_low) + wide(wide_ref[pl.ds(at, EXP_H2), :])
        hidden, slope_two_ref[two, :] = silu_of_twice(half_two)
        two_ref[two, :] = hidden
        for k in range(TASKS):
            mixed[k] = mixed[k] + gates_ref[pl.ds(k * EXPERTS + e, 1), :] * hidden
    mixed_low = jnp.concatenate(mixed, axis=0).astype(bf16)
    at = LOW_TOWERS + TASKS * EXP_H2
    tower_fwd = jnp.concatenate([low_ref[at : at + LANES, :], low_ref[at + LANES :, :]], axis=1)
    tops = [wide_ref[WIDE_TOP + k * LANES : WIDE_TOP + (k + 1) * LANES, :] for k in range(3)]
    pre_tower = dot(tower_fwd, mixed_low) + wide(tops[0])
    logistic = sigmoid(pre_tower)
    upper = pre_tower * logistic
    slope_tower = logistic + upper * (1.0 - logistic)
    head = wide(tops[1])
    logit = jnp.sum((upper * head).reshape(TASKS, TOWER, rows), axis=1)
    logit = logit + wide(tops[2][:TASKS, :])
    prob = 1.0 / (1.0 + jnp.exp(-logit))
    prob_ref[...] = prob
    d_logit = row_weight * (prob - marks_ref[1:, mine].astype(f32))
    d_wide = jnp.broadcast_to(d_logit[:, None, :], (TASKS, TOWER, rows)).reshape(LANES, rows)
    d_tower = (d_wide * head * slope_tower).astype(bf16)
    add(4, 0, fold(d_tower.astype(f32)))
    add(4, 1, fold(d_wide * upper))
    low_rows = jnp.zeros((LANES - TASKS, LANES), f32)
    add(4, 2, jnp.concatenate([fold(d_logit), low_rows], axis=0))
    add(2, ..., dot_nt(mixed_low, d_tower))
    d_mixed = dot(low_ref[LOW_TOWERS : LOW_TOWERS + TASKS * EXP_H2, :], d_tower)
    parts = [d_mixed[k * EXP_H2 : (k + 1) * EXP_H2, :] for k in range(TASKS)]
    for t, (c, q) in enumerate(slots):
        e = place ^ (2 * q + c)
        one, two = pl.ds(t * EXP_H1, EXP_H1), pl.ds(t * EXP_H2, EXP_H2)
        hidden = two_ref[two, :]
        d_hidden = jnp.zeros((EXP_H2, rows), f32)
        for k in range(TASKS):
            at = pl.ds(k * EXPERTS + e, 1)
            d_gates_ref[at, :] = jnp.sum(parts[k] * hidden, axis=0, keepdims=True)
            d_hidden = d_hidden + gates_ref[at, :] * parts[k]
        d_two = d_hidden * slope_two_ref[two, :]
        at = pl.ds(pl.multiple_of(H1 + e * EXP_H2, EXP_H2), EXP_H2)
        add(3, (at, slice(None)), fold(d_two))
        d_two = d_two.astype(bf16)
        add(1, (two, slice(None)), dot_nt(d_two, hidden_ref[one, :]))
        d_one = dot(low_ref[aligned(e, EXP_H1), :], d_two) * slope_ref[one, :]
        add(3, (aligned(e, EXP_H1), slice(None)), fold(d_one))
        d_ref[one, :] = d_one.astype(bf16)
    d_gates = d_gates_ref[...].reshape(TASKS, EXPERTS, rows)
    centered = d_gates - jnp.sum(gates * d_gates, axis=1, keepdims=True)
    d_ref[pl.ds(H1, GATES), :] = (gates * centered).reshape(GATES, rows).astype(bf16)
    add(0, ..., dot(d_ref[...], inputs))

    if last:
        for t, (c, q) in enumerate(slots):
            one, two = pl.ds(t * EXP_H1, EXP_H1), pl.ds(t * EXP_H2, EXP_H2)
            out = send_ref if c else keep_ref
            for s in range(FIELDS):
                at = pl.ds(q * BIG + s * EXP_H1, EXP_H1)
                out[at, :] = (0.5 * sum_first[one, s * LANES : (s + 1) * LANES]).astype(bf16)
            out[pl.ds(q * BIG + FIELDS * EXP_H1, EXP_H1), :] = (0.5 * sum_second[two, :]).T.astype(bf16)
        ones = jnp.ones((8, LANES), f32)
        bias = dot_nt(0.5 * ones, sum_bias[...], lax.Precision.HIGHEST)[:1, :]
        lines = [bias[:, r * LANES : (r + 1) * LANES] for r in range((H1 + H2) // LANES)]
        lines += [dot_nt(ones, sum_top[k], lax.Precision.HIGHEST)[:1, :] for k in range(3)]
        lines += [jnp.zeros((1, LANES), f32)] * (8 * QUADS - len(lines))
        for out in (keep_ref, send_ref):
            at = QUADS * BIG
            for q in range(QUADS):
                block = sum_tower[pl.ds(q * TOWER_ROWS, TOWER_ROWS), :TOWER]
                below = sum_tower[pl.ds(EXP_H2 + q * TOWER_ROWS, TOWER_ROWS), TOWER:]
                out[pl.ds(at, TOWER_ROWS), :] = jnp.concatenate([block, below], axis=1).astype(bf16)
                at += TOWER_ROWS
                out[pl.ds(at, LINE_ROWS), :] = two_parts(jnp.concatenate(lines[8 * q : 8 * q + 8], axis=0))
                at += LINE_ROWS
                block = sum_first[pl.ds(H1, GATES), q * LANES : (q + 1) * LANES]
                out[pl.ds(at, GATE_ROWS), :] = block.astype(bf16)
                at += GATE_ROWS


def back_kernel(spans, *refs):
    d_refs, refs = refs[: len(spans)], refs[len(spans) :]
    own_ref, other_ref, gate_ref, out_own = refs[:4]
    half, at = H1 // 2, 0
    for (low, high), d_ref in zip(spans, d_refs):
        here = slice(low, high)
        turned = dot(own_ref[...], d_ref[:half, here]) + dot(other_ref[...], d_ref[half:H1, here])
        turned = turned + dot(gate_ref[...], d_ref[H1:, here])
        grads = turned.T
        width, rows = out_own.shape[1], pl.ds(at, high - low)
        out_own[rows, :] = grads[:, :width]
        for s, ref in enumerate(refs[-FIELDS + 1 :]):
            ref[rows, :] = grads[:, (s + 1) * width : (s + 2) * width].astype(bf16)
        at += high - low


def two_parts(lines):
    low = lines.astype(bf16)
    return jnp.concatenate([low.astype(f32), lines - low.astype(f32)], axis=0).astype(bf16)


def whole(parts):
    half = parts.shape[0] // 2
    return parts[:half] + parts[half:]


def add_cores_kernel(place_ref, keep_ref, got_ref, *outs):
    quad = place_ref[0] >> 1

    def both(at):
        return keep_ref[at, :].astype(f32), got_ref[at, :].astype(f32)

    for q, out in enumerate(outs):
        a, b = both(pl.ds(q * BIG, BIG))
        out[:BIG, :] = (a + b).astype(bf16)
        a, b = both(pl.ds(pl.multiple_of(QUADS * BIG + (quad ^ q) * SMALL, SMALL), SMALL))
        out[BIG:, :] = (a + b).astype(bf16)
        lines = slice(TOWER_ROWS, TOWER_ROWS + LINE_ROWS)
        out[BIG + TOWER_ROWS : BIG + TOWER_ROWS + LINE_ROWS, :] = two_parts(whole(a[lines]) + whole(b[lines]))


def add_quads_kernel(place_ref, *refs):
    parts, outs = refs[:QUADS], refs[QUADS:]
    quad, field = place_ref[0] >> 1, place_ref[1]

    def four(at):
        return [ref[at, :].astype(f32) for ref in parts]

    def total(at):
        a, b, c, d = four(at)
        return ((a + b) + (c + d)).astype(bf16)

    second = total(pl.ds(FIELDS * EXP_H1, EXP_H1))
    tower = total(pl.ds(BIG, TOWER_ROWS))
    a, b, c, d = [whole(v) for v in four(pl.ds(BIG + TOWER_ROWS, LINE_ROWS))]
    lines = two_parts((a + b) + (c + d))
    gate = total(pl.ds(PIECE - GATE_ROWS, GATE_ROWS))
    for s, out in enumerate(outs):
        out[:EXP_H1, :] = total(pl.ds(s * EXP_H1, EXP_H1))
        out[EXP_H1 : 2 * EXP_H1, :] = second
        at = 2 * EXP_H1
        out[at : at + TOWER_ROWS, :] = tower
        at += TOWER_ROWS
        out[at : at + LINE_ROWS, :] = lines
        out[at + LINE_ROWS :, :] = jnp.where(quad == s, gate, jnp.zeros_like(gate))


def add_fields_kernel(place_ref, *refs):
    parts, out = refs[:FIELDS], refs[FIELDS]
    odd = place_ref[1] % 2 == 1
    a, b, c, d = [ref[...].astype(f32) for ref in parts]

    def total(a, b, c, d):
        return (a + jnp.where(odd, d, b)) + (c + jnp.where(odd, b, d))

    out[...] = total(a, b, c, d).astype(bf16)
    lines = slice(2 * EXP_H1 + TOWER_ROWS, 2 * EXP_H1 + TOWER_ROWS + LINE_ROWS)
    out[lines, :] = two_parts(total(*[whole(v[lines]) for v in (a, b, c, d)]))


def join_done_kernel(place_ref, *refs):
    parts, (stack_ref, tower_ref, lines_ref, gate_ref) = refs[:QUADS], refs[QUADS:]
    quad = place_ref[0] >> 1
    for q, ref in enumerate(parts):
        stack_ref[q] = ref[: 2 * EXP_H1, :]
        at = 2 * EXP_H1
        tower_ref[aligned(quad ^ q, TOWER_ROWS), :] = ref[at : at + TOWER_ROWS, :].astype(f32)
        at += TOWER_ROWS
        lines_ref[aligned(quad ^ q, 8), :] = whole(ref[at : at + LINE_ROWS, :].astype(f32))
    a, b, c, d = [ref[2 * EXP_H1 + TOWER_ROWS + LINE_ROWS :, :].astype(f32) for ref in parts]
    gate_ref[...] = (a + b) + (c + d)


def assemble_kernel(start, place_ref, *refs):
    parts, (out_ref, wide_ref, sems) = refs[:FIELDS], refs[-3:]
    rows, size = out_ref.shape[0] // FIELDS, wide_ref.shape[1]
    copies = []
    for s, part in enumerate(parts):
        at = pl.ds(lax.rem(place_ref[1] + s, FIELDS) * rows + start, size)
        if s:
            wide_ref[s - 1] = part[...].astype(f32)
        source = wide_ref.at[s - 1] if s else part
        copies.append(pltpu.make_async_copy(source, out_ref.at[at, :], sems.at[s]))
        copies[-1].start()
    for copy in copies:
        copy.wait()


def update_kernel(core, place_ref, grads_ref, *refs):
    first_w, first_m, first_v, second_w, second_m, second_v, second_a = refs[:7]
    outs = refs[-8:]
    outs[7][...] = jnp.zeros((8, LANES), f32)
    expert = place_ref[0] ^ (2 * pl.program_id(0) + core)
    at = aligned(expert, EXP_H1)
    grads = grads_ref[pl.program_id(0)].astype(f32)
    new = adamw(first_w[:, at], first_m[:, at], first_v[:, at], grads[:EXP_H1].T)
    outs[0][...], outs[1][...], outs[2][...] = new
    new = adamw(second_w[at, :], second_m[at, :], second_v[at, :], grads[EXP_H1:])
    outs[3][...], outs[4][...], outs[5][...] = new
    outs[6][...] = blend(second_a[at, :], new[0])


def on_device(
    inputs,
    labels,
    user_ids,
    first_weight,
    first_mean,
    first_square,
    gate_weight,
    gate_mean,
    gate_square,
    second_weight,
    second_mean,
    second_square,
    tower_weight,
    tower_mean,
    tower_square,
    head_weight,
    head_mean,
    head_square,
    biases,
    bias_mean,
    bias_square,
    second_average,
    tower_average,
    head_average,
):
    nfield, nbatch = lax.axis_size("field"), lax.axis_size("batch")
    field, batch = lax.axis_index("field"), lax.axis_index("batch")
    rows_dev, columns = inputs.shape
    rows = rows_dev // nfield
    width = nfield * columns
    users_total = rows_dev * nbatch // USER_ROWS
    place = jnp.stack([batch % GROUP, field]).astype(jnp.int32)

    def shift(value, by):
        return lax.ppermute(value, "field", [(i, (i + by) % nfield) for i in range(nfield)])

    def cross(value, mask):
        return lax.ppermute(value, "batch", [(i, i ^ mask) for i in range(nbatch)])

    def from_fields(value):
        return [value] + [shift(value, s) for s in range(1, nfield)]

    def from_quads(value):
        return [value] + [cross(value, 2 * q) for q in range(1, QUADS)]

    starts = [0]
    for part in CHUNKS:
        starts.append(starts[-1] + part * rows // 32)
    nchunks = len(CHUNKS)

    ids = user_ids.reshape(1, rows)
    labels_t = labels.T
    expert_block = pl.BlockSpec((columns, EXP_H1), lambda i, place_ref: (0, place_ref[0]))
    high = users_total // LANES
    lines = 2 * rows // LANES
    sent = pl.pallas_call(
        piece_kernel,
        grid_spec=pltpu.PrefetchScalarGridSpec(
            num_scalar_prefetch=1, grid=(1,), in_specs=[expert_block, vmem, vmem], out_specs=vmem
        ),
        out_shape=shaped((EXP_H1 + GATES + lines, columns), bf16),
        compiler_params=params(),
        cost_estimate=cost(1e6, 1e5),
        name="first_piece",
    )(place, first_weight, gate_weight.T, user_ids.reshape(rows // LANES, LANES))
    def own_rows(low, high, deps):
        count = (high - low) * nfield
        return pl.pallas_call(
            functools.partial(rows_kernel, starts[low:high]),
            out_shape=[shaped((starts[c + 1] - starts[c], columns), bf16) for c in range(low, high) for _ in range(nfield)],
            in_specs=[smem, anywhere] + [anywhere] * len(deps),
            out_specs=[hbm] * count,
            scratch_shapes=[pltpu.SemaphoreType.DMA((count,))],
            compiler_params=params(),
            cost_estimate=cost(1e3, 1e3),
            name="own_rows",
        )(place, inputs, *deps)

    def exchange_rows(mine, *others):
        return [mine] + [shift(o, s + 1) for s, o in enumerate(others)]

    def exchange_rows_after(deps, rows_of):
        mine, *others = rows_of
        return exchange_rows(mine, *once_there("rows_to_send", others, deps))

    chunk_rows = own_rows(0, nchunks, [])
    chunk_rows = [chunk_rows[c * nfield : (c + 1) * nfield] for c in range(nchunks)]
    prepared = call(
        prepare_kernel,
        "prepare_weights",
        [shaped((LOW_ROWS, LANES), bf16), shaped((WIDE_ROWS, LANES), f32), shaped((1 + TASKS, rows), jnp.int32)],
        [vmem] * 6,
        [
            second_weight,
            tower_weight,
            head_weight.reshape(1, LANES),
            jnp.pad(biases, (0, LANES - TASKS)).reshape(1, -1),
            ids,
            labels_t,
        ],
    )
    bundle, gate_t = call(
        join_fields_kernel,
        "join_fields",
        [shaped((EXP_H1 + lines, width), bf16), shaped((GATES, width), bf16)],
        [vmem] * FIELDS,
        from_fields(sent),
        deps=[chunk_rows[0][0], prepared[0]],
    )
    arrived = [exchange_rows_after([gate_t], chunk_rows[0])]
    own, digits, joined, gate_t = call(
        join_quads_kernel,
        "join_quads",
        [
            shaped((QUADS, EXP_H1, width), bf16),
            shaped((QUADS, lines, width), bf16),
            shaped((starts[1], width), bf16),
            shaped((GATES, width), bf16),
        ],
        [vmem] * (QUADS + FIELDS + 1),
        [*from_quads(bundle), *arrived[0], gate_t],
    )
    arrived[0] = [joined]
    arrived.append(exchange_rows_after([digits], chunk_rows[1]))
    counts = call(count_kernel, "user_counts", shaped((LANES, high), f32), [vmem], [digits])
    hop = GROUP
    while hop < nbatch:
        counts = counts + cross(counts, hop)
        hop *= 2
    counts_other = cross(counts, 1)
    other = cross(own, 1)
    turned_own, gate_all = call(
        turn_kernel,
        "turn_first",
        [shaped((width, H1 // 2), bf16), shaped((width, GATES), bf16)],
        [vmem] * 2,
        [own, gate_t],
    )
    turned_other = cross(turned_own, 1)

    sum_shapes = [
        shaped((H1 + GATES, width), f32),
        shaped((H2, EXP_H1), f32),
        shaped((TASKS * EXP_H2, TASKS * TOWER), f32),
        shaped((H1 + H2, LANES), f32),
        shaped((3, LANES, LANES), f32),
    ]

    def run_layers(c, sums, deps):
        last = c == nchunks - 1
        low, chunk = starts[c], starts[c + 1] - starts[c]
        low_weights, wide_biases, marks = prepared
        operands = [*arrived[c], marks, own, other, gate_t, counts, counts_other, low_weights, wide_biases]
        out_shape = [shaped((H1 + GATES, chunk), bf16), shaped((TASKS, chunk), f32)] + sum_shapes
        if last:
            out_shape += [shaped((QUADS * PIECE, LANES), bf16)] * 2

        def once(shape):
            return pl.BlockSpec(shape, lambda i: (0,) * len(shape), pipeline_mode=pl.Buffered(1))

        return pl.pallas_call(
            functools.partial(layers_kernel, last, bool(sums), len(deps), loss_scale * users_total, low, len(arrived[c])),
            grid=(1,),
            out_shape=out_shape,
            in_specs=[smem]
            + [once(o.shape) for o in operands]
            + [vmem] * len(sums)
            + [hbm] * len(deps),
            out_specs=[once(o.shape) for o in out_shape[:2]]
            + [vmem] * NSUM
            + [once(o.shape) for o in out_shape[2 + NSUM :]],
            input_output_aliases={1 + len(operands) + i: 2 + i for i in range(len(sums))},
            scratch_shapes=[
                pltpu.VMEM((H1, chunk), bf16),
                pltpu.VMEM((H1, chunk), f32),
                pltpu.VMEM((H2, chunk), f32),
                pltpu.VMEM((H2, chunk), f32),
                pltpu.VMEM((GATES, chunk), f32),
                pltpu.VMEM((GATES, chunk), f32),
            ],
            compiler_params=params(LAYERS_MIB),
            cost_estimate=cost(LAYERS_COST * chunk, 1e3),
            name="layers",
        )(place, *operands, *sums, *deps)


    bounds = [0]
    for part in RETURNS:
        bounds.append(bounds[-1] + part * rows // 32)

    def give_back(i, deps):
        spans, taken = [], []
        for c in range(nchunks):
            low, high = max(bounds[i], starts[c]), min(bounds[i + 1], starts[c + 1])
            if low < high:
                spans.append((low - starts[c], high - starts[c]))
                taken.append(d_chunks[c])
        size = bounds[i + 1] - bounds[i]
        mine, *others = call(
            functools.partial(back_kernel, spans),
            "input_gradients",
            [shaped((size, columns), f32)] + [shaped((size, columns), bf16)] * (nfield - 1),
            [vmem] * (len(taken) + 3),
            [*taken, turned_own, turned_other, gate_all],
            flops=BACK_COST * size,
            deps=deps,
            mib=12,
        )
        return [mine] + [shift(o, -(s + 1)) for s, o in enumerate(others)]

    sums, probs, d_chunks, returned = [], [], [], []
    for c in range(nchunks):
        if c == nchunks - 1:
            returned.append(give_back(0, [probs[-1]]))
        d_chunk, prob, *sums = run_layers(c, sums, [r[0] for r in returned])
        probs.append(prob)
        d_chunks.append(d_chunk)
        if c + 2 < nchunks:
            arrived.append(exchange_rows_after([prob], chunk_rows[c + 2]))
    keep, send = sums[NSUM:]
    returned.append(give_back(1, [keep]))
    (send,) = once_there("gradients_to_send", [send], returned[0][1:])

    pieces = call(
        add_cores_kernel,
        "add_cores",
        [shaped((PIECE, LANES), bf16)] * QUADS,
        [smem, vmem, vmem],
        [place, keep, cross(send, 1)],
        deps=returned[1][:1],
    )
    parts = [pieces[0]] + [cross(pieces[q], 2 * q) for q in range(1, QUADS)]
    hop = GROUP
    while hop < nbatch:
        parts = [(p.astype(f32) + cross(p, hop).astype(f32)).astype(bf16) for p in parts]
        hop *= 2
    blocks = call(
        add_quads_kernel,
        "add_quads",
        [shaped((2 * EXP_H1 + SMALL, LANES), bf16)] * nfield,
        [smem] + [vmem] * QUADS,
        [place] + parts,
        deps=returned[1][1:],
    )
    returned.append(give_back(2, [blocks[0]]))
    def assemble(i, before, deps):
        return pl.pallas_call(
            functools.partial(assemble_kernel, bounds[i]),
            out_shape=[shaped((rows_dev, columns), f32)],
            in_specs=[smem, anywhere] + [vmem] * (nfield - 1) + [hbm] * (len(before) + len(deps)),
            out_specs=[hbm],
            input_output_aliases={1 + nfield: 0} if before else {},
            scratch_shapes=[
                pltpu.VMEM((nfield - 1, bounds[i + 1] - bounds[i], columns), f32),
                pltpu.SemaphoreType.DMA((nfield,)),
            ],
            compiler_params=params(),
            cost_estimate=cost(1e3, 1e3),
            name="assemble_input_grad",
        )(place, *returned[i], *before, *deps)

    input_grad = assemble(0, [], [blocks[0]])
    input_grad = assemble(1, input_grad, [blocks[0]])
    done = call(
        add_fields_kernel,
        "add_fields",
        shaped((2 * EXP_H1 + SMALL, LANES), bf16),
        [smem] + [vmem] * nfield,
        [place, blocks[0]] + [shift(blocks[s], -s) for s in range(1, nfield)],
        deps=[returned[2][0], *input_grad],
    )
    done_own, g_tower, lines, g_gate = call(
        join_done_kernel,
        "join_gradients",
        [
            shaped((QUADS, 2 * EXP_H1, LANES), bf16),
            shaped((LANES, LANES), f32),
            shaped((8 * QUADS, LANES), f32),
            shaped((GATES, columns), f32),
        ],
        [smem] + [vmem] * QUADS,
        [place] + from_quads(done),
    )
    done_other = cross(done_own, 1)

    def run_update(core, grads, before):
        first_spec = pl.BlockSpec((columns, EXP_H1), lambda q, place_ref: (0, place_ref[0] ^ (2 * q + core)))
        second_spec = pl.BlockSpec((EXP_H1, EXP_H2), lambda q, place_ref: (place_ref[0] ^ (2 * q + core), 0))
        operands = [
            grads,
            first_weight,
            first_mean,
            first_square,
            second_weight,
            second_mean,
            second_square,
            second_average,
        ]
        specs = [first_spec] * 3 + [second_spec] * 4
        before = list(before or [])[:7]
        return pl.pallas_call(
            functools.partial(update_kernel, core),
            grid_spec=pltpu.PrefetchScalarGridSpec(
                num_scalar_prefetch=1,
                grid=(QUADS,),
                in_specs=[vmem] * len(operands) + [anywhere] * len(before),
                out_specs=specs + [pl.BlockSpec((8, LANES), lambda q, place_ref: (0, 0))],
            ),
            out_shape=[shaped((columns, H1), f32)] * 3
            + [shaped((H1, EXP_H2), f32)] * 4
            + [shaped((8, LANES), f32)],
            input_output_aliases={1 + len(operands) + i: i for i in range(len(before))},
            compiler_params=params(),
            cost_estimate=cost(1e6, 8e6),
            name="update_layers",
        )(place, *operands, *before)

    updated_half = run_update(0, done_own, None)
    updated = run_update(1, done_other, updated_half)
    new_first, new_second, avg_second = updated[:3], updated[3:6], updated[6]

    at = (H1 + H2) // LANES
    g_head = lines[at + 1]
    g_bias = jnp.concatenate([lines[: at + 1].reshape(-1), lines[at + 2, :TASKS]])
    new_gate = adamw(gate_weight, gate_mean, gate_square, g_gate.T)
    new_tower = adamw(tower_weight, tower_mean, tower_square, g_tower)
    avg_tower = blend(tower_average, new_tower[0])
    new_head = adamw(head_weight, head_mean, head_square, g_head)
    avg_head = blend(head_average, new_head[0])
    new_bias = adamw(biases, bias_mean, bias_square, g_bias)

    (input_grad,) = assemble(2, input_grad, [updated[7]])
    predicted = jnp.concatenate(probs, axis=1).T
    return (
        predicted,
        input_grad,
        *new_first,
        *new_gate,
        *new_second,
        *new_tower,
        *new_head,
        *new_bias,
        avg_second,
        avg_tower,
        avg_head,
    )


def solution(mesh):
    fields, copied = P("field", None), P()
    rows = P(("batch", "field"), None)
    in_specs = (
        (P("batch", "field"), rows, P(("batch", "field"))) + (fields,) * 6 + (copied,) * 15
    )
    out_specs = (rows, P("batch", "field")) + (fields,) * 6 + (copied,) * 15
    return jax.shard_map(
        on_device, mesh=mesh, in_specs=in_specs, out_specs=out_specs, check_vma=False
    )
```
